32 devices in a mesh: groups: 2 (over x), row: 4 (over y, core), col: 4 (over z).
Axes of the slice: x: 2, y: 2, z: 4, core: 2. Of those that a mesh axis runs over, the one named last changes fastest.
Arguments:
- zroot: float32 [4096, 2048], P(('groups', 'row')), parts along dimension 0, as said below
- panel_one: float32 [8, 2048, 1024], P(('groups', 'col'), 'row'), parts along dimension 0, may hold values from -0.125 to 0.125
- inv_one: float32 [8, 1024, 1024], P(('groups', 'col')), parts along dimension 0
- panel_two_j: float32 [16, 1024, 512], P(('groups', 'col'), 'row'), parts along dimension 0, may hold values from -0.109375 to 0.109375
- panel_two_r: float32 [16, 2048, 512], P(('groups', 'col'), 'row'), parts along dimension 0, may hold values from -0.109375 to 0.109375
- inv_two: float32 [16, 512, 512], P(('groups', 'col')), parts along dimension 0
- parents: int32 [16], P(('groups', 'col')), parts along dimension 0, may hold values from 0 to 3
- widths: int32 [16], P(('groups', 'col')), parts along dimension 0, may hold values from 256 to 512, as said below
- pattern_j: int32 [16, 16], P(('groups', 'col'), 'row'), parts along dimension 0, may hold values 0 or 1
- pattern_r: int32 [16, 32], P(('groups', 'col'), 'row'), parts along dimension 0, may hold values 0 or 1
Outputs:
- var_one: float32 [8, 1024], P(('groups', 'col'), 'row'), parts along dimension 0
- var_two: float32 [16, 512], P(('groups', 'col'), 'row'), parts along dimension 0
- z_two_j: float32 [16, 1024, 512], P(('groups', 'col'), 'row'), parts along dimension 0
- z_two_r: float32 [16, 2048, 512], P(('groups', 'col'), 'row'), parts along dimension 0
The draws below stay inside these ranges and needn't reach their ends.
There are 2 independent parts, one for each index of `groups`. The reference program is written for one: setup_inputs(seed, part) draws one part's arguments, and reference() takes and returns one part's arrays. A program takes and returns all parts, laid end to end along the dimension named above; each array names one. Nothing has to cross between parts.
Inputs may be any that keep to these rules, and one draw needn't show every extreme that they name: zroot is symmetric: it equals its transpose up to rounding, as a selected inverse block of a symmetric matrix does. `widths`: the live width of each level-2 supernode; columns at or past it are padding. `parents`: index of the level-1 parent of each level-2 supernode. `pattern_j`: 1 where a tile of 64 rows of the panel is stored. `pattern_r`: 1 where a tile of 64 rows of the panel is stored.
All inputs are finite; a program needn't handle non-finite values. No bound on the sum of `pattern_j` or of `pattern_r` on one device may be relied on, other than what follows from the above.
Results may differ from the reference program's by a relative error of at most 0.0003.
Values sent between devices are 32-bit elements; how exact they have to be, the bound alone decides.
A program may use at most 128 MiB of HBM per device.

```python
import math
import jax
import jax.numpy as jnp
import numpy as np
from jax import lax

WR = 2048
W1 = 1024
W2 = 512
TILE = 64
P1 = 4
P2 = 8
WA = 3072


def triangle(key, count, width):
    first, second = jax.random.split(key)
    entries = jax.random.normal(first, (count, width, width), jnp.float32)
    diagonal = jax.random.uniform(second, (count, width), jnp.float32, 0.7, 1.4)
    lower = jnp.tril(entries, -1) * (0.5 / math.sqrt(width))
    return lower + diagonal[:, :, None] * jnp.eye(width, dtype=jnp.float32)


def draw_inv_one(key, part):
    return triangle(jax.random.fold_in(key, 11), P1, W1)


def draw_inv_two(key, part):
    return triangle(jax.random.fold_in(key, 23), P2, W2)


def draw_zroot(key, part):
    first, second = jax.random.split(jax.random.fold_in(key, 37), 2)
    noise = jax.random.normal(first, (WR, WR), jnp.float32)
    sym = (noise + noise.T) * (0.35 / math.sqrt(WR))
    diagonal = jax.random.uniform(second, (WR,), jnp.float32, 0.8, 1.6)
    base = sym + diagonal[:, None] * jnp.eye(WR, dtype=jnp.float32)
    return base


def draw_widths(key, part):
    first, second = jax.random.split(jax.random.fold_in(key, 41))
    values = jax.random.randint(first, (P2,), W2 // 2, W2 + 1)
    place = jax.random.randint(second, (), 0, P2)
    values = values.at[place].set(W2)
    values = values.at[(place + 1) % P2].set(W2 // 2)
    return values.astype(jnp.int32)


def touch_ends(values, key, least, high):
    spot = [jax.random.randint(jax.random.fold_in(key, axis), (), 0, length) for axis, length in enumerate(values.shape)]
    longest = values.shape.index(max(values.shape))
    beside = spot[:longest] + [(spot[longest] + 1) % values.shape[longest]] + spot[longest + 1:]
    return values.at[tuple(spot)].set(least).at[tuple(beside)].set(high)


def steps_of(rng, dims, cuts, low, high):
    factor_of, own = 1.0, jax.random.fold_in(rng, 6)
    for position, shards_of in cuts:
        heights = jnp.exp(jax.random.uniform(jax.random.fold_in(own, position), (shards_of,), jnp.float32, low / len(cuts), high / len(cuts)))
        factor_of = factor_of * jnp.repeat(heights, dims[position] // shards_of).reshape([-1 if axis == position else 1 for axis in range(len(dims))])
    return factor_of


def rank_bounds(number_of, skew):
    portions = [(1 << 20) // math.isqrt(grade ** skew) + 1 for grade in range(1, number_of + 1)]
    scale = 1 + sum(portions) // (1 << 30)
    return np.cumsum(np.array([max(1, weight // scale) for weight in portions]))


def ranked(own_key, shape, count, skew):
    grid = rank_bounds(count, skew)
    pick = jax.random.randint(jax.random.fold_in(own_key, 1), shape, 0, int(grid[count - 1]))
    grade = jnp.searchsorted(jnp.asarray(grid, jnp.int32), pick, side="right")
    return jax.random.permutation(jax.random.fold_in(own_key, 2), count)[grade].astype(jnp.int32)


def scatter_about(stream_key, dims, deviation, bound, cuts=(), kind=jnp.bfloat16):
    gain = steps_of(stream_key, dims, cuts, -0.22, 0.18) if cuts else 1.0
    values = jax.random.normal(stream_key, dims, jnp.float32) * deviation * gain
    return jnp.minimum(jnp.maximum(values, -bound), bound).astype(kind)


def setup_inputs(seed: int = 0, part: int = 0) -> dict:
    splits = jax.random.split(jax.random.key(seed), 11)
    part_splits = jax.random.split(jax.random.fold_in(splits[10], part), 11)
    zroot = draw_zroot(jax.random.fold_in(jax.random.fold_in(splits[10], part), 71), part)
    panel_one = scatter_about(part_splits[1], (P1, WR, W1), WR ** -0.5, 0.125, ((0, 4), (1, 4)), jnp.float32)
    inv_one = draw_inv_one(jax.random.fold_in(jax.random.fold_in(splits[10], part), 71), part)
    panel_two_j = scatter_about(part_splits[3], (P2, W1, W2), WA ** -0.5, 0.109375, ((0, 4), (1, 4)), jnp.float32)
    panel_two_r = scatter_about(part_splits[4], (P2, WR, W2), WA ** -0.5, 0.109375, ((0, 4), (1, 4)), jnp.float32)
    inv_two = draw_inv_two(jax.random.fold_in(jax.random.fold_in(splits[10], part), 71), part)
    parents = touch_ends(ranked(part_splits[6], (P2,), P1, 2), jax.random.fold_in(part_splits[6], 3), 0, P1 - 1).astype(jnp.int32)
    widths = draw_widths(jax.random.fold_in(jax.random.fold_in(splits[10], part), 71), part)
    pattern_j = touch_ends((jax.random.randint(part_splits[8], (P2, W1 // TILE), 0, 4) < 3).astype(jnp.int32), jax.random.fold_in(part_splits[8], 1), 0, 1)
    pattern_r = touch_ends((jax.random.randint(part_splits[9], (P2, WR // TILE), 0, 4) < 3).astype(jnp.int32), jax.random.fold_in(part_splits[9], 1), 0, 1)
    return dict(zroot=zroot, panel_one=panel_one, inv_one=inv_one, panel_two_j=panel_two_j, panel_two_r=panel_two_r, inv_two=inv_two, parents=parents, widths=widths, pattern_j=pattern_j, pattern_r=pattern_r)


def product(left, right):
    return jnp.dot(left, right, precision=lax.Precision.HIGHEST, preferred_element_type=jnp.float32)


def reference(zroot, panel_one, inv_one, panel_two_j, panel_two_r, inv_two, parents, widths, pattern_j, pattern_r):
    def level_one(pieces):
        panel, inverse = pieces
        factor = product(panel, inverse)
        root_block = -product(zroot, factor)
        diagonal_block = product(inverse.T, inverse) - product(factor.T, root_block)
        return root_block, diagonal_block

    all_rj, all_jj = lax.map(level_one, (panel_one, inv_one))
    var_one = jnp.diagonal(all_jj, axis1=1, axis2=2)

    def level_two(pieces):
        panel_j, panel_r, inverse, parent, width, tiles_j, tiles_r = pieces
        live = (jnp.arange(W2) < width).astype(jnp.float32)
        masked_j = panel_j * jnp.repeat(tiles_j.astype(jnp.float32), TILE)[:, None] * live[None, :]
        masked_r = panel_r * jnp.repeat(tiles_r.astype(jnp.float32), TILE)[:, None] * live[None, :]
        factor_j = product(masked_j, inverse)
        factor_r = product(masked_r, inverse)
        parent_jj = all_jj[parent]
        parent_rj = all_rj[parent]
        block_j = -(product(parent_jj, factor_j) + product(parent_rj.T, factor_r))
        block_r = -(product(parent_rj, factor_j) + product(zroot, factor_r))
        squares = jnp.sum(inverse * inverse, axis=0)
        variance = live * (squares - jnp.sum(factor_j * block_j, axis=0) - jnp.sum(factor_r * block_r, axis=0))
        return variance, block_j, block_r

    var_two, z_two_j, z_two_r = lax.map(level_two, (panel_two_j, panel_two_r, inv_two, parents, widths, pattern_j, pattern_r))
    return var_one, var_two, z_two_j, z_two_r
```

```python
import jax
import jax.numpy as jnp
from jax import lax
from jax.experimental import pallas as pl
from jax.experimental.pallas import tpu as pltpu
from jax.sharding import PartitionSpec as P

TILE = 64
PRECISION = lax.Precision.HIGH


def product(left, right):
    return jnp.dot(left, right, precision=PRECISION, preferred_element_type=jnp.float32)


def crossed(left, right):
    return lax.dot_general(
        left, right, (((0,), (0,)), ((), ())), precision=PRECISION, preferred_element_type=jnp.float32
    )


def swap(block, bit):
    n = lax.axis_size("row")
    return lax.ppermute(block, "row", [(i, i ^ bit) for i in range(n)])


def own_first(array, axis):
    n = lax.axis_size("row")
    me = lax.axis_index("row")
    share = array.shape[axis] // n
    pieces = [
        lax.dynamic_slice_in_dim(array, (me ^ d) * share, share, axis) for d in range(n)
    ]
    return jnp.concatenate(pieces, axis)


def row_blocks(block):
    n = lax.axis_size("row")
    held = {0: block}
    bit = n // 2
    while bit:
        for d in sorted(held):
            held[d | bit] = swap(held[d], bit)
        bit //= 2
    return [held[d] for d in range(n)]


def row_sum(pieces):
    n = lax.axis_size("row")
    held = dict(enumerate(pieces))
    bit = 1
    while bit < n:
        for d in [d for d in sorted(held) if not d & bit]:
            held[d] = held[d] + swap(held.pop(d | bit), bit)
        bit *= 2
    return held[0]


def reordered(block, d):
    n = lax.axis_size("row")
    share = block.shape[1] // n
    return jnp.concatenate(
        [block[:, (d ^ e) * share : ((d ^ e) + 1) * share] for e in range(n)], 1
    )


def general_body(
    zroot,
    panel_one,
    inv_one,
    panel_two_j,
    panel_two_r,
    inv_two,
    parents,
    widths,
    pattern_j,
    pattern_r,
):
    n = lax.axis_size("row")
    width_one = inv_one.shape[1]
    node_rows = width_one // n
    nodes, width_two = inv_two.shape[:2]
    root_rows = zroot.shape[0]

    inverse = own_first(inv_one[0], 1)
    factor = product(panel_one[0], inverse)
    all_factors = lax.all_gather(factor, "col", axis=0)
    gram = crossed(inverse[:, :node_rows], inverse)
    factor_tied, gram = lax.optimization_barrier((factor, gram))
    all_grams = lax.all_gather(gram, "col", axis=0)

    live = (jnp.arange(width_two)[None, :] < widths[:, None]).astype(jnp.float32)
    mask_j = jnp.repeat(pattern_j.astype(jnp.float32), TILE, axis=1)
    mask_r = jnp.repeat(pattern_r.astype(jnp.float32), TILE, axis=1)
    factor_j = []
    factor_r = []
    for i in range(nodes):
        masked_j = panel_two_j[i] * mask_j[i][:, None] * live[i][None, :]
        masked_r = panel_two_r[i] * mask_r[i][:, None] * live[i][None, :]
        factor_j.append(product(masked_j, inv_two[i]))
        factor_r.append(product(masked_r, inv_two[i]))
    near_j = jnp.concatenate(factor_j, 1)
    full_j = jnp.concatenate(row_blocks(near_j), 0)

    root = own_first(zroot, 1)
    full_factor = jnp.concatenate(
        [reordered(block, d) for d, block in enumerate(row_blocks(factor))], 0
    )
    image = product(root, full_factor)
    terms = jnp.sum(factor * image, axis=0).reshape(n, node_rows)
    own_squares = jnp.sum(inverse[:, :node_rows] ** 2, axis=0)
    var_one = (own_squares + row_sum([terms[d] for d in range(n)]))[None, :]

    all_factors, var_one = lax.optimization_barrier((all_factors, var_one))

    parent_factor = [
        lax.dynamic_index_in_dim(all_factors, parents[i], 0, False) for i in range(nodes)
    ]
    reduced = [
        factor_r[i] - product(parent_factor[i], full_j[:, i * width_two : (i + 1) * width_two])
        for i in range(nodes)
    ]
    block_r = []
    sums_j = []
    for i in range(nodes):
        block_r.append(-product(root, jnp.concatenate(row_blocks(reduced[i]), 0)))
        upper = crossed(parent_factor[i], block_r[i]).reshape(n, node_rows, width_two)
        sums_j.append(row_sum([upper[d] for d in range(n)]))
    block_j = []
    for i in range(nodes):
        parent_gram = lax.dynamic_index_in_dim(all_grams, parents[i], 0, False)
        near = product(parent_gram, full_j[:, i * width_two : (i + 1) * width_two])
        block_j.append(-(near + sums_j[i]))

    corrections = jnp.stack(
        [
            jnp.sum(factor_j[i] * block_j[i], axis=0) + jnp.sum(factor_r[i] * block_r[i], axis=0)
            for i in range(nodes)
        ]
    )
    share = width_two // n
    me = lax.axis_index("row")
    ordered = own_first(corrections, 1).reshape(nodes, n, share)
    summed = row_sum([ordered[:, d] for d in range(n)])
    squares = jnp.sum(inv_two * inv_two, axis=1)
    live_share = lax.dynamic_slice_in_dim(live, me * share, share, 1)
    square_share = lax.dynamic_slice_in_dim(squares, me * share, share, 1)
    var_two = live_share * (square_share - summed)
    return (var_one, var_two, jnp.stack(block_j), jnp.stack(block_r))


PIECE = 32
RING = 8
AHEAD = 2
STEP = 128


def mm(left, right):
    return jnp.dot(left, right, precision=PRECISION, preferred_element_type=jnp.float32)


def mm_t(left, right):
    return lax.dot_general(
        left, right, (((0,), (0,)), ((), ())), precision=PRECISION, preferred_element_type=jnp.float32
    )


def exchange_kernel(
    picks,
    own,
    near_j,
    near_r,
    root,
    z_j,
    z_r,
    var_a,
    var_b,
    held,
    staged,
    full_j,
    chosen,
    reduced,
    across,
    beside,
    part_in,
    part_y,
    vec_a,
    vec_b,
    line_send,
    line_recv,
    j_send,
    j_recv,
    g_send,
    g_recv,
    r_send,
    r_recv,
    u_send,
    u_recv,
    a_send,
    a_recv,
    b_send,
    b_recv,
):
    rows = root.shape[0]
    width = own.shape[1]
    node = near_j.shape[0]
    nodes, _, two = z_r.shape
    chunks = own.shape[0] // PIECE
    steps = rows // STEP
    per = STEP // PIECE
    half = width // 2

    z = lax.axis_index("col")
    r = lax.axis_index("row")
    core = r % 2
    side = r // 2
    twin = r + 1 - 2 * core
    over = (r + 2) % 4
    diag = (twin + 2) % 4
    inner = jnp.logical_or(z == 1, z == 2)
    outer = jnp.logical_not(inner)

    def remote(src, dst, send, recv, device):
        return pltpu.make_async_remote_copy(
            src_ref=src,
            dst_ref=dst,
            send_sem=send,
            recv_sem=recv,
            device_id=device,
            device_id_type=pl.DeviceIdType.MESH,
        )

    def at_row(index):
        return (lax.axis_index("groups"), index, z)

    def at_col(index):
        return (lax.axis_index("groups"), r, index)

    barrier = pltpu.get_barrier_semaphore()

    def greet(device):
        pl.semaphore_signal(barrier, inc=1, device_id=device, device_id_type=pl.DeviceIdType.MESH)

    for peer in (twin, over, diag):
        greet(at_row(peer))

    @pl.when(outer)
    def _():
        greet(at_col(1 + z // 3))
        pl.semaphore_wait(barrier, 4)

    @pl.when(inner)
    def _():
        greet(at_col(3 - z))
        greet(at_col(((z - 1) * 3) % 4))
        pl.semaphore_wait(barrier, 5)

    def piece(t):
        return pl.ds(pl.multiple_of(t * PIECE, PIECE), PIECE)

    def line(stream, t):
        at = piece(t)
        if stream == 0:
            src, dst, device = own.at[at], held.at[2, at], at_col(1 + z // 3)
        elif stream == 1:
            src, dst, device = own.at[at], held.at[0, at], at_col(3 - z)
        elif stream == 2:
            src, dst, device = held.at[2, at], held.at[1, at], at_col(3 - z)
        else:
            src = staged.at[stream - 3, piece(t % RING)]
            dst, device = held.at[stream - 3, at], at_col(((z - 1) * 3) % 4)
        return remote(src, dst, line_send.at[stream, t], line_recv.at[stream, t], device)

    def to_middle(t):
        line(1, t).start()
        line(0, t).wait_recv()
        line(2, t).start()

    def chunk(t):
        @pl.when(inner)
        def _():
            @pl.when(t + AHEAD < chunks)
            def _():
                to_middle(t + AHEAD)

            line(1, t).wait_recv()
            line(2, t).wait_recv()
            at = piece(t)
            for m in range(nodes):
                pick = picks[nodes + m]

                @pl.when(t >= RING)
                def _():
                    line(3 + m, t - RING).wait_send()

                staged[m, piece(t % RING), :] = jnp.where(
                    pick == 0, own[at, :], jnp.where(pick == 1, held[0, at, :], held[1, at, :])
                )
                line(3 + m, t).start()

        @pl.when(outer)
        def _():
            line(3, t).wait_recv()
            line(4, t).wait_recv()

    def j_copy(k):
        mine = pl.ds(pl.multiple_of(r * node, node), node)
        theirs = pl.ds(pl.multiple_of(over * node, node), node)
        if k == 2:
            return remote(full_j.at[theirs], full_j.at[theirs], j_send.at[2], j_recv.at[2], at_row(twin))
        return remote(near_j, full_j.at[mine], j_send.at[k], j_recv.at[k], at_row(over if k == 0 else twin))

    def g_copy(k):
        at = pl.ds(pl.multiple_of(core * rows, rows), rows)
        top = pl.ds(0, rows)
        if k == 0:
            columns = pl.ds(pl.multiple_of((1 - side) * half, half), half)
            return remote(own.at[top, columns], across.at[at], g_send.at[0], g_recv.at[0], at_row(over))
        if k == 1:
            columns = pl.ds(pl.multiple_of((1 - core) * half, half), half)
            return remote(own.at[top, columns], beside, g_send.at[1], g_recv.at[1], at_row(twin))
        return remote(across.at[at], across.at[at], g_send.at[2], g_recv.at[2], at_row(twin))

    def r_copy(k, step):
        who = over if k == 2 else r
        at = pl.ds(pl.multiple_of(who * rows + step * STEP, STEP), STEP)
        return remote(
            reduced.at[at],
            reduced.at[at],
            r_send.at[k, step],
            r_recv.at[k, step],
            at_row(over if k == 0 else twin),
        )

    @pl.when(outer)
    def _():
        def go(t, carry):
            line(0, t).start()
            return carry

        lax.fori_loop(0, chunks, go, 0)

    for k in (0, 1):
        j_copy(k).start()

    @pl.when(inner)
    def _():
        def go(t, carry):
            to_middle(t)
            return carry

        lax.fori_loop(0, AHEAD, go, 0)

    for k in (0, 1):
        g_copy(k).start()

    mine_j = pl.ds(pl.multiple_of(r * node, node), node)
    full_j[mine_j, :] = near_j[...]
    for m in range(nodes):
        z_r[m] = jnp.zeros_like(z_r[m])

    def pick_rows(m, at):
        pick = picks[m]
        first = jnp.where(pick == 0, own[at, :], held[0, at, :])
        second = jnp.where(pick == 2, held[1, at, :], held[2, at, :])
        return jnp.where(pick < 2, first, second)

    def reduce_step(step):
        at = pl.ds(pl.multiple_of(step * STEP, STEP), STEP)
        to = pl.ds(pl.multiple_of(r * rows + step * STEP, STEP), STEP)
        for m in range(nodes):
            block = pick_rows(m, at)
            chosen[m, at, :] = block
            columns = slice(m * two, (m + 1) * two)
            reduced[to, columns] = near_r[at, columns] - mm(block, full_j[:, columns])
        r_copy(0, step).start()
        r_copy(1, step).start()

    def gather_step(step):
        r_copy(0, step).wait_recv()
        r_copy(2, step).start()

    def root_step(step):
        r_copy(1, step).wait_recv()
        r_copy(2, step).wait_recv()
        places = [pl.ds(pl.multiple_of(d * rows + step * STEP, STEP), STEP) for d in range(4)]
        left = jnp.concatenate([root[:, place] for place in places], 1)
        for m in range(nodes):
            columns = slice(m * two, (m + 1) * two)
            right = jnp.concatenate([reduced[place, columns] for place in places], 0)
            z_r[m] -= mm(left, right)

    def to_tile(vec):
        return jnp.concatenate([vec[:, i * 128 : (i + 1) * 128] for i in range(vec.shape[1] // 128)], 0)

    def to_peers(tile, send, recv):
        return [
            remote(tile.at[0], tile.at[1 + k], send.at[k], recv.at[k], at_row(peer))
            for k, peer in enumerate((twin, over, diag))
        ]

    def level_one():
        def colsum(at, where):
            return jnp.sum(at * where, axis=0, keepdims=True)

        mine = pl.ds(pl.multiple_of(r * rows, rows), rows)
        theirs = pl.ds(pl.multiple_of(twin * rows, rows), rows)
        far = pl.ds(pl.multiple_of((1 - side) * 2 * rows, 2 * rows), 2 * rows)
        sums = []
        for h in range(2):
            columns = slice(h * half, (h + 1) * half)
            block = own[0:rows, columns]
            sums.append(colsum(block, mm(root[:, mine], block)))
        g_copy(1).wait_recv()
        pair = mm(root[:, theirs], beside[...])
        lift = pl.ds(pl.multiple_of(core * half, half), half)
        pair = 2.0 * colsum(own[0:rows, lift], pair)
        g_copy(2).wait_recv()
        cross = mm(root[:, far], across[...])
        lift = pl.ds(pl.multiple_of(side * half, half), half)
        cross = 2.0 * colsum(own[0:rows, lift], cross)
        for h in range(2):
            sums[h] = sums[h] + jnp.where(core == h, pair, 0.0) + jnp.where(side == h, cross, 0.0)
        vec_a[0] = to_tile(jnp.concatenate(sums, 1))

    def walk(base):
        def go(s, carry):
            chunk(base + s)
            return carry

        return go

    lax.fori_loop(0, per, walk(0), 0)
    j_copy(0).wait_recv()
    j_copy(2).start()
    j_copy(1).wait_recv()
    j_copy(2).wait_recv()
    reduce_step(0)
    g_copy(0).wait_recv()
    g_copy(2).start()

    def macro(step, carry):
        lax.fori_loop(0, per - 1, walk(step * per), 0)
        gather_step(step - 1)
        chunk(step * per + per - 1)
        root_step(step - 1)
        reduce_step(step)
        return carry

    lax.fori_loop(1, 2, macro, 0)
    level_one()
    for copy in to_peers(vec_a, a_send, a_recv):
        copy.start()
    lax.fori_loop(2, steps, macro, 0)

    def node_step(step):
        at = pl.ds(rows + step * STEP, STEP)
        for m in range(nodes):
            z_j[m, step * STEP : (step + 1) * STEP, :] = mm(
                pick_rows(m, at), full_j[:, m * two : (m + 1) * two]
            )

    base = steps * per
    lax.fori_loop(base, base + per - 1, walk(0), 0)
    gather_step(steps - 1)
    root_step(steps - 1)

    parts = full_j.shape[0] // node
    part_out = across
    part_own = beside

    def upper(m, dest):
        columns = pl.ds(pl.multiple_of(dest * node, node), node)
        return mm_t(chosen[m, :, columns], z_r[m])

    def u_copy(k):
        at = pl.ds(0, 2 * node)
        if k < 2:
            return remote(part_out.at[pl.ds(k * 2 * node, 2 * node)], part_in.at[k], u_send.at[k], u_recv.at[k], at_row(twin))
        return remote(part_own.at[pl.ds((k - 2) * node, node)], part_y.at[k - 2], u_send.at[k], u_recv.at[k], at_row(over))

    for copy in (g_copy(0), g_copy(1), g_copy(2)):
        copy.wait_send()
    for m in range(nodes):
        part_out[m * 2 * node : m * 2 * node + node, :] = upper(m, diag)
        part_out[m * 2 * node + node : (m + 1) * 2 * node, :] = upper(m, twin)
        u_copy(m).start()
    chunk(base + per - 1)
    for m in range(nodes):
        far = upper(m, over)
        u_copy(m).wait_recv()
        part_own[m * node : (m + 1) * node, :] = far + part_in[m, 0:node, :]
        u_copy(2 + m).start()
    node_step(0)
    for m in range(nodes):
        part_in[m, node : 2 * node, :] = part_in[m, node : 2 * node, :] + upper(m, r)
    for copy in to_peers(vec_a, a_send, a_recv):
        copy.wait()
    var_a[...] = vec_a[0] + vec_a[1] + vec_a[2] + vec_a[3]
    sums_r = [
        jnp.sum(near_r[:, m * two : (m + 1) * two] * z_r[m], axis=0, keepdims=True) for m in range(nodes)
    ]
    lax.fori_loop(base + per, base + 2 * per, walk(0), 0)
    node_step(1)
    for m in range(nodes):
        u_copy(2 + m).wait_recv()
        z_j[m] = -(z_j[m] + part_in[m, node : 2 * node, :] + part_y[m])
        sums_r[m] = sums_r[m] + jnp.sum(near_j[:, m * two : (m + 1) * two] * z_j[m], axis=0, keepdims=True)
    vec_b[0] = to_tile(jnp.concatenate(sums_r, 1))
    for copy in to_peers(vec_b, b_send, b_recv):
        copy.start()

    @pl.when(outer)
    def _():
        def go(t, carry):
            line(0, t).wait_send()
            return carry

        lax.fori_loop(0, chunks, go, 0)

    @pl.when(inner)
    def _():
        def go(t, carry):
            line(1, t).wait_send()
            line(2, t).wait_send()
            return carry

        lax.fori_loop(0, chunks, go, 0)

        def last(t, carry):
            line(3, t).wait_send()
            line(4, t).wait_send()
            return carry

        lax.fori_loop(chunks - RING, chunks, last, 0)

    for k in range(3):
        j_copy(k).wait_send()

    def sent(step, carry):
        for k in range(3):
            r_copy(k, step).wait_send()
        return carry

    lax.fori_loop(0, steps, sent, 0)
    for k in range(4):
        u_copy(k).wait_send()
    for copy in to_peers(vec_b, b_send, b_recv):
        copy.wait()
    var_b[...] = vec_b[0] + vec_b[1] + vec_b[2] + vec_b[3]


def line_body(
    zroot,
    panel_one,
    inv_one,
    panel_two_j,
    panel_two_r,
    inv_two,
    parents,
    widths,
    pattern_j,
    pattern_r,
):
    n = lax.axis_size("row")
    width = inv_one.shape[1]
    node = width // n
    nodes, two = inv_two.shape[:2]
    rows = zroot.shape[0]
    me = lax.axis_index("row")
    z = lax.axis_index("col")

    low = z < 2
    beyond = lax.ppermute(parents, "col", [(0, 1), (3, 2)])
    place = jnp.where(low, z, 3 - z)
    ours = jnp.where(low, parents, 3 - parents)
    theirs = jnp.where(low, beyond, 3 - beyond)
    slot = jnp.arange(1, nodes + 1, dtype=jnp.int32)
    ours = jnp.where(place == 1, (ours + 3) % 4, jnp.where(ours == 0, 0, slot))
    picks = jnp.concatenate([ours, jnp.maximum(theirs - 1, 0)]).astype(jnp.int32)

    inverse = inv_one[0]
    mine = lax.dynamic_slice_in_dim(inverse, me * node, node, 1)
    own = jnp.concatenate([product(panel_one[0], inverse), crossed(mine, inverse)], 0)

    live = (jnp.arange(two)[None, :] < widths[:, None]).astype(jnp.float32)
    mask_j = jnp.repeat(pattern_j.astype(jnp.float32), TILE, axis=1)
    mask_r = jnp.repeat(pattern_r.astype(jnp.float32), TILE, axis=1)
    factor_j = []
    factor_r = []
    for i in range(nodes):
        masked_j = panel_two_j[i] * mask_j[i][:, None] * live[i][None, :]
        masked_r = panel_two_r[i] * mask_r[i][:, None] * live[i][None, :]
        factor_j.append(product(masked_j, inv_two[i]))
        factor_r.append(product(masked_r, inv_two[i]))
    near_j = jnp.concatenate(factor_j, 1)
    near_r = jnp.concatenate(factor_r, 1)

    chunks = own.shape[0] // PIECE
    steps = rows // STEP
    f32 = jnp.float32
    vmem = pl.BlockSpec(memory_space=pltpu.VMEM)
    dma = pltpu.SemaphoreType.DMA
    z_j, z_r, sums_a, sums_b = pl.pallas_call(
        exchange_kernel,
        out_shape=(
            jax.ShapeDtypeStruct((nodes, node, two), f32),
            jax.ShapeDtypeStruct((nodes, rows, two), f32),
            jax.ShapeDtypeStruct((width // 128, 128), f32),
            jax.ShapeDtypeStruct((nodes * two // 128, 128), f32),
        ),
        in_specs=[pl.BlockSpec(memory_space=pltpu.SMEM)] + [vmem] * 4,
        out_specs=(vmem,) * 4,
        scratch_shapes=[
            pltpu.VMEM((3,) + own.shape, f32),
            pltpu.VMEM((nodes, RING * PIECE, width), f32),
            pltpu.VMEM((width, nodes * two), f32),
            pltpu.VMEM((nodes, rows, width), f32),
            pltpu.VMEM((4 * rows, nodes * two), f32),
            pltpu.VMEM((2 * rows, width // 2), f32),
            pltpu.VMEM((rows, width // 2), f32),
            pltpu.VMEM((nodes, 2 * node, two), f32),
            pltpu.VMEM((nodes, node, two), f32),
            pltpu.VMEM((4, width // 128, 128), f32),
            pltpu.VMEM((4, nodes * two // 128, 128), f32),
            dma((5, chunks)),
            dma((5, chunks)),
            dma((3,)),
            dma((3,)),
            dma((3,)),
            dma((3,)),
            dma((3, steps)),
            dma((3, steps)),
            dma((4,)),
            dma((4,)),
            dma((3,)),
            dma((3,)),
            dma((3,)),
            dma((3,)),
        ],
        compiler_params=pltpu.CompilerParams(
            collective_id=0, has_side_effects=True, vmem_limit_bytes=61 * 1024 * 1024
        ),
    )(picks, own, near_j, near_r, zroot)

    share_one = width // n
    squares = jnp.sum(mine**2, axis=0)
    corr_one = lax.dynamic_slice_in_dim(sums_a.reshape(width), me * share_one, share_one, 0)
    var_one = (squares + corr_one)[None, :]
    share = two // n
    squares_two = lax.dynamic_slice_in_dim(jnp.sum(inv_two * inv_two, axis=1), me * share, share, 1)
    corr_two = lax.dynamic_slice_in_dim(sums_b.reshape(nodes, two), me * share, share, 1)
    live_share = lax.dynamic_slice_in_dim(live, me * share, share, 1)
    var_two = live_share * (squares_two - corr_two)
    return (var_one, var_two, z_j, z_r)


def solution(mesh):
    fits = mesh.shape["row"] == 4 and mesh.shape["col"] == 4
    return jax.shard_map(
        line_body if fits else general_body,
        mesh=mesh,
        in_specs=(
            P(("groups", "row"), None),
            P(("groups", "col"), "row", None),
            P(("groups", "col"), None, None),
            P(("groups", "col"), "row", None),
            P(("groups", "col"), "row", None),
            P(("groups", "col"), None, None),
            P(("groups", "col")),
            P(("groups", "col")),
            P(("groups", "col"), "row"),
            P(("groups", "col"), "row"),
        ),
        out_specs=(
            P(("groups", "col"), "row"),
            P(("groups", "col"), "row"),
            P(("groups", "col"), "row", None),
            P(("groups", "col"), "row", None),
        ),
        check_vma=False,
    )
```

```python
import jax
import jax.numpy as jnp
from jax import lax
from jax.experimental import pallas as pl
from jax.experimental.pallas import tpu as pltpu
from jax.sharding import PartitionSpec as P

TILE = 64
PRECISION = lax.Precision.HIGH


def product(left, right):
    return jnp.dot(left, right, precision=PRECISION, preferred_element_type=jnp.float32)


def crossed(left, right):
    return lax.dot_general(
        left, right, (((0,), (0,)), ((), ())), precision=PRECISION, preferred_element_type=jnp.float32
    )


def swap(block, bit):
    n = lax.axis_size("row")
    return lax.ppermute(block, "row", [(i, i ^ bit) for i in range(n)])


def own_first(array, axis):
    n = lax.axis_size("row")
    me = lax.axis_index("row")
    share = array.shape[axis] // n
    pieces = [
        lax.dynamic_slice_in_dim(array, (me ^ d) * share, share, axis) for d in range(n)
    ]
    return jnp.concatenate(pieces, axis)


def row_blocks(block):
    n = lax.axis_size("row")
    held = {0: block}
    bit = n // 2
    while bit:
        for d in sorted(held):
            held[d | bit] = swap(held[d], bit)
        bit //= 2
    return [held[d] for d in range(n)]


def row_sum(pieces):
    n = lax.axis_size("row")
    held = dict(enumerate(pieces))
    bit = 1
    while bit < n:
        for d in [d for d in sorted(held) if not d & bit]:
            held[d] = held[d] + swap(held.pop(d | bit), bit)
        bit *= 2
    return held[0]


def reordered(block, d):
    n = lax.axis_size("row")
    share = block.shape[1] // n
    return jnp.concatenate(
        [block[:, (d ^ e) * share : ((d ^ e) + 1) * share] for e in range(n)], 1
    )


def general_body(
    zroot,
    panel_one,
    inv_one,
    panel_two_j,
    panel_two_r,
    inv_two,
    parents,
    widths,
    pattern_j,
    pattern_r,
):
    n = lax.axis_size("row")
    width_one = inv_one.shape[1]
    node_rows = width_one // n
    nodes, width_two = inv_two.shape[:2]
    root_rows = zroot.shape[0]

    inverse = own_first(inv_one[0], 1)
    factor = product(panel_one[0], inverse)
    all_factors = lax.all_gather(factor, "col", axis=0)
    gram = crossed(inverse[:, :node_rows], inverse)
    factor_tied, gram = lax.optimization_barrier((factor, gram))
    all_grams = lax.all_gather(gram, "col", axis=0)

    live = (jnp.arange(width_two)[None, :] < widths[:, None]).astype(jnp.float32)
    mask_j = jnp.repeat(pattern_j.astype(jnp.float32), TILE, axis=1)
    mask_r = jnp.repeat(pattern_r.astype(jnp.float32), TILE, axis=1)
    factor_j = []
    factor_r = []
    for i in range(nodes):
        masked_j = panel_two_j[i] * mask_j[i][:, None] * live[i][None, :]
        masked_r = panel_two_r[i] * mask_r[i][:, None] * live[i][None, :]
        factor_j.append(product(masked_j, inv_two[i]))
        factor_r.append(product(masked_r, inv_two[i]))
    near_j = jnp.concatenate(factor_j, 1)
    full_j = jnp.concatenate(row_blocks(near_j), 0)

    root = own_first(zroot, 1)
    full_factor = jnp.concatenate(
        [reordered(block, d) for d, block in enumerate(row_blocks(factor))], 0
    )
    image = product(root, full_factor)
    terms = jnp.sum(factor * image, axis=0).reshape(n, node_rows)
    own_squares = jnp.sum(inverse[:, :node_rows] ** 2, axis=0)
    var_one = (own_squares + row_sum([terms[d] for d in range(n)]))[None, :]

    all_factors, var_one = lax.optimization_barrier((all_factors, var_one))

    parent_factor = [
        lax.dynamic_index_in_dim(all_factors, parents[i], 0, False) for i in range(nodes)
    ]
    reduced = [
        factor_r[i] - product(parent_factor[i], full_j[:, i * width_two : (i + 1) * width_two])
        for i in range(nodes)
    ]
    block_r = []
    sums_j = []
    for i in range(nodes):
        block_r.append(-product(root, jnp.concatenate(row_blocks(reduced[i]), 0)))
        upper = crossed(parent_factor[i], block_r[i]).reshape(n, node_rows, width_two)
        sums_j.append(row_sum([upper[d] for d in range(n)]))
    block_j = []
    for i in range(nodes):
        parent_gram = lax.dynamic_index_in_dim(all_grams, parents[i], 0, False)
        near = product(parent_gram, full_j[:, i * width_two : (i + 1) * width_two])
        block_j.append(-(near + sums_j[i]))

    corrections = jnp.stack(
        [
            jnp.sum(factor_j[i] * block_j[i], axis=0) + jnp.sum(factor_r[i] * block_r[i], axis=0)
            for i in range(nodes)
        ]
    )
    share = width_two // n
    me = lax.axis_index("row")
    ordered = own_first(corrections, 1).reshape(nodes, n, share)
    summed = row_sum([ordered[:, d] for d in range(n)])
    squares = jnp.sum(inv_two * inv_two, axis=1)
    live_share = lax.dynamic_slice_in_dim(live, me * share, share, 1)
    square_share = lax.dynamic_slice_in_dim(squares, me * share, share, 1)
    var_two = live_share * (square_share - summed)
    return (var_one, var_two, jnp.stack(block_j), jnp.stack(block_r))


PIECE = 32
RING = 8
AHEAD = 4
STEP = 128


def mm(left, right):
    return jnp.dot(left, right, precision=PRECISION, preferred_element_type=jnp.float32)


def mm_t(left, right):
    return lax.dot_general(
        left, right, (((0,), (0,)), ((), ())), precision=PRECISION, preferred_element_type=jnp.float32
    )


def line_kernel(
    parents,
    widths,
    tiles_j,
    tiles_r,
    zroot,
    panel_one,
    inv_one,
    panel_j,
    panel_r,
    inv_two,
    var_one,
    var_two,
    z_j,
    z_r,
    root,
    own,
    near_j,
    near_r,
    held,
    staged,
    full_j,
    chosen,
    reduced,
    across,
    beside,
    part_in,
    part_y,
    note,
    vec_a,
    vec_b,
    loads,
    note_send,
    note_recv,
    line_send,
    line_recv,
    j_send,
    j_recv,
    g_send,
    g_recv,
    r_send,
    r_recv,
    u_send,
    u_recv,
    a_send,
    a_recv,
    b_send,
    b_recv,
):
    rows = root.shape[0]
    width = own.shape[1]
    node = near_j.shape[0]
    nodes, _, two = z_r.shape
    chunks = own.shape[0] // PIECE
    steps = rows // STEP
    per = STEP // PIECE
    half = width // 2

    z = lax.axis_index("col")
    r = lax.axis_index("row")
    core = r % 2
    side = r // 2
    twin = r + 1 - 2 * core
    over = (r + 2) % 4
    diag = (twin + 2) % 4
    inner = jnp.logical_or(z == 1, z == 2)
    outer = jnp.logical_not(inner)

    def remote(src, dst, send, recv, device):
        return pltpu.make_async_remote_copy(
            src_ref=src,
            dst_ref=dst,
            send_sem=send,
            recv_sem=recv,
            device_id=device,
            device_id_type=pl.DeviceIdType.MESH,
        )

    def at_row(index):
        return (lax.axis_index("groups"), index, z)

    def at_col(index):
        return (lax.axis_index("groups"), r, index)

    def span(index, size):
        return pl.ds(pl.multiple_of(index * size, size), size)

    def child(m):
        return pl.ds(m * two, two)

    def load(k):
        if k == 0:
            return pltpu.make_async_copy(panel_one.at[0], own.at[pl.ds(0, rows)], loads.at[0])
        if k < 3:
            h = k - 1
            return pltpu.make_async_copy(inv_one.at[0, pl.ds(h * half, half)], chosen.at[h], loads.at[k])
        if k < 5:
            m = k - 3
            return pltpu.make_async_copy(panel_j.at[m], near_j.at[:, child(m)], loads.at[k])
        if k == 5:
            return pltpu.make_async_copy(inv_two, part_in, loads.at[5])
        if k < 8:
            m = k - 6
            return pltpu.make_async_copy(panel_r.at[m], near_r.at[:, child(m)], loads.at[k])
        return pltpu.make_async_copy(zroot, root, loads.at[8])

    for k in range(9):
        load(k).start()

    barrier = pltpu.get_barrier_semaphore()

    def greet(device):
        pl.semaphore_signal(barrier, inc=1, device_id=device, device_id_type=pl.DeviceIdType.MESH)

    for peer in (twin, over, diag):
        greet(at_row(peer))

    @pl.when(outer)
    def _():
        greet(at_col(1 + z // 3))

    @pl.when(inner)
    def _():
        greet(at_col(3 - z))
        greet(at_col(((z - 1) * 3) % 4))

    low = z < 2
    place = jnp.where(low, z, 3 - z)
    kin = [jnp.where(low, parents[m], 3 - parents[m]) for m in range(nodes)]
    picks = [
        jnp.where(place == 1, (kin[m] + 3) % 4, jnp.where(kin[m] == 0, 0, 1 + m)) for m in range(nodes)
    ]
    note[0] = jnp.zeros(note.shape[1:], jnp.int32)
    for m in range(nodes):
        note[0, m : m + 1, :] = jnp.full((1, width), kin[m], jnp.int32)

    @pl.when(outer)
    def _():
        pl.semaphore_wait(barrier, 4)

    @pl.when(inner)
    def _():
        pl.semaphore_wait(barrier, 5)

    def note_copy():
        return remote(note.at[0], note.at[1], note_send, note_recv, at_col(1 + z // 3))

    @pl.when(outer)
    def _():
        note_copy().start()

    def line(stream, t):
        at = span(t, PIECE)
        if stream == 0:
            src, dst, device = own.at[at], held.at[2, at], at_col(1 + z // 3)
        elif stream == 1:
            src, dst, device = own.at[at], held.at[0, at], at_col(3 - z)
        elif stream == 2:
            src, dst, device = held.at[2, at], held.at[1, at], at_col(3 - z)
        else:
            src = staged.at[stream - 3, span(t % RING, PIECE)]
            dst, device = held.at[stream - 3, at], at_col(((z - 1) * 3) % 4)
        return remote(src, dst, line_send.at[stream, t], line_recv.at[stream, t], device)

    def to_inner(first, last):
        @pl.when(outer)
        def _():
            def go(t, carry):
                line(0, t).start()
                return carry

            lax.fori_loop(first, last, go, 0)

    def forward(t):
        line(0, t).wait_recv()
        line(2, t).start()

    def chunk(t):
        @pl.when(inner)
        def _():
            @pl.when(t + AHEAD < chunks)
            def _():
                line(1, t + AHEAD).start()
                forward(t + AHEAD)

            line(1, t).wait_recv()
            line(2, t).wait_recv()
            at = span(t, PIECE)
            for m in range(nodes):
                pick = note[1, m : m + 1, :]

                @pl.when(t >= RING)
                def _():
                    line(3 + m, t - RING).wait_send()

                staged[m, span(t % RING, PIECE), :] = jnp.where(
                    pick < 2, own[at, :], jnp.where(pick == 2, held[0, at, :], held[1, at, :])
                )
                line(3 + m, t).start()

        @pl.when(outer)
        def _():
            line(3, t).wait_recv()
            line(4, t).wait_recv()

    def j_copy(k):
        mine = span(r, node)
        theirs = span(over, node)
        if k == 2:
            return remote(full_j.at[theirs], full_j.at[theirs], j_send.at[2], j_recv.at[2], at_row(twin))
        return remote(near_j, full_j.at[mine], j_send.at[k], j_recv.at[k], at_row(over if k == 0 else twin))

    def g_copy(k):
        at = span(core, rows)
        top = pl.ds(0, rows)
        if k == 0:
            columns = span(1 - side, half)
            return remote(own.at[top, columns], across.at[at], g_send.at[0], g_recv.at[0], at_row(over))
        if k == 1:
            columns = span(1 - core, half)
            return remote(own.at[top, columns], beside, g_send.at[1], g_recv.at[1], at_row(twin))
        return remote(across.at[at], across.at[at], g_send.at[2], g_recv.at[2], at_row(twin))

    def r_copy(k, step):
        who = over if k == 2 else r
        at = pl.ds(pl.multiple_of(who * rows + step * STEP, STEP), STEP)
        return remote(
            reduced.at[at],
            reduced.at[at],
            r_send.at[k, step],
            r_recv.at[k, step],
            at_row(over if k == 0 else twin),
        )

    def pick_rows(m, at):
        pick = picks[m]
        first = jnp.where(pick == 0, own[at, :], held[0, at, :])
        second = jnp.where(pick == 2, held[1, at, :], held[2, at, :])
        return jnp.where(pick < 2, first, second)

    def reduce_step(step):
        at = span(step, STEP)
        to = pl.ds(pl.multiple_of(r * rows + step * STEP, STEP), STEP)
        for m in range(nodes):
            block = pick_rows(m, at)
            chosen[m, at, :] = block
            reduced[to, child(m)] = near_r[at, child(m)] - mm(block, full_j[:, child(m)])
        r_copy(0, step).start()
        r_copy(1, step).start()

    def gather_step(step):
        r_copy(0, step).wait_recv()
        r_copy(2, step).start()

    def root_wait(step):
        r_copy(1, step).wait_recv()
        r_copy(2, step).wait_recv()

    def root_step(step, m):
        places = [pl.ds(pl.multiple_of(d * rows + step * STEP, STEP), STEP) for d in range(4)]
        left = jnp.concatenate([root[:, at] for at in places], 1)
        right = jnp.concatenate([reduced[at, child(m)] for at in places], 0)
        z_r[m] -= mm(left, right)

    def to_tile(vec):
        return jnp.concatenate([vec[:, i * 128 : (i + 1) * 128] for i in range(vec.shape[1] // 128)], 0)

    def shared(pieces):
        total = jnp.zeros_like(pieces[0])
        for d, one in enumerate(pieces):
            total = total + jnp.where(r == d, one, 0.0)
        return total

    def to_peers(tile, send, recv):
        return [
            remote(tile.at[0], tile.at[1 + k], send.at[k], recv.at[k], at_row(peer))
            for k, peer in enumerate((twin, over, diag))
        ]

    def colsum(left, right):
        return jnp.sum(left * right, axis=0, keepdims=True)

    def factor(first, size):
        at = pl.ds(first, size)
        own[at, :] = mm(own[at, 0:half], chosen[0]) + mm(own[at, half:width], chosen[1])

    for k in range(3):
        load(k).wait()
    factor(0, STEP)
    to_inner(0, per)

    @pl.when(inner)
    def _():
        line(1, 0).start()
        line(1, 1).start()

    factor(STEP, rows - STEP)
    to_inner(per, steps * per)

    @pl.when(inner)
    def _():
        forward(0)
        line(1, 2).start()
        forward(1)
        line(1, 3).start()

    def masked(panel, tiles, at, m, first, count):
        column = lax.broadcasted_iota(jnp.int32, (1, two), 1)
        live = (column < widths[m]).astype(jnp.float32)
        blocks = [
            panel[pl.ds(at + i * TILE, TILE), child(m)] * (live * tiles[m, first + i].astype(jnp.float32))
            for i in range(count)
        ]
        return jnp.concatenate(blocks, 0)

    for k in range(3, 6):
        load(k).wait()
    for m in range(nodes):
        near_j[:, child(m)] = mm(masked(near_j, tiles_j, 0, m, 0, node // TILE), part_in[m])
    for k in (0, 1):
        j_copy(k).start()
    for k in (0, 1):
        g_copy(k).start()

    @pl.when(inner)
    def _():
        forward(2)
        forward(3)
        note_copy().wait_recv()

    full_j[span(r, node), :] = near_j[...]
    for k in range(6, 8):
        load(k).wait()
    for m in range(nodes):
        near_r[:, child(m)] = mm(masked(near_r, tiles_r, 0, m, 0, rows // TILE), part_in[m])
        z_r[m] = jnp.zeros_like(z_r[m])
    chunk(0)

    def gram(k):
        columns = pl.ds(pl.multiple_of(r * node + k * STEP, STEP), STEP)
        own[rows + k * STEP : rows + (k + 1) * STEP, :] = mm_t(chosen[0, :, columns], chosen[0]) + mm_t(
            chosen[1, :, columns], chosen[1]
        )
        to_inner((steps + k) * per, (steps + k + 1) * per)

    gram(0)
    chunk(1)
    gram(1)
    chunk(2)
    squares_one = sum(
        colsum(chosen[h, :, span(r, node)], chosen[h, :, span(r, node)]) for h in range(2)
    )
    squares_two = [colsum(part_in[m], part_in[m]) for m in range(nodes)]
    chunk(3)
    j_copy(0).wait_recv()
    j_copy(2).start()
    j_copy(1).wait_recv()
    j_copy(2).wait_recv()
    reduce_step(0)

    load(8).wait()
    sums = []

    def diagonal(h):
        block = own[0:rows, h * half : (h + 1) * half]
        sums.append(colsum(block, mm(root[:, span(r, rows)], block)))

    chunk(per)
    g_copy(0).wait_recv()
    g_copy(2).start()
    diagonal(0)
    chunk(per + 1)
    gather_step(0)
    diagonal(1)
    chunk(per + 2)
    root_wait(0)
    root_step(0, 0)
    chunk(per + 3)
    reduce_step(1)

    g_copy(1).wait_recv()
    g_copy(2).wait_recv()
    chunk(2 * per)
    root_step(0, 1)
    pair = mm(root[:, span(twin, rows)], beside[...])
    pair = 2.0 * colsum(own[0:rows, span(core, half)], pair)
    chunk(2 * per + 1)
    gather_step(1)
    cross = mm(root[:, span(1 - side, 2 * rows)], across[...])
    cross = 2.0 * colsum(own[0:rows, span(side, half)], cross)
    chunk(2 * per + 2)
    root_wait(1)
    root_step(1, 0)
    chunk(2 * per + 3)
    reduce_step(2)

    chunk(3 * per)
    root_step(1, 1)
    for h in range(2):
        sums[h] = sums[h] + jnp.where(core == h, pair, 0.0) + jnp.where(side == h, cross, 0.0)
    vec_a[0] = to_tile(jnp.concatenate(sums, 1))
    for copy in to_peers(vec_a, a_send, a_recv):
        copy.start()
    chunk(3 * per + 1)
    gather_step(2)
    chunk(3 * per + 2)
    root_wait(2)
    root_step(2, 0)
    chunk(3 * per + 3)
    reduce_step(3)

    def node_step(step):
        at = pl.ds(rows + step * STEP, STEP)
        for m in range(nodes):
            z_j[m, step * STEP : (step + 1) * STEP, :] = mm(pick_rows(m, at), full_j[:, child(m)])

    part_out = across
    part_own = beside

    def upper(m, dest):
        return mm_t(chosen[m, :, span(dest, node)], z_r[m])

    def u_copy(k):
        if k < 2:
            out = part_out.at[pl.ds(k * 2 * node, 2 * node)]
            return remote(out, part_in.at[k], u_send.at[k], u_recv.at[k], at_row(twin))
        out = part_own.at[pl.ds((k - 2) * node, node)]
        return remote(out, part_y.at[k - 2], u_send.at[k], u_recv.at[k], at_row(over))

    def upper_twin(m):
        part_out[m * 2 * node : m * 2 * node + node, :] = upper(m, diag)
        part_out[m * 2 * node + node : (m + 1) * 2 * node, :] = upper(m, twin)
        u_copy(m).start()

    def upper_over(m):
        far = upper(m, over)
        u_copy(m).wait_recv()
        part_own[m * node : (m + 1) * node, :] = far + part_in[m, 0:node, :]
        u_copy(2 + m).start()

    def upper_own(m):
        part_in[m, node : 2 * node, :] = part_in[m, node : 2 * node, :] + upper(m, r)

    base = steps * per
    chunk(base)
    root_step(2, 1)
    chunk(base + 1)
    for k in range(3):
        g_copy(k).wait_send()
    chunk(base + 2)
    gather_step(3)
    root_wait(3)
    root_step(3, 0)
    upper_twin(0)
    root_step(3, 1)
    upper_twin(1)
    chunk(base + 3)
    upper_over(0)
    upper_over(1)
    chunk(base + per)
    node_step(0)
    chunk(base + per + 1)
    for m in range(nodes):
        upper_own(m)
    chunk(base + per + 2)
    for copy in to_peers(vec_a, a_send, a_recv):
        copy.wait()
    total = vec_a[0] + vec_a[1] + vec_a[2] + vec_a[3]
    each = total.shape[0] // 4
    mine = shared([total[d * each : (d + 1) * each, :] for d in range(4)])
    var_one[...] = squares_one + jnp.concatenate([mine[i : i + 1, :] for i in range(each)], 1)
    sums_r = [colsum(near_r[:, child(m)], z_r[m]) for m in range(nodes)]
    chunk(base + per + 3)
    node_step(1)
    for m in range(nodes):
        u_copy(2 + m).wait_recv()
        z_j[m] = -(z_j[m] + part_in[m, node : 2 * node, :] + part_y[m])
        sums_r[m] = sums_r[m] + colsum(near_j[:, child(m)], z_j[m])
    vec_b[0] = to_tile(jnp.concatenate(sums_r, 1))
    for copy in to_peers(vec_b, b_send, b_recv):
        copy.start()

    @pl.when(outer)
    def _():
        note_copy().wait_send()

        def go(t, carry):
            line(0, t).wait_send()
            return carry

        lax.fori_loop(0, chunks, go, 0)

    @pl.when(inner)
    def _():
        def go(t, carry):
            line(1, t).wait_send()
            line(2, t).wait_send()
            return carry

        lax.fori_loop(0, chunks, go, 0)

        def last(t, carry):
            line(3, t).wait_send()
            line(4, t).wait_send()
            return carry

        lax.fori_loop(chunks - RING, chunks, last, 0)

    for k in range(3):
        j_copy(k).wait_send()

    def sent(step, carry):
        for k in range(3):
            r_copy(k, step).wait_send()
        return carry

    lax.fori_loop(0, steps, sent, 0)
    for k in range(4):
        u_copy(k).wait_send()
    for copy in to_peers(vec_b, b_send, b_recv):
        copy.wait()
    total = vec_b[0] + vec_b[1] + vec_b[2] + vec_b[3]
    share = two // 4
    column = lax.broadcasted_iota(jnp.int32, (1, share), 1) + r * share
    for m in range(nodes):
        mine = shared([total[m * 4 + d : m * 4 + d + 1, :] for d in range(4)])
        square = shared([squares_two[m][:, d * share : (d + 1) * share] for d in range(4)])
        live = (column < widths[m]).astype(jnp.float32)
        var_two[m : m + 1, :] = live * (square - mine)


def line_body(
    zroot,
    panel_one,
    inv_one,
    panel_two_j,
    panel_two_r,
    inv_two,
    parents,
    widths,
    pattern_j,
    pattern_r,
):
    n = lax.axis_size("row")
    width = inv_one.shape[1]
    node = width // n
    nodes, two = inv_two.shape[:2]
    rows = zroot.shape[0]
    chunks = (rows + node) // PIECE
    steps = rows // STEP
    f32 = jnp.float32
    smem = pl.BlockSpec(memory_space=pltpu.SMEM)
    hbm = pl.BlockSpec(memory_space=pl.ANY)
    vmem = pl.BlockSpec(memory_space=pltpu.VMEM)
    dma = pltpu.SemaphoreType.DMA
    return pl.pallas_call(
        line_kernel,
        out_shape=(
            jax.ShapeDtypeStruct((1, node), f32),
            jax.ShapeDtypeStruct((nodes, two // n), f32),
            jax.ShapeDtypeStruct((nodes, node, two), f32),
            jax.ShapeDtypeStruct((nodes, rows, two), f32),
        ),
        in_specs=[smem] * 4 + [hbm] * 6,
        out_specs=(vmem,) * 4,
        scratch_shapes=[
            pltpu.VMEM(zroot.shape, f32),
            pltpu.VMEM((rows + node, width), f32),
            pltpu.VMEM((node, nodes * two), f32),
            pltpu.VMEM((rows, nodes * two), f32),
            pltpu.VMEM((3, rows + node, width), f32),
            pltpu.VMEM((nodes, RING * PIECE, width), f32),
            pltpu.VMEM((width, nodes * two), f32),
            pltpu.VMEM((nodes, rows, width), f32),
            pltpu.VMEM((4 * rows, nodes * two), f32),
            pltpu.VMEM((2 * rows, width // 2), f32),
            pltpu.VMEM((rows, width // 2), f32),
            pltpu.VMEM((nodes, 2 * node, two), f32),
            pltpu.VMEM((nodes, node, two), f32),
            pltpu.VMEM((2, 8, width), jnp.int32),
            pltpu.VMEM((4, width // 128, 128), f32),
            pltpu.VMEM((4, nodes * two // 128, 128), f32),
            dma((9,)),
            dma,
            dma,
            dma((5, chunks)),
            dma((5, chunks)),
            dma((3,)),
            dma((3,)),
            dma((3,)),
            dma((3,)),
            dma((3, steps)),
            dma((3, steps)),
            dma((4,)),
            dma((4,)),
            dma((3,)),
            dma((3,)),
            dma((3,)),
            dma((3,)),
        ],
        compiler_params=pltpu.CompilerParams(
            collective_id=0, has_side_effects=True, vmem_limit_bytes=60 * 1024 * 1024
        ),
    )(parents, widths, pattern_j, pattern_r, zroot, panel_one, inv_one, panel_two_j, panel_two_r, inv_two)


def solution(mesh):
    fits = mesh.shape["row"] == 4 and mesh.shape["col"] == 4
    return jax.shard_map(
        line_body if fits else general_body,
        mesh=mesh,
        in_specs=(
            P(("groups", "row"), None),
            P(("groups", "col"), "row", None),
            P(("groups", "col"), None, None),
            P(("groups", "col"), "row", None),
            P(("groups", "col"), "row", None),
            P(("groups", "col"), None, None),
            P(("groups", "col")),
            P(("groups", "col")),
            P(("groups", "col"), "row"),
            P(("groups", "col"), "row"),
        ),
        out_specs=(
            P(("groups", "col"), "row"),
            P(("groups", "col"), "row"),
            P(("groups", "col"), "row", None),
            P(("groups", "col"), "row", None),
        ),
        check_vma=False,
    )
```

```python
import jax
import jax.numpy as jnp
from jax import lax
from jax.experimental import pallas as pl
from jax.experimental.pallas import tpu as pltpu
from jax.sharding import PartitionSpec as P

TILE = 64
PRECISION = lax.Precision.HIGH


def product(left, right):
    return jnp.dot(left, right, precision=PRECISION, preferred_element_type=jnp.float32)


def crossed(left, right):
    return lax.dot_general(
        left, right, (((0,), (0,)), ((), ())), precision=PRECISION, preferred_element_type=jnp.float32
    )


def swap(block, bit):
    n = lax.axis_size("row")
    return lax.ppermute(block, "row", [(i, i ^ bit) for i in range(n)])


def own_first(array, axis):
    n = lax.axis_size("row")
    me = lax.axis_index("row")
    share = array.shape[axis] // n
    pieces = [
        lax.dynamic_slice_in_dim(array, (me ^ d) * share, share, axis) for d in range(n)
    ]
    return jnp.concatenate(pieces, axis)


def row_blocks(block):
    n = lax.axis_size("row")
    held = {0: block}
    bit = n // 2
    while bit:
        for d in sorted(held):
            held[d | bit] = swap(held[d], bit)
        bit //= 2
    return [held[d] for d in range(n)]


def row_sum(pieces):
    n = lax.axis_size("row")
    held = dict(enumerate(pieces))
    bit = 1
    while bit < n:
        for d in [d for d in sorted(held) if not d & bit]:
            held[d] = held[d] + swap(held.pop(d | bit), bit)
        bit *= 2
    return held[0]


def reordered(block, d):
    n = lax.axis_size("row")
    share = block.shape[1] // n
    return jnp.concatenate(
        [block[:, (d ^ e) * share : ((d ^ e) + 1) * share] for e in range(n)], 1
    )


def general_body(
    zroot,
    panel_one,
    inv_one,
    panel_two_j,
    panel_two_r,
    inv_two,
    parents,
    widths,
    pattern_j,
    pattern_r,
):
    n = lax.axis_size("row")
    width_one = inv_one.shape[1]
    node_rows = width_one // n
    nodes, width_two = inv_two.shape[:2]
    root_rows = zroot.shape[0]

    inverse = own_first(inv_one[0], 1)
    factor = product(panel_one[0], inverse)
    all_factors = lax.all_gather(factor, "col", axis=0)
    gram = crossed(inverse[:, :node_rows], inverse)
    factor_tied, gram = lax.optimization_barrier((factor, gram))
    all_grams = lax.all_gather(gram, "col", axis=0)

    live = (jnp.arange(width_two)[None, :] < widths[:, None]).astype(jnp.float32)
    mask_j = jnp.repeat(pattern_j.astype(jnp.float32), TILE, axis=1)
    mask_r = jnp.repeat(pattern_r.astype(jnp.float32), TILE, axis=1)
    factor_j = []
    factor_r = []
    for i in range(nodes):
        masked_j = panel_two_j[i] * mask_j[i][:, None] * live[i][None, :]
        masked_r = panel_two_r[i] * mask_r[i][:, None] * live[i][None, :]
        factor_j.append(product(masked_j, inv_two[i]))
        factor_r.append(product(masked_r, inv_two[i]))
    near_j = jnp.concatenate(factor_j, 1)
    full_j = jnp.concatenate(row_blocks(near_j), 0)

    root = own_first(zroot, 1)
    full_factor = jnp.concatenate(
        [reordered(block, d) for d, block in enumerate(row_blocks(factor))], 0
    )
    image = product(root, full_factor)
    terms = jnp.sum(factor * image, axis=0).reshape(n, node_rows)
    own_squares = jnp.sum(inverse[:, :node_rows] ** 2, axis=0)
    var_one = (own_squares + row_sum([terms[d] for d in range(n)]))[None, :]

    all_factors, var_one = lax.optimization_barrier((all_factors, var_one))

    parent_factor = [
        lax.dynamic_index_in_dim(all_factors, parents[i], 0, False) for i in range(nodes)
    ]
    reduced = [
        factor_r[i] - product(parent_factor[i], full_j[:, i * width_two : (i + 1) * width_two])
        for i in range(nodes)
    ]
    block_r = []
    sums_j = []
    for i in range(nodes):
        block_r.append(-product(root, jnp.concatenate(row_blocks(reduced[i]), 0)))
        upper = crossed(parent_factor[i], block_r[i]).reshape(n, node_rows, width_two)
        sums_j.append(row_sum([upper[d] for d in range(n)]))
    block_j = []
    for i in range(nodes):
        parent_gram = lax.dynamic_index_in_dim(all_grams, parents[i], 0, False)
        near = product(parent_gram, full_j[:, i * width_two : (i + 1) * width_two])
        block_j.append(-(near + sums_j[i]))

    corrections = jnp.stack(
        [
            jnp.sum(factor_j[i] * block_j[i], axis=0) + jnp.sum(factor_r[i] * block_r[i], axis=0)
            for i in range(nodes)
        ]
    )
    share = width_two // n
    me = lax.axis_index("row")
    ordered = own_first(corrections, 1).reshape(nodes, n, share)
    summed = row_sum([ordered[:, d] for d in range(n)])
    squares = jnp.sum(inv_two * inv_two, axis=1)
    live_share = lax.dynamic_slice_in_dim(live, me * share, share, 1)
    square_share = lax.dynamic_slice_in_dim(squares, me * share, share, 1)
    var_two = live_share * (square_share - summed)
    return (var_one, var_two, jnp.stack(block_j), jnp.stack(block_r))


PIECE = 16
RING = 16
AHEAD = 8
STEP = 128


def mm(left, right):
    return jnp.dot(left, right, precision=PRECISION, preferred_element_type=jnp.float32)


def mm_t(left, right):
    return lax.dot_general(
        left, right, (((0,), (0,)), ((), ())), precision=PRECISION, preferred_element_type=jnp.float32
    )


def line_kernel(
    parents,
    widths,
    tiles_j,
    tiles_r,
    zroot,
    panel_one,
    inv_one,
    panel_j,
    panel_r,
    inv_two,
    var_one,
    var_two,
    z_j,
    z_r,
    root,
    own,
    near_j,
    near_r,
    held,
    staged,
    full_j,
    chosen,
    reduced,
    across,
    beside,
    part_in,
    part_y,
    note,
    vec_a,
    vec_b,
    loads,
    note_send,
    note_recv,
    line_send,
    line_recv,
    j_send,
    j_recv,
    g_send,
    g_recv,
    r_send,
    r_recv,
    u_send,
    u_recv,
    a_send,
    a_recv,
    b_send,
    b_recv,
):
    rows = root.shape[0]
    width = own.shape[1]
    node = near_j.shape[0]
    nodes, _, two = z_r.shape
    chunks = own.shape[0] // PIECE
    steps = rows // STEP
    per = STEP // PIECE
    half = width // 2

    z = lax.axis_index("col")
    r = lax.axis_index("row")
    core = r % 2
    side = r // 2
    twin = r + 1 - 2 * core
    over = (r + 2) % 4
    diag = (twin + 2) % 4
    inner = jnp.logical_or(z == 1, z == 2)
    outer = jnp.logical_not(inner)

    def remote(src, dst, send, recv, device):
        return pltpu.make_async_remote_copy(
            src_ref=src,
            dst_ref=dst,
            send_sem=send,
            recv_sem=recv,
            device_id=device,
            device_id_type=pl.DeviceIdType.MESH,
        )

    def at_row(index):
        return (lax.axis_index("groups"), index, z)

    def at_col(index):
        return (lax.axis_index("groups"), r, index)

    def span(index, size):
        return pl.ds(pl.multiple_of(index * size, size), size)

    def child(m):
        return pl.ds(m * two, two)

    def load(k):
        if k == 0:
            return pltpu.make_async_copy(panel_one.at[0], own.at[pl.ds(0, rows)], loads.at[0])
        if k < 3:
            h = k - 1
            return pltpu.make_async_copy(inv_one.at[0, pl.ds(h * half, half)], chosen.at[h], loads.at[k])
        if k < 5:
            m = k - 3
            return pltpu.make_async_copy(panel_j.at[m], near_j.at[:, child(m)], loads.at[k])
        if k == 5:
            return pltpu.make_async_copy(inv_two, part_in, loads.at[5])
        if k < 8:
            m = k - 6
            return pltpu.make_async_copy(panel_r.at[m], near_r.at[:, child(m)], loads.at[k])
        return pltpu.make_async_copy(zroot, root, loads.at[8])

    for k in range(9):
        load(k).start()

    barrier = pltpu.get_barrier_semaphore()

    def greet(device):
        pl.semaphore_signal(barrier, inc=1, device_id=device, device_id_type=pl.DeviceIdType.MESH)

    for peer in (twin, over, diag):
        greet(at_row(peer))

    @pl.when(outer)
    def _():
        greet(at_col(1 + z // 3))

    @pl.when(inner)
    def _():
        greet(at_col(3 - z))
        greet(at_col(((z - 1) * 3) % 4))

    low = z < 2
    place = jnp.where(low, z, 3 - z)
    kin = [jnp.where(low, parents[m], 3 - parents[m]) for m in range(nodes)]
    picks = [
        jnp.where(place == 1, (kin[m] + 3) % 4, jnp.where(kin[m] == 0, 0, 1 + m)) for m in range(nodes)
    ]
    note[0] = jnp.zeros(note.shape[1:], jnp.int32)
    for m in range(nodes):
        note[0, m : m + 1, :] = jnp.full((1, width), kin[m], jnp.int32)

    @pl.when(outer)
    def _():
        pl.semaphore_wait(barrier, 4)

    @pl.when(inner)
    def _():
        pl.semaphore_wait(barrier, 5)

    def note_copy():
        return remote(note.at[0], note.at[1], note_send, note_recv, at_col(1 + z // 3))

    @pl.when(outer)
    def _():
        note_copy().start()

    def line(stream, t):
        at = span(t, PIECE)
        if stream == 0:
            src, dst, device = own.at[at], held.at[2, at], at_col(1 + z // 3)
        elif stream == 1:
            src, dst, device = own.at[at], held.at[0, at], at_col(3 - z)
        elif stream == 2:
            src, dst, device = held.at[2, at], held.at[1, at], at_col(3 - z)
        else:
            src = staged.at[stream - 3, span(t % RING, PIECE)]
            dst, device = held.at[stream - 3, at], at_col(((z - 1) * 3) % 4)
        return remote(src, dst, line_send.at[stream, t], line_recv.at[stream, t], device)

    def to_inner(first, last):
        @pl.when(outer)
        def _():
            def go(t, carry):
                line(0, t).start()
                return carry

            lax.fori_loop(first, last, go, 0)

    def forward(t):
        line(0, t).wait_recv()
        line(2, t).start()

    def chunk(t):
        @pl.when(inner)
        def _():
            @pl.when(t + AHEAD < chunks)
            def _():
                line(1, t + AHEAD).start()
                forward(t + AHEAD)

            line(1, t).wait_recv()
            line(2, t).wait_recv()
            at = span(t, PIECE)
            for m in range(nodes):
                pick = note[1, m : m + 1, :]

                @pl.when(t >= RING)
                def _():
                    line(3 + m, t - RING).wait_send()

                staged[m, span(t % RING, PIECE), :] = jnp.where(
                    pick < 2, own[at, :], jnp.where(pick == 2, held[0, at, :], held[1, at, :])
                )
                line(3 + m, t).start()

        @pl.when(outer)
        def _():
            line(3, t).wait_recv()
            line(4, t).wait_recv()

    def quarter(q):
        def go(t, carry):
            chunk(t)
            return carry

        lax.fori_loop(q * per // 4, (q + 1) * per // 4, go, 0)

    def j_copy(k):
        mine = span(r, node)
        theirs = span(over, node)
        if k == 2:
            return remote(full_j.at[theirs], full_j.at[theirs], j_send.at[2], j_recv.at[2], at_row(twin))
        return remote(near_j, full_j.at[mine], j_send.at[k], j_recv.at[k], at_row(over if k == 0 else twin))

    def g_copy(k):
        if k == 4:
            at = pl.ds(0, rows)
            columns = span(1 - core, half)
            return remote(own.at[at, columns], beside, g_send.at[4], g_recv.at[4], at_row(twin))
        top = pl.ds(k // 2 * (rows // 2), rows // 2)
        at = pl.ds(pl.multiple_of(core * rows + k // 2 * (rows // 2), rows // 2), rows // 2)
        if k % 2 == 0:
            columns = span(1 - side, half)
            return remote(own.at[top, columns], across.at[at], g_send.at[k], g_recv.at[k], at_row(over))
        return remote(across.at[at], across.at[at], g_send.at[k], g_recv.at[k], at_row(twin))

    def r_copy(k, step):
        who = over if k == 2 else r
        at = pl.ds(pl.multiple_of(who * rows + step * STEP, STEP), STEP)
        return remote(
            reduced.at[at],
            reduced.at[at],
            r_send.at[k, step],
            r_recv.at[k, step],
            at_row(over if k == 0 else twin),
        )

    def pick_rows(m, at):
        pick = picks[m]
        first = jnp.where(pick == 0, own[at, :], held[0, at, :])
        second = jnp.where(pick == 2, held[1, at, :], held[2, at, :])
        return jnp.where(pick < 2, first, second)

    def reduce_step(step):
        at = span(step, STEP)
        to = pl.ds(pl.multiple_of(r * rows + step * STEP, STEP), STEP)
        for m in range(nodes):
            block = pick_rows(m, at)
            chosen[m, at, :] = block
            reduced[to, child(m)] = near_r[at, child(m)] - mm(block, full_j[:, child(m)])
        r_copy(0, step).start()
        r_copy(1, step).start()

    def gather_step(step):
        r_copy(0, step).wait_recv()
        r_copy(2, step).start()

    def root_wait(step):
        r_copy(1, step).wait_recv()
        r_copy(2, step).wait_recv()

    def root_step(step, m):
        places = [pl.ds(pl.multiple_of(d * rows + step * STEP, STEP), STEP) for d in range(4)]
        left = jnp.concatenate([root[:, at] for at in places], 1)
        right = jnp.concatenate([reduced[at, child(m)] for at in places], 0)
        z_r[m] -= mm(left, right)

    def to_tile(vec):
        return jnp.concatenate([vec[:, i * 128 : (i + 1) * 128] for i in range(vec.shape[1] // 128)], 0)

    def shared(pieces):
        total = jnp.zeros_like(pieces[0])
        for d, one in enumerate(pieces):
            total = total + jnp.where(r == d, one, 0.0)
        return total

    def to_peers(tile, send, recv):
        return [
            remote(tile.at[0], tile.at[1 + k], send.at[k], recv.at[k], at_row(peer))
            for k, peer in enumerate((twin, over, diag))
        ]

    def colsum(left, right):
        return jnp.sum(left * right, axis=0, keepdims=True)

    def factor(first, size):
        at = pl.ds(first, size)
        own[at, :] = mm(own[at, 0:half], chosen[0]) + mm(own[at, half:width], chosen[1])

    for k in range(3):
        load(k).wait()
    factor(0, STEP)
    to_inner(0, per)
    early = AHEAD // 2

    @pl.when(inner)
    def _():
        for t in range(early):
            line(1, t).start()

    factor(STEP, rows - STEP)
    to_inner(per, steps * per)

    @pl.when(inner)
    def _():
        for t in range(early):
            forward(t)
            line(1, early + t).start()

    def masked(panel, tiles, at, m, first, count):
        column = lax.broadcasted_iota(jnp.int32, (1, two), 1)
        live = (column < widths[m]).astype(jnp.float32)
        blocks = [
            panel[pl.ds(at + i * TILE, TILE), child(m)] * (live * tiles[m, first + i].astype(jnp.float32))
            for i in range(count)
        ]
        return jnp.concatenate(blocks, 0)

    for k in range(3, 6):
        load(k).wait()
    for m in range(nodes):
        near_j[:, child(m)] = mm(masked(near_j, tiles_j, 0, m, 0, node // TILE), part_in[m])
    for k in (0, 1):
        j_copy(k).start()
    g_copy(4).start()

    @pl.when(inner)
    def _():
        for t in range(early, AHEAD):
            forward(t)
        note_copy().wait_recv()

    full_j[span(r, node), :] = near_j[...]
    quarter(0)
    for k in range(6, 8):
        load(k).wait()
    for m in range(nodes):
        near_r[:, child(m)] = mm(masked(near_r, tiles_r, 0, m, 0, rows // TILE), part_in[m])
        z_r[m] = jnp.zeros_like(z_r[m])

    def gram(k):
        columns = pl.ds(pl.multiple_of(r * node + k * STEP, STEP), STEP)
        own[rows + k * STEP : rows + (k + 1) * STEP, :] = mm_t(chosen[0, :, columns], chosen[0]) + mm_t(
            chosen[1, :, columns], chosen[1]
        )
        to_inner((steps + k) * per, (steps + k + 1) * per)

    quarter(1)
    gram(0)
    quarter(2)
    gram(1)
    squares_one = sum(
        colsum(chosen[h, :, span(r, node)], chosen[h, :, span(r, node)]) for h in range(2)
    )
    squares_two = [colsum(part_in[m], part_in[m]) for m in range(nodes)]
    quarter(3)
    j_copy(0).wait_recv()
    j_copy(2).start()
    j_copy(1).wait_recv()
    j_copy(2).wait_recv()
    reduce_step(0)

    load(8).wait()
    sums = []

    def diagonal(h):
        block = own[0:rows, h * half : (h + 1) * half]
        sums.append(colsum(block, mm(root[:, span(r, rows)], block)))

    quarter(4)
    diagonal(0)
    quarter(5)
    diagonal(1)
    quarter(6)
    gather_step(0)
    g_copy(0).start()
    quarter(7)
    reduce_step(1)

    quarter(8)
    root_wait(0)
    root_step(0, 0)
    quarter(9)
    root_step(0, 1)
    g_copy(4).wait_recv()
    pair = mm(root[:, span(twin, rows)], beside[...])
    pair = 2.0 * colsum(own[0:rows, span(core, half)], pair)
    quarter(10)
    g_copy(0).wait_recv()
    g_copy(1).start()
    gather_step(1)
    g_copy(2).start()
    quarter(11)
    reduce_step(2)

    quarter(12)
    root_wait(1)
    root_step(1, 0)
    quarter(13)
    root_step(1, 1)
    quarter(14)
    g_copy(2).wait_recv()
    g_copy(3).start()
    gather_step(2)
    quarter(15)
    reduce_step(3)

    def node_step(step):
        at = pl.ds(rows + step * STEP, STEP)
        for m in range(nodes):
            z_j[m, step * STEP : (step + 1) * STEP, :] = mm(pick_rows(m, at), full_j[:, child(m)])

    part_out = across
    part_own = beside

    def upper(m, dest):
        return mm_t(chosen[m, :, span(dest, node)], z_r[m])

    def u_copy(k):
        if k < 2:
            out = part_out.at[pl.ds(k * 2 * node, 2 * node)]
            return remote(out, part_in.at[k], u_send.at[k], u_recv.at[k], at_row(twin))
        out = part_own.at[pl.ds((k - 2) * node, node)]
        return remote(out, part_y.at[k - 2], u_send.at[k], u_recv.at[k], at_row(over))

    def upper_twin(m):
        part_out[m * 2 * node : m * 2 * node + node, :] = upper(m, diag)
        part_out[m * 2 * node + node : (m + 1) * 2 * node, :] = upper(m, twin)
        u_copy(m).start()

    def upper_over(m):
        far = upper(m, over)
        u_copy(m).wait_recv()
        part_own[m * node : (m + 1) * node, :] = far + part_in[m, 0:node, :]
        u_copy(2 + m).start()

    def upper_own(m):
        part_in[m, node : 2 * node, :] = part_in[m, node : 2 * node, :] + upper(m, r)

    quarter(16)
    root_wait(2)
    root_step(2, 0)
    root_step(2, 1)
    g_copy(1).wait_recv()
    g_copy(3).wait_recv()
    quarter(17)
    cross = mm(root[:, span(1 - side, 2 * rows)], across[...])
    cross = 2.0 * colsum(own[0:rows, span(side, half)], cross)
    for h in range(2):
        sums[h] = sums[h] + jnp.where(core == h, pair, 0.0) + jnp.where(side == h, cross, 0.0)
    vec_a[0] = to_tile(jnp.concatenate(sums, 1))
    for copy in to_peers(vec_a, a_send, a_recv):
        copy.start()
    for k in range(5):
        g_copy(k).wait_send()
    quarter(18)
    gather_step(3)
    root_wait(3)
    root_step(3, 0)
    upper_twin(0)
    root_step(3, 1)
    upper_twin(1)
    quarter(19)
    upper_over(0)
    upper_over(1)
    quarter(20)
    node_step(0)
    quarter(21)
    for m in range(nodes):
        upper_own(m)
    quarter(22)
    for copy in to_peers(vec_a, a_send, a_recv):
        copy.wait()
    total = vec_a[0] + vec_a[1] + vec_a[2] + vec_a[3]
    each = total.shape[0] // 4
    mine = shared([total[d * each : (d + 1) * each, :] for d in range(4)])
    var_one[...] = squares_one + jnp.concatenate([mine[i : i + 1, :] for i in range(each)], 1)
    sums_r = [colsum(near_r[:, child(m)], z_r[m]) for m in range(nodes)]
    quarter(23)
    node_step(1)
    for m in range(nodes):
        u_copy(2 + m).wait_recv()
        z_j[m] = -(z_j[m] + part_in[m, node : 2 * node, :] + part_y[m])
        sums_r[m] = sums_r[m] + colsum(near_j[:, child(m)], z_j[m])
    vec_b[0] = to_tile(jnp.concatenate(sums_r, 1))
    for copy in to_peers(vec_b, b_send, b_recv):
        copy.start()

    @pl.when(outer)
    def _():
        note_copy().wait_send()

        def go(t, carry):
            line(0, t).wait_send()
            return carry

        lax.fori_loop(0, chunks, go, 0)

    @pl.when(inner)
    def _():
        def go(t, carry):
            line(1, t).wait_send()
            line(2, t).wait_send()
            return carry

        lax.fori_loop(0, chunks, go, 0)

        def last(t, carry):
            line(3, t).wait_send()
            line(4, t).wait_send()
            return carry

        lax.fori_loop(chunks - RING, chunks, last, 0)

    for k in range(3):
        j_copy(k).wait_send()

    def sent(step, carry):
        for k in range(3):
            r_copy(k, step).wait_send()
        return carry

    lax.fori_loop(0, steps, sent, 0)
    for k in range(4):
        u_copy(k).wait_send()
    for copy in to_peers(vec_b, b_send, b_recv):
        copy.wait()
    total = vec_b[0] + vec_b[1] + vec_b[2] + vec_b[3]
    share = two // 4
    column = lax.broadcasted_iota(jnp.int32, (1, share), 1) + r * share
    for m in range(nodes):
        mine = shared([total[m * 4 + d : m * 4 + d + 1, :] for d in range(4)])
        square = shared([squares_two[m][:, d * share : (d + 1) * share] for d in range(4)])
        live = (column < widths[m]).astype(jnp.float32)
        var_two[m : m + 1, :] = live * (square - mine)


def copy_kernel(*refs):
    sems = refs[-1]
    order = (3, 2, 0, 1)
    ins = [pltpu.make_async_copy(refs[k], refs[8 + k], sems.at[k]) for k in order]
    outs = [pltpu.make_async_copy(refs[8 + k], refs[4 + k], sems.at[4 + k]) for k in order]
    for copy in ins:
        copy.start()
    for first, second in zip(ins, outs):
        first.wait()
        second.start()
    for copy in outs:
        copy.wait()


def line_body(
    zroot,
    panel_one,
    inv_one,
    panel_two_j,
    panel_two_r,
    inv_two,
    parents,
    widths,
    pattern_j,
    pattern_r,
):
    n = lax.axis_size("row")
    width = inv_one.shape[1]
    node = width // n
    nodes, two = inv_two.shape[:2]
    rows = zroot.shape[0]
    chunks = (rows + node) // PIECE
    steps = rows // STEP
    f32 = jnp.float32
    smem = pl.BlockSpec(memory_space=pltpu.SMEM)
    hbm = pl.BlockSpec(memory_space=pl.ANY)
    vmem = pl.BlockSpec(memory_space=pltpu.VMEM)
    dma = pltpu.SemaphoreType.DMA
    results = pl.pallas_call(
        line_kernel,
        out_shape=(
            jax.ShapeDtypeStruct((1, node), f32),
            jax.ShapeDtypeStruct((nodes, two // n), f32),
            jax.ShapeDtypeStruct((nodes, node, two), f32),
            jax.ShapeDtypeStruct((nodes, rows, two), f32),
        ),
        in_specs=[smem] * 4 + [hbm] * 6,
        out_specs=(vmem,) * 4,
        scratch_shapes=[
            pltpu.VMEM(zroot.shape, f32),
            pltpu.VMEM((rows + node, width), f32),
            pltpu.VMEM((node, nodes * two), f32),
            pltpu.VMEM((rows, nodes * two), f32),
            pltpu.VMEM((3, rows + node, width), f32),
            pltpu.VMEM((nodes, RING * PIECE, width), f32),
            pltpu.VMEM((width, nodes * two), f32),
            pltpu.VMEM((nodes, rows, width), f32),
            pltpu.VMEM((4 * rows, nodes * two), f32),
            pltpu.VMEM((2 * rows, width // 2), f32),
            pltpu.VMEM((rows, width // 2), f32),
            pltpu.VMEM((nodes, 2 * node, two), f32),
            pltpu.VMEM((nodes, node, two), f32),
            pltpu.VMEM((2, 8, width), jnp.int32),
            pltpu.VMEM((4, width // 128, 128), f32),
            pltpu.VMEM((4, nodes * two // 128, 128), f32),
            dma((9,)),
            dma,
            dma,
            dma((5, chunks)),
            dma((5, chunks)),
            dma((3,)),
            dma((3,)),
            dma((5,)),
            dma((5,)),
            dma((3, steps)),
            dma((3, steps)),
            dma((4,)),
            dma((4,)),
            dma((3,)),
            dma((3,)),
            dma((3,)),
            dma((3,)),
        ],
        compiler_params=pltpu.CompilerParams(
            collective_id=0, has_side_effects=True, vmem_limit_bytes=60 * 1024 * 1024
        ),
    )(parents, widths, pattern_j, pattern_r, zroot, panel_one, inv_one, panel_two_j, panel_two_r, inv_two)
    return pl.pallas_call(
        copy_kernel,
        out_shape=tuple(jax.ShapeDtypeStruct(one.shape, one.dtype) for one in results),
        in_specs=[hbm] * 4,
        out_specs=(hbm,) * 4,
        scratch_shapes=[pltpu.VMEM(one.shape, one.dtype) for one in results] + [dma((8,))],
        compiler_params=pltpu.CompilerParams(vmem_limit_bytes=60 * 1024 * 1024),
    )(*results)


def solution(mesh):
    fits = mesh.shape["row"] == 4 and mesh.shape["col"] == 4
    return jax.shard_map(
        line_body if fits else general_body,
        mesh=mesh,
        in_specs=(
            P(("groups", "row"), None),
            P(("groups", "col"), "row", None),
            P(("groups", "col"), None, None),
            P(("groups", "col"), "row", None),
            P(("groups", "col"), "row", None),
            P(("groups", "col"), None, None),
            P(("groups", "col")),
            P(("groups", "col")),
            P(("groups", "col"), "row"),
            P(("groups", "col"), "row"),
        ),
        out_specs=(
            P(("groups", "col"), "row"),
            P(("groups", "col"), "row"),
            P(("groups", "col"), "row", None),
            P(("groups", "col"), "row", None),
        ),
        check_vma=False,
    )
```

```python
import functools

import jax
import jax.numpy as jnp
from jax import lax
from jax.experimental import pallas as pl
from jax.experimental.pallas import tpu as pltpu
from jax.sharding import PartitionSpec as P

TILE = 64
PRECISION = lax.Precision.HIGH


def product(left, right):
    return jnp.dot(left, right, precision=PRECISION, preferred_element_type=jnp.float32)


def crossed(left, right):
    return lax.dot_general(
        left, right, (((0,), (0,)), ((), ())), precision=PRECISION, preferred_element_type=jnp.float32
    )


def swap(block, bit):
    n = lax.axis_size("row")
    return lax.ppermute(block, "row", [(i, i ^ bit) for i in range(n)])


def own_first(array, axis):
    n = lax.axis_size("row")
    me = lax.axis_index("row")
    share = array.shape[axis] // n
    pieces = [
        lax.dynamic_slice_in_dim(array, (me ^ d) * share, share, axis) for d in range(n)
    ]
    return jnp.concatenate(pieces, axis)


def row_blocks(block):
    n = lax.axis_size("row")
    held = {0: block}
    bit = n // 2
    while bit:
        for d in sorted(held):
            held[d | bit] = swap(held[d], bit)
        bit //= 2
    return [held[d] for d in range(n)]


def row_sum(pieces):
    n = lax.axis_size("row")
    held = dict(enumerate(pieces))
    bit = 1
    while bit < n:
        for d in [d for d in sorted(held) if not d & bit]:
            held[d] = held[d] + swap(held.pop(d | bit), bit)
        bit *= 2
    return held[0]


def reordered(block, d):
    n = lax.axis_size("row")
    share = block.shape[1] // n
    return jnp.concatenate(
        [block[:, (d ^ e) * share : ((d ^ e) + 1) * share] for e in range(n)], 1
    )


def general_body(
    zroot,
    panel_one,
    inv_one,
    panel_two_j,
    panel_two_r,
    inv_two,
    parents,
    widths,
    pattern_j,
    pattern_r,
):
    n = lax.axis_size("row")
    width_one = inv_one.shape[1]
    node_rows = width_one // n
    nodes, width_two = inv_two.shape[:2]
    root_rows = zroot.shape[0]

    inverse = own_first(inv_one[0], 1)
    factor = product(panel_one[0], inverse)
    all_factors = lax.all_gather(factor, "col", axis=0)
    gram = crossed(inverse[:, :node_rows], inverse)
    factor_tied, gram = lax.optimization_barrier((factor, gram))
    all_grams = lax.all_gather(gram, "col", axis=0)

    live = (jnp.arange(width_two)[None, :] < widths[:, None]).astype(jnp.float32)
    mask_j = jnp.repeat(pattern_j.astype(jnp.float32), TILE, axis=1)
    mask_r = jnp.repeat(pattern_r.astype(jnp.float32), TILE, axis=1)
    factor_j = []
    factor_r = []
    for i in range(nodes):
        masked_j = panel_two_j[i] * mask_j[i][:, None] * live[i][None, :]
        masked_r = panel_two_r[i] * mask_r[i][:, None] * live[i][None, :]
        factor_j.append(product(masked_j, inv_two[i]))
        factor_r.append(product(masked_r, inv_two[i]))
    near_j = jnp.concatenate(factor_j, 1)
    full_j = jnp.concatenate(row_blocks(near_j), 0)

    root = own_first(zroot, 1)
    full_factor = jnp.concatenate(
        [reordered(block, d) for d, block in enumerate(row_blocks(factor))], 0
    )
    image = product(root, full_factor)
    terms = jnp.sum(factor * image, axis=0).reshape(n, node_rows)
    own_squares = jnp.sum(inverse[:, :node_rows] ** 2, axis=0)
    var_one = (own_squares + row_sum([terms[d] for d in range(n)]))[None, :]

    all_factors, var_one = lax.optimization_barrier((all_factors, var_one))

    parent_factor = [
        lax.dynamic_index_in_dim(all_factors, parents[i], 0, False) for i in range(nodes)
    ]
    reduced = [
        factor_r[i] - product(parent_factor[i], full_j[:, i * width_two : (i + 1) * width_two])
        for i in range(nodes)
    ]
    block_r = []
    sums_j = []
    for i in range(nodes):
        block_r.append(-product(root, jnp.concatenate(row_blocks(reduced[i]), 0)))
        upper = crossed(parent_factor[i], block_r[i]).reshape(n, node_rows, width_two)
        sums_j.append(row_sum([upper[d] for d in range(n)]))
    block_j = []
    for i in range(nodes):
        parent_gram = lax.dynamic_index_in_dim(all_grams, parents[i], 0, False)
        near = product(parent_gram, full_j[:, i * width_two : (i + 1) * width_two])
        block_j.append(-(near + sums_j[i]))

    corrections = jnp.stack(
        [
            jnp.sum(factor_j[i] * block_j[i], axis=0) + jnp.sum(factor_r[i] * block_r[i], axis=0)
            for i in range(nodes)
        ]
    )
    share = width_two // n
    me = lax.axis_index("row")
    ordered = own_first(corrections, 1).reshape(nodes, n, share)
    summed = row_sum([ordered[:, d] for d in range(n)])
    squares = jnp.sum(inv_two * inv_two, axis=1)
    live_share = lax.dynamic_slice_in_dim(live, me * share, share, 1)
    square_share = lax.dynamic_slice_in_dim(squares, me * share, share, 1)
    var_two = live_share * (square_share - summed)
    return (var_one, var_two, jnp.stack(block_j), jnp.stack(block_r))


PIECE = 16
RING = 16
AHEAD = 8
STEP = 128


def mm(left, right):
    return jnp.dot(left, right, precision=PRECISION, preferred_element_type=jnp.float32)


def mm_t(left, right):
    return lax.dot_general(
        left, right, (((0,), (0,)), ((), ())), precision=PRECISION, preferred_element_type=jnp.float32
    )


def line_kernel(
    parents,
    widths,
    tiles_j,
    tiles_r,
    zroot,
    panel_one,
    inv_one,
    panel_j,
    panel_r,
    inv_two,
    var_one,
    var_two,
    z_j,
    z_r,
    root,
    own,
    near_j,
    near_r,
    part_out,
    part_own,
    held,
    staged,
    full_j,
    chosen,
    reduced,
    across,
    beside,
    part_in,
    part_y,
    note,
    vec_a,
    vec_b,
    loads,
    note_send,
    note_recv,
    line_send,
    line_recv,
    j_send,
    j_recv,
    g_send,
    g_recv,
    r_send,
    r_recv,
    u_send,
    u_recv,
    a_send,
    a_recv,
    b_send,
    b_recv,
):
    rows = root.shape[0]
    width = own.shape[1]
    node = near_j.shape[0]
    nodes, _, two = z_r.shape
    chunks = own.shape[0] // PIECE
    steps = rows // STEP
    per = STEP // PIECE
    half = width // 2

    z = lax.axis_index("col")
    r = lax.axis_index("row")
    core = r % 2
    side = r // 2
    twin = r + 1 - 2 * core
    over = (r + 2) % 4
    diag = (twin + 2) % 4
    inner = jnp.logical_or(z == 1, z == 2)
    outer = jnp.logical_not(inner)

    def remote(src, dst, send, recv, device):
        return pltpu.make_async_remote_copy(
            src_ref=src,
            dst_ref=dst,
            send_sem=send,
            recv_sem=recv,
            device_id=device,
            device_id_type=pl.DeviceIdType.MESH,
        )

    def at_row(index):
        return (lax.axis_index("groups"), index, z)

    def at_col(index):
        return (lax.axis_index("groups"), r, index)

    def span(index, size):
        return pl.ds(pl.multiple_of(index * size, size), size)

    def child(m):
        return pl.ds(m * two, two)

    def load(k):
        if k == 0:
            return pltpu.make_async_copy(panel_one.at[0], own.at[pl.ds(0, rows)], loads.at[0])
        if k < 3:
            h = k - 1
            return pltpu.make_async_copy(inv_one.at[0, pl.ds(h * half, half)], chosen.at[h], loads.at[k])
        if k < 5:
            m = k - 3
            return pltpu.make_async_copy(panel_j.at[m], near_j.at[:, child(m)], loads.at[k])
        if k == 5:
            return pltpu.make_async_copy(inv_two, part_in, loads.at[5])
        if k < 8:
            m = k - 6
            return pltpu.make_async_copy(panel_r.at[m], near_r.at[:, child(m)], loads.at[k])
        return pltpu.make_async_copy(zroot, root, loads.at[8])

    for k in range(3):
        load(k).start()

    barrier = pltpu.get_barrier_semaphore()

    def greet(device):
        pl.semaphore_signal(barrier, inc=1, device_id=device, device_id_type=pl.DeviceIdType.MESH)

    for peer in (twin, over, diag):
        greet(at_row(peer))

    @pl.when(outer)
    def _():
        greet(at_col(1 + z // 3))

    @pl.when(inner)
    def _():
        greet(at_col(3 - z))
        greet(at_col(((z - 1) * 3) % 4))

    low = z < 2
    place = jnp.where(low, z, 3 - z)
    kin = [jnp.where(low, parents[m], 3 - parents[m]) for m in range(nodes)]
    picks = [
        jnp.where(place == 1, (kin[m] + 3) % 4, jnp.where(kin[m] == 0, 0, 1 + m)) for m in range(nodes)
    ]
    note[0] = jnp.zeros(note.shape[1:], jnp.int32)
    for m in range(nodes):
        note[0, m : m + 1, :] = jnp.full((1, width), kin[m], jnp.int32)

    @pl.when(outer)
    def _():
        pl.semaphore_wait(barrier, 4)

    @pl.when(inner)
    def _():
        pl.semaphore_wait(barrier, 5)

    def note_copy():
        return remote(note.at[0], note.at[1], note_send, note_recv, at_col(1 + z // 3))

    @pl.when(outer)
    def _():
        note_copy().start()

    def line(stream, t):
        at = span(t, PIECE)
        if stream == 0:
            src, dst, device = own.at[at], held.at[2, at], at_col(1 + z // 3)
        elif stream == 1:
            src, dst, device = own.at[at], held.at[0, at], at_col(3 - z)
        elif stream == 2:
            src, dst, device = held.at[2, at], held.at[1, at], at_col(3 - z)
        else:
            src = staged.at[stream - 3, span(t % RING, PIECE)]
            dst, device = held.at[stream - 3, at], at_col(((z - 1) * 3) % 4)
        return remote(src, dst, line_send.at[stream, t], line_recv.at[stream, t], device)

    def to_inner(first, last):
        @pl.when(outer)
        def _():
            def go(t, carry):
                line(0, t).start()
                return carry

            lax.fori_loop(first, last, go, 0)

    def forward(t):
        line(0, t).wait_recv()
        line(2, t).start()

    def chunk(t):
        @pl.when(inner)
        def _():
            @pl.when(t + AHEAD < chunks)
            def _():
                line(1, t + AHEAD).start()
                forward(t + AHEAD)

            line(1, t).wait_recv()
            line(2, t).wait_recv()
            at = span(t, PIECE)
            for m in range(nodes):
                pick = note[1, m : m + 1, :]

                @pl.when(t >= RING)
                def _():
                    line(3 + m, t - RING).wait_send()

                staged[m, span(t % RING, PIECE), :] = jnp.where(
                    pick < 2, own[at, :], jnp.where(pick == 2, held[0, at, :], held[1, at, :])
                )
                line(3 + m, t).start()

        @pl.when(outer)
        def _():
            line(3, t).wait_recv()
            line(4, t).wait_recv()

    def j_copy(k):
        mine = span(r, node)
        theirs = span(over, node)
        if k == 2:
            return remote(full_j.at[theirs], full_j.at[theirs], j_send.at[2], j_recv.at[2], at_row(twin))
        return remote(near_j, full_j.at[mine], j_send.at[k], j_recv.at[k], at_row(over if k == 0 else twin))

    def g_copy(k):
        if k == 4:
            at = pl.ds(0, rows)
            columns = span(1 - core, half)
            return remote(own.at[at, columns], beside, g_send.at[4], g_recv.at[4], at_row(twin))
        top = pl.ds(k // 2 * (rows // 2), rows // 2)
        at = pl.ds(pl.multiple_of(core * rows + k // 2 * (rows // 2), rows // 2), rows // 2)
        if k % 2 == 0:
            columns = span(1 - side, half)
            return remote(own.at[top, columns], across.at[at], g_send.at[k], g_recv.at[k], at_row(over))
        return remote(across.at[at], across.at[at], g_send.at[k], g_recv.at[k], at_row(twin))

    spans = [(k * STEP, STEP) for k in range(steps - 1)]
    spans += [((steps - 1) * STEP, STEP // 2), ((steps - 1) * STEP + STEP // 2, STEP // 2)]

    def r_copy(k, part):
        first, size = spans[part]
        who = over if k == 2 else r
        at = pl.ds(pl.multiple_of(who * rows + first, size), size)
        return remote(
            reduced.at[at],
            reduced.at[at],
            r_send.at[k, part],
            r_recv.at[k, part],
            at_row(over if k == 0 else twin),
        )

    def pick_rows(m, at):
        pick = picks[m]
        first = jnp.where(pick == 0, own[at, :], held[0, at, :])
        second = jnp.where(pick == 2, held[1, at, :], held[2, at, :])
        return jnp.where(pick < 2, first, second)

    def reduce_part(part, m):
        first, size = spans[part]
        at = pl.ds(first, size)
        to = pl.ds(pl.multiple_of(r * rows + first, size), size)
        block = pick_rows(m, at)
        chosen[m, at, :] = block
        reduced[to, child(m)] = near_r[at, child(m)] - mm(block, full_j[:, child(m)])
        if m == nodes - 1:
            r_copy(0, part).start()
            r_copy(1, part).start()

    def gather_part(part):
        r_copy(0, part).wait_recv()
        r_copy(2, part).start()

    def root_wait(part):
        r_copy(1, part).wait_recv()
        r_copy(2, part).wait_recv()

    def root_step(step, m):
        places = [pl.ds(pl.multiple_of(d * rows + step * STEP, STEP), STEP) for d in range(4)]
        left = jnp.concatenate([root[:, at] for at in places], 1)
        right = jnp.concatenate([reduced[at, child(m)] for at in places], 0)
        z_r[m] -= mm(left, right)

    def to_tile(vec):
        return jnp.concatenate([vec[:, i * 128 : (i + 1) * 128] for i in range(vec.shape[1] // 128)], 0)

    def shared(pieces):
        total = jnp.zeros_like(pieces[0])
        for d, one in enumerate(pieces):
            total = total + jnp.where(r == d, one, 0.0)
        return total

    def to_peers(tile, send, recv):
        return [
            remote(tile.at[0], tile.at[1 + k], send.at[k], recv.at[k], at_row(peer))
            for k, peer in enumerate((twin, over, diag))
        ]

    def colsum(left, right):
        return jnp.sum(left * right, axis=0, keepdims=True)

    def factor(first, size):
        at = pl.ds(first, size)
        own[at, :] = mm(own[at, 0:half], chosen[0]) + mm(own[at, half:width], chosen[1])

    def masked(panel, tiles, at, m, first, count):
        column = lax.broadcasted_iota(jnp.int32, (1, two), 1)
        live = (column < widths[m]).astype(jnp.float32)
        blocks = [
            panel[pl.ds(at + i * TILE, TILE), child(m)] * (live * tiles[m, first + i].astype(jnp.float32))
            for i in range(count)
        ]
        return jnp.concatenate(blocks, 0)

    for k in range(3):
        load(k).wait()
    for k in range(3, 9):
        load(k).start()
    factor(0, STEP)
    to_inner(0, per)
    early = 2

    @pl.when(inner)
    def _():
        for t in range(early):
            line(1, t).start()

    for k in range(3, 6):
        load(k).wait()
    for m in range(nodes):
        near_j[:, child(m)] = mm(masked(near_j, tiles_j, 0, m, 0, node // TILE), part_in[m])
    for k in (0, 1):
        j_copy(k).start()

    def pass_on(first, last):
        @pl.when(inner)
        def _():
            for t in range(first, last):
                forward(t)
                if t + early < AHEAD:
                    line(1, t + early).start()

    share = AHEAD // steps
    pass_on(0, share)
    for k in range(1, steps):
        factor(k * STEP, STEP)
        to_inner(k * per, (k + 1) * per)
        pass_on(k * share, (k + 1) * share)
    g_copy(4).start()

    @pl.when(inner)
    def _():
        note_copy().wait_recv()

    full_j[span(r, node), :] = near_j[...]
    for m in range(nodes):
        z_r[m] = jnp.zeros_like(z_r[m])

    def separator_rows(m):
        load(6 + m).wait()
        near_r[:, child(m)] = mm(masked(near_r, tiles_r, 0, m, 0, rows // TILE), part_in[m])

    def gram(k):
        columns = pl.ds(pl.multiple_of(r * node + k * STEP, STEP), STEP)
        own[rows + k * STEP : rows + (k + 1) * STEP, :] = mm_t(chosen[0, :, columns], chosen[0]) + mm_t(
            chosen[1, :, columns], chosen[1]
        )
        to_inner((steps + k) * per, (steps + k + 1) * per)

    one = {}

    def square_sums():
        one["squares"] = sum(
            colsum(chosen[h, :, span(r, node)], chosen[h, :, span(r, node)]) for h in range(2)
        )
        one["squares_two"] = [colsum(part_in[m], part_in[m]) for m in range(nodes)]

    def gathered_j():
        j_copy(0).wait_recv()
        j_copy(2).start()
        j_copy(1).wait_recv()
        j_copy(2).wait_recv()

    def diagonal(h):
        block = own[0:rows, h * half : (h + 1) * half]
        one[h] = colsum(block, mm(root[:, span(r, rows)], block))

    def pair():
        g_copy(4).wait_recv()
        product_two = mm(root[:, span(twin, rows)], beside[...])
        one["pair"] = 2.0 * colsum(own[0:rows, span(core, half)], product_two)

    def cross():
        g_copy(1).wait_recv()
        g_copy(3).wait_recv()
        product_two = mm(root[:, span(1 - side, 2 * rows)], across[...])
        product_two = 2.0 * colsum(own[0:rows, span(side, half)], product_two)
        sums = [
            one[h] + jnp.where(core == h, one["pair"], 0.0) + jnp.where(side == h, product_two, 0.0)
            for h in range(2)
        ]
        vec_a[0] = to_tile(jnp.concatenate(sums, 1))
        for copy in to_peers(vec_a, a_send, a_recv):
            copy.start()

    def level_one_out():
        for copy in to_peers(vec_a, a_send, a_recv):
            copy.wait()
        total = vec_a[0] + vec_a[1] + vec_a[2] + vec_a[3]
        each = total.shape[0] // 4
        mine = shared([total[d * each : (d + 1) * each, :] for d in range(4)])
        var_one[...] = one["squares"] + jnp.concatenate([mine[i : i + 1, :] for i in range(each)], 1)

    def pass_g(k):
        g_copy(k).wait_recv()
        g_copy(k + 1).start()

    def node_step(step, m):
        at = pl.ds(rows + step * STEP, STEP)
        z_j[m, step * STEP : (step + 1) * STEP, :] = mm(pick_rows(m, at), full_j[:, child(m)])

    def upper(m, dest):
        return mm_t(chosen[m, :, span(dest, node)], z_r[m])

    def u_copy(k):
        if k < 2:
            out = part_out.at[pl.ds(k * 2 * node, 2 * node)]
            return remote(out, part_in.at[k], u_send.at[k], u_recv.at[k], at_row(twin))
        out = part_own.at[pl.ds((k - 2) * node, node)]
        return remote(out, part_y.at[k - 2], u_send.at[k], u_recv.at[k], at_row(over))

    def upper_twin(m):
        part_out[m * 2 * node : m * 2 * node + node, :] = upper(m, diag)
        part_out[m * 2 * node + node : (m + 1) * 2 * node, :] = upper(m, twin)
        u_copy(m).start()

    def upper_over(m):
        far = upper(m, over)
        u_copy(m).wait_recv()
        part_own[m * node : (m + 1) * node, :] = far + part_in[m, 0:node, :]
        u_copy(2 + m).start()

    def upper_own(m):
        part_in[m, node : 2 * node, :] = part_in[m, node : 2 * node, :] + upper(m, r)

    def separator_sums():
        one["sums_r"] = [colsum(near_r[:, child(m)], z_r[m]) for m in range(nodes)]

    def item(function, *arguments):
        return functools.partial(function, *arguments)

    work = {
        0: [item(separator_rows, 0)],
        1: [item(separator_rows, 1)],
        2: [item(gram, 0)],
        4: [item(gram, 1)],
        5: [square_sums],
        7: [gathered_j, item(reduce_part, 0, 0)],
        8: [item(reduce_part, 0, 1)],
        9: [load(8).wait, item(diagonal, 0)],
        11: [item(diagonal, 1)],
        14: [item(gather_part, 0), g_copy(0).start],
        15: [item(reduce_part, 1, 0)],
        16: [item(reduce_part, 1, 1)],
        17: [item(root_wait, 0), item(root_step, 0, 0)],
        18: [item(root_step, 0, 1)],
        19: [pair],
        22: [item(pass_g, 0), item(gather_part, 1), g_copy(2).start],
        23: [item(reduce_part, 2, 0)],
        24: [item(reduce_part, 2, 1)],
        25: [item(root_wait, 1), item(root_step, 1, 0)],
        26: [item(root_step, 1, 1)],
        27: [item(reduce_part, 3, 0)],
        28: [item(reduce_part, 3, 1)],
        29: [item(pass_g, 2)],
        30: [item(gather_part, 2)],
        31: [item(reduce_part, 4, 0), item(reduce_part, 4, 1)],
        32: [item(root_wait, 2), item(root_step, 2, 0)],
        33: [item(root_step, 2, 1), item(gather_part, 3)],
        35: [item(gather_part, 4), item(root_wait, 3), item(root_wait, 4), item(root_step, 3, 0)],
        36: [item(upper_twin, 0)],
        37: [item(upper_over, 0), item(root_step, 3, 1)],
        38: [item(upper_twin, 1)],
        39: [item(upper_over, 1)],
        40: [cross],
        41: [item(node_step, 0, 0)],
        42: [item(node_step, 0, 1)],
        43: [item(upper_own, 0)],
        44: [item(upper_own, 1)],
        45: [level_one_out],
        46: [separator_sums],
    }
    done = 0
    for last in sorted(work) + [chunks - 1]:
        if last == done:
            chunk(last)
        else:

            def go(t, carry):
                chunk(t)
                return carry

            lax.fori_loop(done, last + 1, go, 0)
        done = last + 1
        for function in work.get(last, ()):
            function()

    sums_r = one["sums_r"]
    for m in range(nodes):
        node_step(1, m)
    for m in range(nodes):
        u_copy(2 + m).wait_recv()
        z_j[m] = -(z_j[m] + part_in[m, node : 2 * node, :] + part_y[m])
        sums_r[m] = sums_r[m] + colsum(near_j[:, child(m)], z_j[m])
    vec_b[0] = to_tile(jnp.concatenate(sums_r, 1))
    for copy in to_peers(vec_b, b_send, b_recv):
        copy.start()

    @pl.when(outer)
    def _():
        note_copy().wait_send()

        def go(t, carry):
            line(0, t).wait_send()
            return carry

        lax.fori_loop(0, chunks, go, 0)

    @pl.when(inner)
    def _():
        def go(t, carry):
            line(1, t).wait_send()
            line(2, t).wait_send()
            return carry

        lax.fori_loop(0, chunks, go, 0)

        def last(t, carry):
            line(3, t).wait_send()
            line(4, t).wait_send()
            return carry

        lax.fori_loop(chunks - RING, chunks, last, 0)

    for k in range(3):
        j_copy(k).wait_send()
    for k in range(5):
        g_copy(k).wait_send()
    for part in range(len(spans)):
        for k in range(3):
            r_copy(k, part).wait_send()
    for k in range(4):
        u_copy(k).wait_send()
    for copy in to_peers(vec_b, b_send, b_recv):
        copy.wait()
    total = vec_b[0] + vec_b[1] + vec_b[2] + vec_b[3]
    share = two // 4
    column = lax.broadcasted_iota(jnp.int32, (1, share), 1) + r * share
    for m in range(nodes):
        mine = shared([total[m * 4 + d : m * 4 + d + 1, :] for d in range(4)])
        square = shared([one["squares_two"][m][:, d * share : (d + 1) * share] for d in range(4)])
        live = (column < widths[m]).astype(jnp.float32)
        var_two[m : m + 1, :] = live * (square - mine)


def copy_kernel(*refs):
    sems = refs[-1]
    order = (3, 2, 0, 1)
    ins = [pltpu.make_async_copy(refs[k], refs[8 + k], sems.at[k]) for k in order]
    outs = [pltpu.make_async_copy(refs[8 + k], refs[4 + k], sems.at[4 + k]) for k in order]
    for copy in ins:
        copy.start()
    for first, second in zip(ins, outs):
        first.wait()
        second.start()
    for copy in outs:
        copy.wait()


def line_body(
    zroot,
    panel_one,
    inv_one,
    panel_two_j,
    panel_two_r,
    inv_two,
    parents,
    widths,
    pattern_j,
    pattern_r,
):
    n = lax.axis_size("row")
    width = inv_one.shape[1]
    node = width // n
    nodes, two = inv_two.shape[:2]
    rows = zroot.shape[0]
    chunks = (rows + node) // PIECE
    steps = rows // STEP
    f32 = jnp.float32
    smem = pl.BlockSpec(memory_space=pltpu.SMEM)
    hbm = pl.BlockSpec(memory_space=pl.ANY)
    vmem = pl.BlockSpec(memory_space=pltpu.VMEM)
    dma = pltpu.SemaphoreType.DMA
    results = pl.pallas_call(
        line_kernel,
        out_shape=(
            jax.ShapeDtypeStruct((1, node), f32),
            jax.ShapeDtypeStruct((nodes, two // n), f32),
            jax.ShapeDtypeStruct((nodes, node, two), f32),
            jax.ShapeDtypeStruct((nodes, rows, two), f32),
        ),
        in_specs=[smem] * 4 + [hbm] * 6,
        out_specs=(vmem,) * 4,
        scratch_shapes=[
            pltpu.VMEM(zroot.shape, f32),
            pltpu.VMEM((rows + node, width), f32),
            pltpu.VMEM((node, nodes * two), f32),
            pltpu.VMEM((rows, nodes * two), f32),
            pltpu.VMEM((nodes * 2 * node, two), f32),
            pltpu.VMEM((nodes * node, two), f32),
            pltpu.VMEM((3, rows + node, width), f32),
            pltpu.VMEM((nodes, RING * PIECE, width), f32),
            pltpu.VMEM((width, nodes * two), f32),
            pltpu.VMEM((nodes, rows, width), f32),
            pltpu.VMEM((4 * rows, nodes * two), f32),
            pltpu.VMEM((2 * rows, width // 2), f32),
            pltpu.VMEM((rows, width // 2), f32),
            pltpu.VMEM((nodes, 2 * node, two), f32),
            pltpu.VMEM((nodes, node, two), f32),
            pltpu.VMEM((2, 8, width), jnp.int32),
            pltpu.VMEM((4, width // 128, 128), f32),
            pltpu.VMEM((4, nodes * two // 128, 128), f32),
            dma((9,)),
            dma,
            dma,
            dma((5, chunks)),
            dma((5, chunks)),
            dma((3,)),
            dma((3,)),
            dma((5,)),
            dma((5,)),
            dma((3, steps + 1)),
            dma((3, steps + 1)),
            dma((4,)),
            dma((4,)),
            dma((3,)),
            dma((3,)),
            dma((3,)),
            dma((3,)),
        ],
        compiler_params=pltpu.CompilerParams(
            collective_id=0, has_side_effects=True, vmem_limit_bytes=60 * 1024 * 1024
        ),
    )(parents, widths, pattern_j, pattern_r, zroot, panel_one, inv_one, panel_two_j, panel_two_r, inv_two)
    return pl.pallas_call(
        copy_kernel,
        out_shape=tuple(jax.ShapeDtypeStruct(one.shape, one.dtype) for one in results),
        in_specs=[hbm] * 4,
        out_specs=(hbm,) * 4,
        scratch_shapes=[pltpu.VMEM(one.shape, one.dtype) for one in results] + [dma((8,))],
        compiler_params=pltpu.CompilerParams(vmem_limit_bytes=60 * 1024 * 1024),
    )(*results)


def solution(mesh):
    fits = mesh.shape["row"] == 4 and mesh.shape["col"] == 4
    return jax.shard_map(
        line_body if fits else general_body,
        mesh=mesh,
        in_specs=(
            P(("groups", "row"), None),
            P(("groups", "col"), "row", None),
            P(("groups", "col"), None, None),
            P(("groups", "col"), "row", None),
            P(("groups", "col"), "row", None),
            P(("groups", "col"), None, None),
            P(("groups", "col")),
            P(("groups", "col")),
            P(("groups", "col"), "row"),
            P(("groups", "col"), "row"),
        ),
        out_specs=(
            P(("groups", "col"), "row"),
            P(("groups", "col"), "row"),
            P(("groups", "col"), "row", None),
            P(("groups", "col"), "row", None),
        ),
        check_vma=False,
    )
```

```python
import functools

import jax
import jax.numpy as jnp
from jax import lax
from jax.experimental import pallas as pl
from jax.experimental.pallas import tpu as pltpu
from jax.sharding import PartitionSpec as P

TILE = 64
PRECISION = lax.Precision.HIGH


def product(left, right):
    return jnp.dot(left, right, precision=PRECISION, preferred_element_type=jnp.float32)


def crossed(left, right):
    return lax.dot_general(
        left, right, (((0,), (0,)), ((), ())), precision=PRECISION, preferred_element_type=jnp.float32
    )


def swap(block, bit):
    n = lax.axis_size("row")
    return lax.ppermute(block, "row", [(i, i ^ bit) for i in range(n)])


def own_first(array, axis):
    n = lax.axis_size("row")
    me = lax.axis_index("row")
    share = array.shape[axis] // n
    pieces = [
        lax.dynamic_slice_in_dim(array, (me ^ d) * share, share, axis) for d in range(n)
    ]
    return jnp.concatenate(pieces, axis)


def row_blocks(block):
    n = lax.axis_size("row")
    held = {0: block}
    bit = n // 2
    while bit:
        for d in sorted(held):
            held[d | bit] = swap(held[d], bit)
        bit //= 2
    return [held[d] for d in range(n)]


def row_sum(pieces):
    n = lax.axis_size("row")
    held = dict(enumerate(pieces))
    bit = 1
    while bit < n:
        for d in [d for d in sorted(held) if not d & bit]:
            held[d] = held[d] + swap(held.pop(d | bit), bit)
        bit *= 2
    return held[0]


def reordered(block, d):
    n = lax.axis_size("row")
    share = block.shape[1] // n
    return jnp.concatenate(
        [block[:, (d ^ e) * share : ((d ^ e) + 1) * share] for e in range(n)], 1
    )


def general_body(
    zroot,
    panel_one,
    inv_one,
    panel_two_j,
    panel_two_r,
    inv_two,
    parents,
    widths,
    pattern_j,
    pattern_r,
):
    n = lax.axis_size("row")
    width_one = inv_one.shape[1]
    node_rows = width_one // n
    nodes, width_two = inv_two.shape[:2]
    root_rows = zroot.shape[0]

    inverse = own_first(inv_one[0], 1)
    factor = product(panel_one[0], inverse)
    all_factors = lax.all_gather(factor, "col", axis=0)
    gram = crossed(inverse[:, :node_rows], inverse)
    factor_tied, gram = lax.optimization_barrier((factor, gram))
    all_grams = lax.all_gather(gram, "col", axis=0)

    live = (jnp.arange(width_two)[None, :] < widths[:, None]).astype(jnp.float32)
    mask_j = jnp.repeat(pattern_j.astype(jnp.float32), TILE, axis=1)
    mask_r = jnp.repeat(pattern_r.astype(jnp.float32), TILE, axis=1)
    factor_j = []
    factor_r = []
    for i in range(nodes):
        masked_j = panel_two_j[i] * mask_j[i][:, None] * live[i][None, :]
        masked_r = panel_two_r[i] * mask_r[i][:, None] * live[i][None, :]
        factor_j.append(product(masked_j, inv_two[i]))
        factor_r.append(product(masked_r, inv_two[i]))
    near_j = jnp.concatenate(factor_j, 1)
    full_j = jnp.concatenate(row_blocks(near_j), 0)

    root = own_first(zroot, 1)
    full_factor = jnp.concatenate(
        [reordered(block, d) for d, block in enumerate(row_blocks(factor))], 0
    )
    image = product(root, full_factor)
    terms = jnp.sum(factor * image, axis=0).reshape(n, node_rows)
    own_squares = jnp.sum(inverse[:, :node_rows] ** 2, axis=0)
    var_one = (own_squares + row_sum([terms[d] for d in range(n)]))[None, :]

    all_factors, var_one = lax.optimization_barrier((all_factors, var_one))

    parent_factor = [
        lax.dynamic_index_in_dim(all_factors, parents[i], 0, False) for i in range(nodes)
    ]
    reduced = [
        factor_r[i] - product(parent_factor[i], full_j[:, i * width_two : (i + 1) * width_two])
        for i in range(nodes)
    ]
    block_r = []
    sums_j = []
    for i in range(nodes):
        block_r.append(-product(root, jnp.concatenate(row_blocks(reduced[i]), 0)))
        upper = crossed(parent_factor[i], block_r[i]).reshape(n, node_rows, width_two)
        sums_j.append(row_sum([upper[d] for d in range(n)]))
    block_j = []
    for i in range(nodes):
        parent_gram = lax.dynamic_index_in_dim(all_grams, parents[i], 0, False)
        near = product(parent_gram, full_j[:, i * width_two : (i + 1) * width_two])
        block_j.append(-(near + sums_j[i]))

    corrections = jnp.stack(
        [
            jnp.sum(factor_j[i] * block_j[i], axis=0) + jnp.sum(factor_r[i] * block_r[i], axis=0)
            for i in range(nodes)
        ]
    )
    share = width_two // n
    me = lax.axis_index("row")
    ordered = own_first(corrections, 1).reshape(nodes, n, share)
    summed = row_sum([ordered[:, d] for d in range(n)])
    squares = jnp.sum(inv_two * inv_two, axis=1)
    live_share = lax.dynamic_slice_in_dim(live, me * share, share, 1)
    square_share = lax.dynamic_slice_in_dim(squares, me * share, share, 1)
    var_two = live_share * (square_share - summed)
    return (var_one, var_two, jnp.stack(block_j), jnp.stack(block_r))


PIECE = 16
RING = 16
AHEAD = 8
STEP = 128


def mm(left, right):
    return jnp.dot(left, right, precision=PRECISION, preferred_element_type=jnp.float32)


def mm_t(left, right):
    return lax.dot_general(
        left, right, (((0,), (0,)), ((), ())), precision=PRECISION, preferred_element_type=jnp.float32
    )


def line_kernel(
    parents,
    widths,
    tiles_j,
    tiles_r,
    zroot,
    panel_one,
    inv_one,
    panel_j,
    panel_r,
    inv_two,
    var_one,
    var_two,
    z_j,
    z_r,
    root,
    own,
    near_j,
    near_r,
    part_out,
    part_own,
    held,
    staged,
    full_j,
    chosen,
    reduced,
    across,
    beside,
    part_in,
    part_y,
    note,
    vec_a,
    vec_b,
    loads,
    note_send,
    note_recv,
    line_send,
    line_recv,
    j_send,
    j_recv,
    g_send,
    g_recv,
    r_send,
    r_recv,
    u_send,
    u_recv,
    a_send,
    a_recv,
    b_send,
    b_recv,
):
    rows = root.shape[0]
    width = own.shape[1]
    node = near_j.shape[0]
    nodes, _, two = z_r.shape
    chunks = own.shape[0] // PIECE
    steps = rows // STEP
    per = STEP // PIECE
    half = width // 2

    z = lax.axis_index("col")
    r = lax.axis_index("row")
    core = r % 2
    side = r // 2
    twin = r + 1 - 2 * core
    over = (r + 2) % 4
    diag = (twin + 2) % 4
    inner = jnp.logical_or(z == 1, z == 2)
    outer = jnp.logical_not(inner)

    def remote(src, dst, send, recv, device):
        return pltpu.make_async_remote_copy(
            src_ref=src,
            dst_ref=dst,
            send_sem=send,
            recv_sem=recv,
            device_id=device,
            device_id_type=pl.DeviceIdType.MESH,
        )

    def at_row(index):
        return (lax.axis_index("groups"), index, z)

    def at_col(index):
        return (lax.axis_index("groups"), r, index)

    def span(index, size):
        return pl.ds(pl.multiple_of(index * size, size), size)

    def child(m):
        return pl.ds(m * two, two)

    def load(k):
        if k == 0:
            return pltpu.make_async_copy(panel_one.at[0], own.at[pl.ds(0, rows)], loads.at[0])
        if k < 3:
            h = k - 1
            return pltpu.make_async_copy(inv_one.at[0, pl.ds(h * half, half)], chosen.at[h], loads.at[k])
        if k < 5:
            m = k - 3
            return pltpu.make_async_copy(panel_j.at[m], near_j.at[:, child(m)], loads.at[k])
        if k == 5:
            return pltpu.make_async_copy(inv_two, part_in, loads.at[5])
        if k < 8:
            m = k - 6
            return pltpu.make_async_copy(panel_r.at[m], near_r.at[:, child(m)], loads.at[k])
        return pltpu.make_async_copy(zroot, root, loads.at[8])

    for k in range(3):
        load(k).start()

    barrier = pltpu.get_barrier_semaphore()

    def greet(device):
        pl.semaphore_signal(barrier, inc=1, device_id=device, device_id_type=pl.DeviceIdType.MESH)

    for peer in (twin, over, diag):
        greet(at_row(peer))

    @pl.when(outer)
    def _():
        greet(at_col(1 + z // 3))

    @pl.when(inner)
    def _():
        greet(at_col(3 - z))
        greet(at_col(((z - 1) * 3) % 4))

    low = z < 2
    place = jnp.where(low, z, 3 - z)
    kin = [jnp.where(low, parents[m], 3 - parents[m]) for m in range(nodes)]
    picks = [
        jnp.where(place == 1, (kin[m] + 3) % 4, jnp.where(kin[m] == 0, 0, 1 + m)) for m in range(nodes)
    ]
    note[0] = jnp.zeros(note.shape[1:], jnp.int32)
    for m in range(nodes):
        note[0, m : m + 1, :] = jnp.full((1, width), kin[m], jnp.int32)

    @pl.when(outer)
    def _():
        pl.semaphore_wait(barrier, 4)

    @pl.when(inner)
    def _():
        pl.semaphore_wait(barrier, 5)

    def note_copy():
        return remote(note.at[0], note.at[1], note_send, note_recv, at_col(1 + z // 3))

    @pl.when(outer)
    def _():
        note_copy().start()

    def line(stream, t):
        at = span(t, PIECE)
        if stream == 0:
            src, dst, device = own.at[at], held.at[2, at], at_col(1 + z // 3)
        elif stream == 1:
            src, dst, device = own.at[at], held.at[0, at], at_col(3 - z)
        elif stream == 2:
            src, dst, device = held.at[2, at], held.at[1, at], at_col(3 - z)
        else:
            src = staged.at[stream - 3, span(t % RING, PIECE)]
            dst, device = held.at[stream - 3, at], at_col(((z - 1) * 3) % 4)
        return remote(src, dst, line_send.at[stream, t], line_recv.at[stream, t], device)

    def to_inner(first, last):
        @pl.when(outer)
        def _():
            def go(t, carry):
                line(0, t).start()
                return carry

            lax.fori_loop(first, last, go, 0)

    def forward(t):
        line(0, t).wait_recv()
        line(2, t).start()

    def chunk(t):
        @pl.when(inner)
        def _():
            @pl.when(t + AHEAD < chunks)
            def _():
                line(1, t + AHEAD).start()
                forward(t + AHEAD)

            line(1, t).wait_recv()
            line(2, t).wait_recv()
            at = span(t, PIECE)
            for m in range(nodes):
                pick = note[1, m : m + 1, :]

                @pl.when(t >= RING)
                def _():
                    line(3 + m, t - RING).wait_send()

                staged[m, span(t % RING, PIECE), :] = jnp.where(
                    pick < 2, own[at, :], jnp.where(pick == 2, held[0, at, :], held[1, at, :])
                )
                line(3 + m, t).start()

        @pl.when(outer)
        def _():
            line(3, t).wait_recv()
            line(4, t).wait_recv()

    def j_copy(k):
        mine = span(r, node)
        theirs = span(over, node)
        if k == 2:
            return remote(full_j.at[theirs], full_j.at[theirs], j_send.at[2], j_recv.at[2], at_row(twin))
        return remote(near_j, full_j.at[mine], j_send.at[k], j_recv.at[k], at_row(over if k == 0 else twin))

    def g_copy(k):
        if k == 4:
            at = pl.ds(0, rows)
            columns = span(1 - core, half)
            return remote(own.at[at, columns], beside, g_send.at[4], g_recv.at[4], at_row(twin))
        top = pl.ds(k // 2 * (rows // 2), rows // 2)
        at = pl.ds(pl.multiple_of(core * rows + k // 2 * (rows // 2), rows // 2), rows // 2)
        if k % 2 == 0:
            columns = span(1 - side, half)
            return remote(own.at[top, columns], across.at[at], g_send.at[k], g_recv.at[k], at_row(over))
        return remote(across.at[at], across.at[at], g_send.at[k], g_recv.at[k], at_row(twin))

    spans = [(k * STEP, STEP) for k in range(steps - 1)]
    spans += [((steps - 1) * STEP, STEP // 2), ((steps - 1) * STEP + STEP // 2, STEP // 2)]

    def r_copy(k, part):
        first, size = spans[part]
        who = over if k == 2 else r
        at = pl.ds(pl.multiple_of(who * rows + first, size), size)
        return remote(
            reduced.at[at],
            reduced.at[at],
            r_send.at[k, part],
            r_recv.at[k, part],
            at_row(over if k == 0 else twin),
        )

    def pick_rows(m, at):
        pick = picks[m]
        first = jnp.where(pick == 0, own[at, :], held[0, at, :])
        second = jnp.where(pick == 2, held[1, at, :], held[2, at, :])
        return jnp.where(pick < 2, first, second)

    def reduce_part(part, m):
        first, size = spans[part]
        at = pl.ds(first, size)
        to = pl.ds(pl.multiple_of(r * rows + first, size), size)
        block = pick_rows(m, at)
        chosen[m, at, :] = block
        reduced[to, child(m)] = near_r[at, child(m)] - mm(block, full_j[:, child(m)])
        if m == nodes - 1:
            r_copy(0, part).start()
            r_copy(1, part).start()

    def gather_part(part):
        r_copy(0, part).wait_recv()
        r_copy(2, part).start()

    def root_wait(part):
        r_copy(1, part).wait_recv()
        r_copy(2, part).wait_recv()

    def root_step(step, m):
        places = [pl.ds(pl.multiple_of(d * rows + step * STEP, STEP), STEP) for d in range(4)]
        left = jnp.concatenate([root[:, at] for at in places], 1)
        right = jnp.concatenate([reduced[at, child(m)] for at in places], 0)
        z_r[m] -= mm(left, right)

    def to_tile(vec):
        return jnp.concatenate([vec[:, i * 128 : (i + 1) * 128] for i in range(vec.shape[1] // 128)], 0)

    def shared(pieces):
        total = jnp.zeros_like(pieces[0])
        for d, one in enumerate(pieces):
            total = total + jnp.where(r == d, one, 0.0)
        return total

    def to_peers(tile, send, recv):
        return [
            remote(tile.at[0], tile.at[1 + k], send.at[k], recv.at[k], at_row(peer))
            for k, peer in enumerate((twin, over, diag))
        ]

    def colsum(left, right):
        return jnp.sum(left * right, axis=0, keepdims=True)

    def factor(first, size):
        at = pl.ds(first, size)
        own[at, :] = mm(own[at, 0:half], chosen[0]) + mm(own[at, half:width], chosen[1])

    def masked(panel, tiles, at, m, first, count):
        column = lax.broadcasted_iota(jnp.int32, (1, two), 1)
        live = (column < widths[m]).astype(jnp.float32)
        blocks = [
            panel[pl.ds(at + i * TILE, TILE), child(m)] * (live * tiles[m, first + i].astype(jnp.float32))
            for i in range(count)
        ]
        return jnp.concatenate(blocks, 0)

    for k in range(3):
        load(k).wait()
    for k in range(3, 9):
        load(k).start()
    factor(0, STEP)
    to_inner(0, per)
    early = 2

    @pl.when(inner)
    def _():
        for t in range(early):
            line(1, t).start()

    for k in range(3, 6):
        load(k).wait()
    for m in range(nodes):
        near_j[:, child(m)] = mm(masked(near_j, tiles_j, 0, m, 0, node // TILE), part_in[m])
    for k in (0, 1):
        j_copy(k).start()

    def pass_on(first, last):
        @pl.when(inner)
        def _():
            for t in range(first, last):
                forward(t)
                if t + early < AHEAD:
                    line(1, t + early).start()

    share = AHEAD // steps
    pass_on(0, share)
    for k in range(1, steps):
        factor(k * STEP, STEP)
        to_inner(k * per, (k + 1) * per)
        pass_on(k * share, (k + 1) * share)
    g_copy(4).start()

    @pl.when(inner)
    def _():
        note_copy().wait_recv()

    full_j[span(r, node), :] = near_j[...]
    for m in range(nodes):
        z_r[m] = jnp.zeros_like(z_r[m])

    def separator_rows(m):
        load(6 + m).wait()
        near_r[:, child(m)] = mm(masked(near_r, tiles_r, 0, m, 0, rows // TILE), part_in[m])

    def gram(k):
        columns = pl.ds(pl.multiple_of(r * node + k * STEP, STEP), STEP)
        own[rows + k * STEP : rows + (k + 1) * STEP, :] = mm_t(chosen[0, :, columns], chosen[0]) + mm_t(
            chosen[1, :, columns], chosen[1]
        )
        to_inner((steps + k) * per, (steps + k + 1) * per)

    one = {}

    def square_sums():
        one["squares"] = sum(
            colsum(chosen[h, :, span(r, node)], chosen[h, :, span(r, node)]) for h in range(2)
        )
        one["squares_two"] = [colsum(part_in[m], part_in[m]) for m in range(nodes)]

    def gathered_j():
        j_copy(0).wait_recv()
        j_copy(2).start()
        j_copy(1).wait_recv()
        j_copy(2).wait_recv()

    def diagonal(h):
        block = own[0:rows, h * half : (h + 1) * half]
        one[h] = colsum(block, mm(root[:, span(r, rows)], block))

    def pair():
        g_copy(4).wait_recv()
        product_two = mm(root[:, span(twin, rows)], beside[...])
        one["pair"] = 2.0 * colsum(own[0:rows, span(core, half)], product_two)

    def cross():
        g_copy(1).wait_recv()
        g_copy(3).wait_recv()
        product_two = mm(root[:, span(1 - side, 2 * rows)], across[...])
        product_two = 2.0 * colsum(own[0:rows, span(side, half)], product_two)
        sums = [
            one[h] + jnp.where(core == h, one["pair"], 0.0) + jnp.where(side == h, product_two, 0.0)
            for h in range(2)
        ]
        vec_a[0] = to_tile(jnp.concatenate(sums, 1))
        for copy in to_peers(vec_a, a_send, a_recv):
            copy.start()

    def level_one_out():
        for copy in to_peers(vec_a, a_send, a_recv):
            copy.wait()
        total = vec_a[0] + vec_a[1] + vec_a[2] + vec_a[3]
        each = total.shape[0] // 4
        mine = shared([total[d * each : (d + 1) * each, :] for d in range(4)])
        var_one[0:1, :] = one["squares"]
        var_one[1:2, :] = jnp.concatenate([mine[i : i + 1, :] for i in range(each)], 1)

    def pass_g(k):
        g_copy(k).wait_recv()
        g_copy(k + 1).start()

    def node_step(step, m):
        at = pl.ds(rows + step * STEP, STEP)
        z_j[m, step * STEP : (step + 1) * STEP, :] = mm(pick_rows(m, at), full_j[:, child(m)])

    def upper(m, dest):
        return mm_t(chosen[m, :, span(dest, node)], z_r[m])

    def u_copy(k):
        if k < 2:
            out = part_out.at[pl.ds(k * 2 * node, 2 * node)]
            return remote(out, part_in.at[k], u_send.at[k], u_recv.at[k], at_row(twin))
        out = part_own.at[pl.ds((k - 2) * node, node)]
        return remote(out, part_y.at[k - 2], u_send.at[k], u_recv.at[k], at_row(over))

    def upper_twin(m):
        part_out[m * 2 * node : m * 2 * node + node, :] = upper(m, diag)
        part_out[m * 2 * node + node : (m + 1) * 2 * node, :] = upper(m, twin)
        u_copy(m).start()

    def upper_over(m):
        far = upper(m, over)
        u_copy(m).wait_recv()
        part_own[m * node : (m + 1) * node, :] = far + part_in[m, 0:node, :]
        u_copy(2 + m).start()

    def upper_own(m):
        part_in[m, node : 2 * node, :] = part_in[m, node : 2 * node, :] + upper(m, r)

    def separator_sums():
        one["sums_r"] = [colsum(near_r[:, child(m)], z_r[m]) for m in range(nodes)]

    def item(function, *arguments):
        return functools.partial(function, *arguments)

    work = {
        0: [item(separator_rows, 0)],
        1: [item(separator_rows, 1)],
        2: [item(gram, 0)],
        4: [item(gram, 1)],
        5: [square_sums],
        7: [gathered_j, item(reduce_part, 0, 0)],
        8: [item(reduce_part, 0, 1)],
        9: [load(8).wait, item(diagonal, 0)],
        11: [item(diagonal, 1)],
        14: [item(gather_part, 0), g_copy(0).start],
        15: [item(reduce_part, 1, 0)],
        16: [item(reduce_part, 1, 1)],
        17: [item(root_wait, 0), item(root_step, 0, 0)],
        18: [item(root_step, 0, 1)],
        19: [pair],
        22: [item(pass_g, 0), item(gather_part, 1), g_copy(2).start],
        23: [item(reduce_part, 2, 0)],
        24: [item(reduce_part, 2, 1)],
        25: [item(root_wait, 1), item(root_step, 1, 0)],
        26: [item(root_step, 1, 1)],
        27: [item(reduce_part, 3, 0)],
        28: [item(reduce_part, 3, 1)],
        29: [item(pass_g, 2)],
        30: [item(gather_part, 2)],
        31: [item(reduce_part, 4, 0), item(reduce_part, 4, 1)],
        32: [item(root_wait, 2), item(root_step, 2, 0)],
        33: [item(root_step, 2, 1), item(gather_part, 3)],
        35: [item(gather_part, 4), item(root_wait, 3), item(root_wait, 4), item(root_step, 3, 0)],
        36: [item(upper_twin, 0)],
        37: [item(upper_over, 0), item(root_step, 3, 1)],
        38: [item(upper_twin, 1)],
        39: [item(upper_over, 1)],
        40: [cross],
        41: [item(node_step, 0, 0)],
        42: [item(node_step, 0, 1)],
        43: [item(upper_own, 0)],
        44: [item(upper_own, 1)],
        45: [level_one_out],
        46: [separator_sums],
    }
    done = 0
    for last in sorted(work) + [chunks - 1]:
        if last == done:
            chunk(last)
        else:

            def go(t, carry):
                chunk(t)
                return carry

            lax.fori_loop(done, last + 1, go, 0)
        done = last + 1
        for function in work.get(last, ()):
            function()

    sums_r = one["sums_r"]
    for m in range(nodes):
        node_step(1, m)
    for m in range(nodes):
        u_copy(2 + m).wait_recv()
        z_j[m] = -(z_j[m] + part_in[m, node : 2 * node, :] + part_y[m])
        sums_r[m] = sums_r[m] + colsum(near_j[:, child(m)], z_j[m])
    vec_b[0] = to_tile(jnp.concatenate(sums_r, 1))
    for copy in to_peers(vec_b, b_send, b_recv):
        copy.start()

    @pl.when(outer)
    def _():
        note_copy().wait_send()

        def go(t, carry):
            line(0, t).wait_send()
            return carry

        lax.fori_loop(0, chunks, go, 0)

    @pl.when(inner)
    def _():
        def go(t, carry):
            line(1, t).wait_send()
            line(2, t).wait_send()
            return carry

        lax.fori_loop(0, chunks, go, 0)

        def last(t, carry):
            line(3, t).wait_send()
            line(4, t).wait_send()
            return carry

        lax.fori_loop(chunks - RING, chunks, last, 0)

    for k in range(3):
        j_copy(k).wait_send()
    for k in range(5):
        g_copy(k).wait_send()
    for part in range(len(spans)):
        for k in range(3):
            r_copy(k, part).wait_send()
    for k in range(4):
        u_copy(k).wait_send()
    for copy in to_peers(vec_b, b_send, b_recv):
        copy.wait()
    total = vec_b[0] + vec_b[1] + vec_b[2] + vec_b[3]
    share = two // 4
    for m in range(nodes):
        mine = shared([total[m * 4 + d : m * 4 + d + 1, :] for d in range(4)])
        square = shared([one["squares_two"][m][:, d * share : (d + 1) * share] for d in range(4)])
        var_two[m : m + 1, :] = square - mine


def line_body(
    zroot,
    panel_one,
    inv_one,
    panel_two_j,
    panel_two_r,
    inv_two,
    parents,
    widths,
    pattern_j,
    pattern_r,
):
    n = lax.axis_size("row")
    width = inv_one.shape[1]
    node = width // n
    nodes, two = inv_two.shape[:2]
    rows = zroot.shape[0]
    chunks = (rows + node) // PIECE
    steps = rows // STEP
    f32 = jnp.float32
    smem = pl.BlockSpec(memory_space=pltpu.SMEM)
    hbm = pl.BlockSpec(memory_space=pl.ANY)
    vmem = pl.BlockSpec(memory_space=pltpu.VMEM)
    dma = pltpu.SemaphoreType.DMA
    var_one, var_two, z_j, z_r = pl.pallas_call(
        line_kernel,
        out_shape=(
            jax.ShapeDtypeStruct((2, node), f32),
            jax.ShapeDtypeStruct((nodes, two // n), f32),
            jax.ShapeDtypeStruct((nodes, node, two), f32),
            jax.ShapeDtypeStruct((nodes, rows, two), f32),
        ),
        in_specs=[smem] * 4 + [hbm] * 6,
        out_specs=(vmem,) * 4,
        scratch_shapes=[
            pltpu.VMEM(zroot.shape, f32),
            pltpu.VMEM((rows + node, width), f32),
            pltpu.VMEM((node, nodes * two), f32),
            pltpu.VMEM((rows, nodes * two), f32),
            pltpu.VMEM((nodes * 2 * node, two), f32),
            pltpu.VMEM((nodes * node, two), f32),
            pltpu.VMEM((3, rows + node, width), f32),
            pltpu.VMEM((nodes, RING * PIECE, width), f32),
            pltpu.VMEM((width, nodes * two), f32),
            pltpu.VMEM((nodes, rows, width), f32),
            pltpu.VMEM((4 * rows, nodes * two), f32),
            pltpu.VMEM((2 * rows, width // 2), f32),
            pltpu.VMEM((rows, width // 2), f32),
            pltpu.VMEM((nodes, 2 * node, two), f32),
            pltpu.VMEM((nodes, node, two), f32),
            pltpu.VMEM((2, 8, width), jnp.int32),
            pltpu.VMEM((4, width // 128, 128), f32),
            pltpu.VMEM((4, nodes * two // 128, 128), f32),
            dma((9,)),
            dma,
            dma,
            dma((5, chunks)),
            dma((5, chunks)),
            dma((3,)),
            dma((3,)),
            dma((5,)),
            dma((5,)),
            dma((3, steps + 1)),
            dma((3, steps + 1)),
            dma((4,)),
            dma((4,)),
            dma((3,)),
            dma((3,)),
            dma((3,)),
            dma((3,)),
        ],
        compiler_params=pltpu.CompilerParams(
            collective_id=0, has_side_effects=True, vmem_limit_bytes=60 * 1024 * 1024
        ),
    )(parents, widths, pattern_j, pattern_r, zroot, panel_one, inv_one, panel_two_j, panel_two_r, inv_two)
    first = lax.axis_index("row") * (two // n)
    live = (first + jnp.arange(two // n)[None, :] < widths[:, None]).astype(jnp.float32)
    return (var_one[0:1] + var_one[1:2], live * var_two, z_j, z_r)


def solution(mesh):
    fits = mesh.shape["row"] == 4 and mesh.shape["col"] == 4
    return jax.shard_map(
        line_body if fits else general_body,
        mesh=mesh,
        in_specs=(
            P(("groups", "row"), None),
            P(("groups", "col"), "row", None),
            P(("groups", "col"), None, None),
            P(("groups", "col"), "row", None),
            P(("groups", "col"), "row", None),
            P(("groups", "col"), None, None),
            P(("groups", "col")),
            P(("groups", "col")),
            P(("groups", "col"), "row"),
            P(("groups", "col"), "row"),
        ),
        out_specs=(
            P(("groups", "col"), "row"),
            P(("groups", "col"), "row"),
            P(("groups", "col"), "row", None),
            P(("groups", "col"), "row", None),
        ),
        check_vma=False,
    )
```

```python
import functools

import jax
import jax.numpy as jnp
from jax import lax
from jax.experimental import pallas as pl
from jax.experimental.pallas import tpu as pltpu
from jax.sharding import PartitionSpec as P

TILE = 64
PRECISION = lax.Precision.HIGH


def product(left, right):
    return jnp.dot(left, right, precision=PRECISION, preferred_element_type=jnp.float32)


def crossed(left, right):
    return lax.dot_general(
        left, right, (((0,), (0,)), ((), ())), precision=PRECISION, preferred_element_type=jnp.float32
    )


def swap(block, bit):
    n = lax.axis_size("row")
    return lax.ppermute(block, "row", [(i, i ^ bit) for i in range(n)])


def own_first(array, axis):
    n = lax.axis_size("row")
    me = lax.axis_index("row")
    share = array.shape[axis] // n
    pieces = [
        lax.dynamic_slice_in_dim(array, (me ^ d) * share, share, axis) for d in range(n)
    ]
    return jnp.concatenate(pieces, axis)


def row_blocks(block):
    n = lax.axis_size("row")
    held = {0: block}
    bit = n // 2
    while bit:
        for d in sorted(held):
            held[d | bit] = swap(held[d], bit)
        bit //= 2
    return [held[d] for d in range(n)]


def row_sum(pieces):
    n = lax.axis_size("row")
    held = dict(enumerate(pieces))
    bit = 1
    while bit < n:
        for d in [d for d in sorted(held) if not d & bit]:
            held[d] = held[d] + swap(held.pop(d | bit), bit)
        bit *= 2
    return held[0]


def reordered(block, d):
    n = lax.axis_size("row")
    share = block.shape[1] // n
    return jnp.concatenate(
        [block[:, (d ^ e) * share : ((d ^ e) + 1) * share] for e in range(n)], 1
    )


def general_body(
    zroot,
    panel_one,
    inv_one,
    panel_two_j,
    panel_two_r,
    inv_two,
    parents,
    widths,
    pattern_j,
    pattern_r,
):
    n = lax.axis_size("row")
    width_one = inv_one.shape[1]
    node_rows = width_one // n
    nodes, width_two = inv_two.shape[:2]
    root_rows = zroot.shape[0]

    inverse = own_first(inv_one[0], 1)
    factor = product(panel_one[0], inverse)
    all_factors = lax.all_gather(factor, "col", axis=0)
    gram = crossed(inverse[:, :node_rows], inverse)
    factor_tied, gram = lax.optimization_barrier((factor, gram))
    all_grams = lax.all_gather(gram, "col", axis=0)

    live = (jnp.arange(width_two)[None, :] < widths[:, None]).astype(jnp.float32)
    mask_j = jnp.repeat(pattern_j.astype(jnp.float32), TILE, axis=1)
    mask_r = jnp.repeat(pattern_r.astype(jnp.float32), TILE, axis=1)
    factor_j = []
    factor_r = []
    for i in range(nodes):
        masked_j = panel_two_j[i] * mask_j[i][:, None] * live[i][None, :]
        masked_r = panel_two_r[i] * mask_r[i][:, None] * live[i][None, :]
        factor_j.append(product(masked_j, inv_two[i]))
        factor_r.append(product(masked_r, inv_two[i]))
    near_j = jnp.concatenate(factor_j, 1)
    full_j = jnp.concatenate(row_blocks(near_j), 0)

    root = own_first(zroot, 1)
    full_factor = jnp.concatenate(
        [reordered(block, d) for d, block in enumerate(row_blocks(factor))], 0
    )
    image = product(root, full_factor)
    terms = jnp.sum(factor * image, axis=0).reshape(n, node_rows)
    own_squares = jnp.sum(inverse[:, :node_rows] ** 2, axis=0)
    var_one = (own_squares + row_sum([terms[d] for d in range(n)]))[None, :]

    all_factors, var_one = lax.optimization_barrier((all_factors, var_one))

    parent_factor = [
        lax.dynamic_index_in_dim(all_factors, parents[i], 0, False) for i in range(nodes)
    ]
    reduced = [
        factor_r[i] - product(parent_factor[i], full_j[:, i * width_two : (i + 1) * width_two])
        for i in range(nodes)
    ]
    block_r = []
    sums_j = []
    for i in range(nodes):
        block_r.append(-product(root, jnp.concatenate(row_blocks(reduced[i]), 0)))
        upper = crossed(parent_factor[i], block_r[i]).reshape(n, node_rows, width_two)
        sums_j.append(row_sum([upper[d] for d in range(n)]))
    block_j = []
    for i in range(nodes):
        parent_gram = lax.dynamic_index_in_dim(all_grams, parents[i], 0, False)
        near = product(parent_gram, full_j[:, i * width_two : (i + 1) * width_two])
        block_j.append(-(near + sums_j[i]))

    corrections = jnp.stack(
        [
            jnp.sum(factor_j[i] * block_j[i], axis=0) + jnp.sum(factor_r[i] * block_r[i], axis=0)
            for i in range(nodes)
        ]
    )
    share = width_two // n
    me = lax.axis_index("row")
    ordered = own_first(corrections, 1).reshape(nodes, n, share)
    summed = row_sum([ordered[:, d] for d in range(n)])
    squares = jnp.sum(inv_two * inv_two, axis=1)
    live_share = lax.dynamic_slice_in_dim(live, me * share, share, 1)
    square_share = lax.dynamic_slice_in_dim(squares, me * share, share, 1)
    var_two = live_share * (square_share - summed)
    return (var_one, var_two, jnp.stack(block_j), jnp.stack(block_r))


PIECE = 16
RING = 16
AHEAD = 8
STEP = 128


def mm(left, right):
    return jnp.dot(left, right, precision=PRECISION, preferred_element_type=jnp.float32)


def mm_t(left, right):
    return lax.dot_general(
        left, right, (((0,), (0,)), ((), ())), precision=PRECISION, preferred_element_type=jnp.float32
    )


def line_kernel(
    parents,
    widths,
    tiles_j,
    tiles_r,
    zroot,
    panel_one,
    inv_one,
    panel_j,
    panel_r,
    inv_two,
    var_one,
    var_two,
    z_j,
    z_r,
    root,
    own,
    near_j,
    near_r,
    part_out,
    part_own,
    held,
    staged,
    full_j,
    chosen,
    reduced,
    across,
    beside,
    part_in,
    part_y,
    note,
    vec_a,
    vec_b,
    loads,
    note_send,
    note_recv,
    line_send,
    line_recv,
    j_send,
    j_recv,
    g_send,
    g_recv,
    r_send,
    r_recv,
    u_send,
    u_recv,
    a_send,
    a_recv,
    b_send,
    b_recv,
):
    rows = root.shape[0]
    width = own.shape[1]
    node = near_j.shape[0]
    nodes, _, two = z_r.shape
    chunks = own.shape[0] // PIECE
    steps = rows // STEP
    per = STEP // PIECE
    half = width // 2

    z = lax.axis_index("col")
    r = lax.axis_index("row")
    core = r % 2
    side = r // 2
    twin = r + 1 - 2 * core
    over = (r + 2) % 4
    diag = (twin + 2) % 4
    inner = jnp.logical_or(z == 1, z == 2)
    outer = jnp.logical_not(inner)

    def remote(src, dst, send, recv, device):
        return pltpu.make_async_remote_copy(
            src_ref=src,
            dst_ref=dst,
            send_sem=send,
            recv_sem=recv,
            device_id=device,
            device_id_type=pl.DeviceIdType.MESH,
        )

    def at_row(index):
        return (lax.axis_index("groups"), index, z)

    def at_col(index):
        return (lax.axis_index("groups"), r, index)

    def span(index, size):
        return pl.ds(pl.multiple_of(index * size, size), size)

    def child(m):
        return pl.ds(m * two, two)

    def load(k):
        if k == 0:
            return pltpu.make_async_copy(panel_one.at[0], own.at[pl.ds(0, rows)], loads.at[0])
        if k < 3:
            h = k - 1
            return pltpu.make_async_copy(inv_one.at[0, pl.ds(h * half, half)], chosen.at[h], loads.at[k])
        if k < 5:
            m = k - 3
            return pltpu.make_async_copy(panel_j.at[m], near_j.at[:, child(m)], loads.at[k])
        if k == 5:
            return pltpu.make_async_copy(inv_two, part_in, loads.at[5])
        if k < 8:
            m = k - 6
            return pltpu.make_async_copy(panel_r.at[m], near_r.at[:, child(m)], loads.at[k])
        return pltpu.make_async_copy(zroot, root, loads.at[8])

    for k in range(3):
        load(k).start()

    barrier = pltpu.get_barrier_semaphore()

    def greet(device):
        pl.semaphore_signal(barrier, inc=1, device_id=device, device_id_type=pl.DeviceIdType.MESH)

    for peer in (twin, over, diag):
        greet(at_row(peer))

    @pl.when(outer)
    def _():
        greet(at_col(1 + z // 3))

    @pl.when(inner)
    def _():
        greet(at_col(3 - z))
        greet(at_col(((z - 1) * 3) % 4))

    low = z < 2
    place = jnp.where(low, z, 3 - z)
    kin = [jnp.where(low, parents[m], 3 - parents[m]) for m in range(nodes)]
    picks = [
        jnp.where(place == 1, (kin[m] + 3) % 4, jnp.where(kin[m] == 0, 0, 1 + m)) for m in range(nodes)
    ]
    note[0] = jnp.zeros(note.shape[1:], jnp.int32)
    for m in range(nodes):
        note[0, m : m + 1, :] = jnp.full((1, width), kin[m], jnp.int32)

    @pl.when(outer)
    def _():
        pl.semaphore_wait(barrier, 4)

    @pl.when(inner)
    def _():
        pl.semaphore_wait(barrier, 5)

    def note_copy():
        return remote(note.at[0], note.at[1], note_send, note_recv, at_col(1 + z // 3))

    @pl.when(outer)
    def _():
        note_copy().start()

    def line(stream, t):
        at = span(t, PIECE)
        if stream == 0:
            src, dst, device = own.at[at], held.at[2, at], at_col(1 + z // 3)
        elif stream == 1:
            src, dst, device = own.at[at], held.at[0, at], at_col(3 - z)
        elif stream == 2:
            src, dst, device = held.at[2, at], held.at[1, at], at_col(3 - z)
        else:
            src = staged.at[stream - 3, span(t % RING, PIECE)]
            dst, device = held.at[stream - 3, at], at_col(((z - 1) * 3) % 4)
        return remote(src, dst, line_send.at[stream, t], line_recv.at[stream, t], device)

    def to_inner(first, last):
        @pl.when(outer)
        def _():
            def go(t, carry):
                line(0, t).start()
                return carry

            lax.fori_loop(first, last, go, 0)

    def forward(t):
        line(0, t).wait_recv()
        line(2, t).start()

    def chunk(t):
        @pl.when(inner)
        def _():
            @pl.when(t + AHEAD < chunks)
            def _():
                line(1, t + AHEAD).start()
                forward(t + AHEAD)

            line(1, t).wait_recv()
            line(2, t).wait_recv()
            at = span(t, PIECE)
            for m in range(nodes):
                pick = note[1, m : m + 1, :]

                @pl.when(t >= RING)
                def _():
                    line(3 + m, t - RING).wait_send()

                staged[m, span(t % RING, PIECE), :] = jnp.where(
                    pick < 2, own[at, :], jnp.where(pick == 2, held[0, at, :], held[1, at, :])
                )
                line(3 + m, t).start()

        @pl.when(outer)
        def _():
            line(3, t).wait_recv()
            line(4, t).wait_recv()

    def j_copy(k):
        mine = span(r, node)
        theirs = span(over, node)
        if k == 2:
            return remote(full_j.at[theirs], full_j.at[theirs], j_send.at[2], j_recv.at[2], at_row(twin))
        return remote(near_j, full_j.at[mine], j_send.at[k], j_recv.at[k], at_row(over if k == 0 else twin))

    def g_copy(k):
        if k == 4:
            at = pl.ds(0, rows)
            columns = span(1 - core, half)
            return remote(own.at[at, columns], beside, g_send.at[4], g_recv.at[4], at_row(twin))
        top = pl.ds(k // 2 * (rows // 2), rows // 2)
        at = pl.ds(pl.multiple_of(core * rows + k // 2 * (rows // 2), rows // 2), rows // 2)
        if k % 2 == 0:
            columns = span(1 - side, half)
            return remote(own.at[top, columns], across.at[at], g_send.at[k], g_recv.at[k], at_row(over))
        return remote(across.at[at], across.at[at], g_send.at[k], g_recv.at[k], at_row(twin))

    spans = [(k * STEP, STEP) for k in range(steps - 1)]
    spans += [((steps - 1) * STEP, STEP // 2), ((steps - 1) * STEP + STEP // 2, STEP // 2)]

    def r_copy(k, part):
        first, size = spans[part]
        who = over if k == 2 else r
        at = pl.ds(pl.multiple_of(who * rows + first, size), size)
        return remote(
            reduced.at[at],
            reduced.at[at],
            r_send.at[k, part],
            r_recv.at[k, part],
            at_row(over if k == 0 else twin),
        )

    def twice(function):
        def go(h, carry):
            function(h)
            return carry

        lax.fori_loop(0, 2, go, 0)

    part_two = two // 2

    def within(m, h):
        return pl.ds(pl.multiple_of(m * two + h * part_two, part_two), part_two)

    def pick_rows(m, at):
        pick = picks[m]
        first = jnp.where(pick == 0, own[at, :], held[0, at, :])
        second = jnp.where(pick == 2, held[1, at, :], held[2, at, :])
        return jnp.where(pick < 2, first, second)

    def reduce_part(part, m):
        first, size = spans[part]
        at = pl.ds(first, size)
        to = pl.ds(pl.multiple_of(r * rows + first, size), size)
        chosen[m, at, :] = pick_rows(m, at)

        def go(h):
            columns = within(m, h)
            reduced[to, columns] = near_r[at, columns] - mm(chosen[m, at, :], full_j[:, columns])

        twice(go)
        if m == nodes - 1:
            r_copy(0, part).start()
            r_copy(1, part).start()

    def gather_part(part):
        r_copy(0, part).wait_recv()
        r_copy(2, part).start()

    def root_wait(part):
        r_copy(1, part).wait_recv()
        r_copy(2, part).wait_recv()

    def root_step(step, m):
        places = [pl.ds(pl.multiple_of(d * rows + step * STEP, STEP), STEP) for d in range(4)]

        def go(h):
            columns = within(0, h)
            left = jnp.concatenate([root[:, at] for at in places], 1)
            right = jnp.concatenate([reduced[at, within(m, h)] for at in places], 0)
            z_r[m, :, columns] -= mm(left, right)

        twice(go)

    def to_tile(vec):
        return jnp.concatenate([vec[:, i * 128 : (i + 1) * 128] for i in range(vec.shape[1] // 128)], 0)

    def shared(pieces):
        total = jnp.zeros_like(pieces[0])
        for d, one in enumerate(pieces):
            total = total + jnp.where(r == d, one, 0.0)
        return total

    def to_peers(tile, send, recv):
        return [
            remote(tile.at[0], tile.at[1 + k], send.at[k], recv.at[k], at_row(peer))
            for k, peer in enumerate((twin, over, diag))
        ]

    def colsum(left, right):
        return jnp.sum(left * right, axis=0, keepdims=True)

    def factor(first, size):
        at = pl.ds(first, size)
        own[at, :] = mm(own[at, 0:half], chosen[0]) + mm(own[at, half:width], chosen[1])

    def masked(panel, tiles, at, m, first, count):
        column = lax.broadcasted_iota(jnp.int32, (1, two), 1)
        live = (column < widths[m]).astype(jnp.float32)
        blocks = [
            panel[pl.ds(at + i * TILE, TILE), child(m)] * (live * tiles[m, first + i].astype(jnp.float32))
            for i in range(count)
        ]
        return jnp.concatenate(blocks, 0)

    for k in range(3):
        load(k).wait()
    for k in range(3, 9):
        load(k).start()
    factor(0, STEP)
    to_inner(0, per)
    early = 2

    @pl.when(inner)
    def _():
        for t in range(early):
            line(1, t).start()

    for k in range(3, 6):
        load(k).wait()
    for m in range(nodes):
        near_j[:, child(m)] = mm(masked(near_j, tiles_j, 0, m, 0, node // TILE), part_in[m])
    for k in (0, 1):
        j_copy(k).start()

    def pass_on(first, last):
        @pl.when(inner)
        def _():
            for t in range(first, last):
                forward(t)
                if t + early < AHEAD:
                    line(1, t + early).start()

    share = AHEAD // steps
    pass_on(0, share)
    for k in range(1, steps):
        factor(k * STEP, STEP)
        to_inner(k * per, (k + 1) * per)
        pass_on(k * share, (k + 1) * share)
    g_copy(4).start()

    @pl.when(inner)
    def _():
        note_copy().wait_recv()

    full_j[span(r, node), :] = near_j[...]
    for m in range(nodes):
        z_r[m] = jnp.zeros_like(z_r[m])

    def separator_rows(m):
        load(6 + m).wait()

        def go(h):
            size = rows // 2
            at = pl.multiple_of(h * size, size)
            count = size // TILE
            near_r[pl.ds(at, size), child(m)] = mm(masked(near_r, tiles_r, at, m, h * count, count), part_in[m])

        twice(go)

    def gram(k):
        columns = pl.ds(pl.multiple_of(r * node + k * STEP, STEP), STEP)
        own[rows + k * STEP : rows + (k + 1) * STEP, :] = mm_t(chosen[0, :, columns], chosen[0]) + mm_t(
            chosen[1, :, columns], chosen[1]
        )
        to_inner((steps + k) * per, (steps + k + 1) * per)

    one = {}

    def square_sums():
        one["squares"] = sum(
            colsum(chosen[h, :, span(r, node)], chosen[h, :, span(r, node)]) for h in range(2)
        )
        one["squares_two"] = [colsum(part_in[m], part_in[m]) for m in range(nodes)]

    def gathered_j():
        j_copy(0).wait_recv()
        j_copy(2).start()
        j_copy(1).wait_recv()
        j_copy(2).wait_recv()

    def diagonal(h):
        block = own[0:rows, h * half : (h + 1) * half]
        one[h] = colsum(block, mm(root[:, span(r, rows)], block))

    def pair():
        g_copy(4).wait_recv()
        product_two = mm(root[:, span(twin, rows)], beside[...])
        one["pair"] = 2.0 * colsum(own[0:rows, span(core, half)], product_two)

    def cross():
        g_copy(1).wait_recv()
        g_copy(3).wait_recv()
        product_two = mm(root[:, span(1 - side, 2 * rows)], across[...])
        product_two = 2.0 * colsum(own[0:rows, span(side, half)], product_two)
        sums = [
            one[h] + jnp.where(core == h, one["pair"], 0.0) + jnp.where(side == h, product_two, 0.0)
            for h in range(2)
        ]
        vec_a[0] = to_tile(jnp.concatenate(sums, 1))
        for copy in to_peers(vec_a, a_send, a_recv):
            copy.start()

    def level_one_out():
        for copy in to_peers(vec_a, a_send, a_recv):
            copy.wait()
        total = vec_a[0] + vec_a[1] + vec_a[2] + vec_a[3]
        each = total.shape[0] // 4
        mine = shared([total[d * each : (d + 1) * each, :] for d in range(4)])
        var_one[...] = one["squares"] + jnp.concatenate([mine[i : i + 1, :] for i in range(each)], 1)

    def pass_g(k):
        g_copy(k).wait_recv()
        g_copy(k + 1).start()

    def node_step(step, m):
        at = pl.ds(rows + step * STEP, STEP)
        block = pick_rows(m, at)

        def go(h):
            z_j[m, step * STEP : (step + 1) * STEP, within(0, h)] = mm(block, full_j[:, within(m, h)])

        twice(go)

    def upper(m, dest):
        return mm_t(chosen[m, :, span(dest, node)], z_r[m])

    def u_copy(k):
        if k < 2:
            out = part_out.at[pl.ds(k * 2 * node, 2 * node)]
            return remote(out, part_in.at[k], u_send.at[k], u_recv.at[k], at_row(twin))
        out = part_own.at[pl.ds((k - 2) * node, node)]
        return remote(out, part_y.at[k - 2], u_send.at[k], u_recv.at[k], at_row(over))

    def upper_twin(m):
        def go(h):
            at = pl.ds(pl.multiple_of((2 * m + h) * node, node), node)
            part_out[at, :] = upper(m, (twin + 2 - 2 * h) % 4)

        twice(go)
        u_copy(m).start()

    def upper_over(m):
        far = upper(m, over)
        u_copy(m).wait_recv()
        part_own[m * node : (m + 1) * node, :] = far + part_in[m, 0:node, :]
        u_copy(2 + m).start()

    def upper_own(m):
        part_in[m, node : 2 * node, :] = part_in[m, node : 2 * node, :] + upper(m, r)

    def separator_sums():
        one["sums_r"] = [colsum(near_r[:, child(m)], z_r[m]) for m in range(nodes)]

    def item(function, *arguments):
        return functools.partial(function, *arguments)

    work = {
        0: [item(separator_rows, 0)],
        1: [item(separator_rows, 1)],
        2: [item(gram, 0)],
        4: [item(gram, 1)],
        5: [square_sums],
        7: [gathered_j, item(reduce_part, 0, 0)],
        8: [item(reduce_part, 0, 1)],
        9: [load(8).wait, item(diagonal, 0)],
        11: [item(diagonal, 1)],
        14: [item(gather_part, 0), g_copy(0).start],
        15: [item(reduce_part, 1, 0)],
        16: [item(reduce_part, 1, 1)],
        17: [item(root_wait, 0), item(root_step, 0, 0)],
        18: [item(root_step, 0, 1)],
        19: [pair],
        22: [item(pass_g, 0), item(gather_part, 1), g_copy(2).start],
        23: [item(reduce_part, 2, 0)],
        24: [item(reduce_part, 2, 1)],
        25: [item(root_wait, 1), item(root_step, 1, 0)],
        26: [item(root_step, 1, 1)],
        27: [item(reduce_part, 3, 0)],
        28: [item(reduce_part, 3, 1)],
        29: [item(pass_g, 2)],
        30: [item(gather_part, 2)],
        31: [item(reduce_part, 4, 0), item(reduce_part, 4, 1)],
        32: [item(root_wait, 2), item(root_step, 2, 0)],
        33: [item(root_step, 2, 1), item(gather_part, 3)],
        35: [item(gather_part, 4), item(root_wait, 3), item(root_wait, 4), item(root_step, 3, 0)],
        36: [item(upper_twin, 0)],
        37: [item(upper_over, 0), item(root_step, 3, 1)],
        38: [item(upper_twin, 1)],
        39: [item(upper_over, 1)],
        40: [cross],
        41: [item(node_step, 0, 0)],
        42: [item(node_step, 0, 1)],
        43: [item(upper_own, 0)],
        44: [item(upper_own, 1)],
        45: [level_one_out],
        46: [separator_sums],
    }
    done = 0
    for last in sorted(work) + [chunks - 1]:
        if last == done:
            chunk(last)
        else:

            def go(t, carry):
                chunk(t)
                return carry

            lax.fori_loop(done, last + 1, go, 0)
        done = last + 1
        for function in work.get(last, ()):
            function()

    sums_r = one["sums_r"]
    for m in range(nodes):
        node_step(1, m)
    for m in range(nodes):
        u_copy(2 + m).wait_recv()
        z_j[m] = -(z_j[m] + part_in[m, node : 2 * node, :] + part_y[m])
        sums_r[m] = sums_r[m] + colsum(near_j[:, child(m)], z_j[m])
    vec_b[0] = to_tile(jnp.concatenate(sums_r, 1))
    for copy in to_peers(vec_b, b_send, b_recv):
        copy.start()

    @pl.when(outer)
    def _():
        note_copy().wait_send()

        def go(t, carry):
            line(0, t).wait_send()
            return carry

        lax.fori_loop(0, chunks, go, 0)

    @pl.when(inner)
    def _():
        def go(t, carry):
            line(1, t).wait_send()
            line(2, t).wait_send()
            return carry

        lax.fori_loop(0, chunks, go, 0)

        def last(t, carry):
            line(3, t).wait_send()
            line(4, t).wait_send()
            return carry

        lax.fori_loop(chunks - RING, chunks, last, 0)

    for k in range(3):
        j_copy(k).wait_send()
    for k in range(5):
        g_copy(k).wait_send()
    for part in range(len(spans)):
        for k in range(3):
            r_copy(k, part).wait_send()
    for k in range(4):
        u_copy(k).wait_send()
    for copy in to_peers(vec_b, b_send, b_recv):
        copy.wait()
    total = vec_b[0] + vec_b[1] + vec_b[2] + vec_b[3]
    share = two // 4
    column = lax.broadcasted_iota(jnp.int32, (1, share), 1) + r * share
    for m in range(nodes):
        mine = shared([total[m * 4 + d : m * 4 + d + 1, :] for d in range(4)])
        square = shared([one["squares_two"][m][:, d * share : (d + 1) * share] for d in range(4)])
        live = (column < widths[m]).astype(jnp.float32)
        var_two[m : m + 1, :] = live * (square - mine)


def copy_kernel(*refs):
    sems = refs[-1]
    order = (3, 2, 0, 1)
    ins = [pltpu.make_async_copy(refs[k], refs[8 + k], sems.at[k]) for k in order]
    outs = [pltpu.make_async_copy(refs[8 + k], refs[4 + k], sems.at[4 + k]) for k in order]
    for copy in ins:
        copy.start()
    for first, second in zip(ins, outs):
        first.wait()
        second.start()
    for copy in outs:
        copy.wait()


def line_body(
    zroot,
    panel_one,
    inv_one,
    panel_two_j,
    panel_two_r,
    inv_two,
    parents,
    widths,
    pattern_j,
    pattern_r,
):
    n = lax.axis_size("row")
    width = inv_one.shape[1]
    node = width // n
    nodes, two = inv_two.shape[:2]
    rows = zroot.shape[0]
    chunks = (rows + node) // PIECE
    steps = rows // STEP
    f32 = jnp.float32
    smem = pl.BlockSpec(memory_space=pltpu.SMEM)
    hbm = pl.BlockSpec(memory_space=pl.ANY)
    vmem = pl.BlockSpec(memory_space=pltpu.VMEM)
    dma = pltpu.SemaphoreType.DMA
    results = pl.pallas_call(
        line_kernel,
        out_shape=(
            jax.ShapeDtypeStruct((1, node), f32),
            jax.ShapeDtypeStruct((nodes, two // n), f32),
            jax.ShapeDtypeStruct((nodes, node, two), f32),
            jax.ShapeDtypeStruct((nodes, rows, two), f32),
        ),
        in_specs=[smem] * 4 + [hbm] * 6,
        out_specs=(vmem,) * 4,
        scratch_shapes=[
            pltpu.VMEM(zroot.shape, f32),
            pltpu.VMEM((rows + node, width), f32),
            pltpu.VMEM((node, nodes * two), f32),
            pltpu.VMEM((rows, nodes * two), f32),
            pltpu.VMEM((nodes * 2 * node, two), f32),
            pltpu.VMEM((nodes * node, two), f32),
            pltpu.VMEM((3, rows + node, width), f32),
            pltpu.VMEM((nodes, RING * PIECE, width), f32),
            pltpu.VMEM((width, nodes * two), f32),
            pltpu.VMEM((nodes, rows, width), f32),
            pltpu.VMEM((4 * rows, nodes * two), f32),
            pltpu.VMEM((2 * rows, width // 2), f32),
            pltpu.VMEM((rows, width // 2), f32),
            pltpu.VMEM((nodes, 2 * node, two), f32),
            pltpu.VMEM((nodes, node, two), f32),
            pltpu.VMEM((2, 8, width), jnp.int32),
            pltpu.VMEM((4, width // 128, 128), f32),
            pltpu.VMEM((4, nodes * two // 128, 128), f32),
            dma((9,)),
            dma,
            dma,
            dma((5, chunks)),
            dma((5, chunks)),
            dma((3,)),
            dma((3,)),
            dma((5,)),
            dma((5,)),
            dma((3, steps + 1)),
            dma((3, steps + 1)),
            dma((4,)),
            dma((4,)),
            dma((3,)),
            dma((3,)),
            dma((3,)),
            dma((3,)),
        ],
        compiler_params=pltpu.CompilerParams(
            collective_id=0, has_side_effects=True, vmem_limit_bytes=60 * 1024 * 1024
        ),
    )(parents, widths, pattern_j, pattern_r, zroot, panel_one, inv_one, panel_two_j, panel_two_r, inv_two)
    return pl.pallas_call(
        copy_kernel,
        out_shape=tuple(jax.ShapeDtypeStruct(one.shape, one.dtype) for one in results),
        in_specs=[hbm] * 4,
        out_specs=(hbm,) * 4,
        scratch_shapes=[pltpu.VMEM(one.shape, one.dtype) for one in results] + [dma((8,))],
        compiler_params=pltpu.CompilerParams(vmem_limit_bytes=60 * 1024 * 1024),
    )(*results)


def solution(mesh):
    fits = mesh.shape["row"] == 4 and mesh.shape["col"] == 4
    return jax.shard_map(
        line_body if fits else general_body,
        mesh=mesh,
        in_specs=(
            P(("groups", "row"), None),
            P(("groups", "col"), "row", None),
            P(("groups", "col"), None, None),
            P(("groups", "col"), "row", None),
            P(("groups", "col"), "row", None),
            P(("groups", "col"), None, None),
            P(("groups", "col")),
            P(("groups", "col")),
            P(("groups", "col"), "row"),
            P(("groups", "col"), "row"),
        ),
        out_specs=(
            P(("groups", "col"), "row"),
            P(("groups", "col"), "row"),
            P(("groups", "col"), "row", None),
            P(("groups", "col"), "row", None),
        ),
        check_vma=False,
    )
```

```python
import functools

import jax
import jax.numpy as jnp
from jax import lax
from jax.experimental import pallas as pl
from jax.experimental.pallas import tpu as pltpu
from jax.sharding import PartitionSpec as P

TILE = 64
PRECISION = lax.Precision.HIGH


def product(left, right):
    return jnp.dot(left, right, precision=PRECISION, preferred_element_type=jnp.float32)


def crossed(left, right):
    return lax.dot_general(
        left, right, (((0,), (0,)), ((), ())), precision=PRECISION, preferred_element_type=jnp.float32
    )


def swap(block, bit):
    n = lax.axis_size("row")
    return lax.ppermute(block, "row", [(i, i ^ bit) for i in range(n)])


def own_first(array, axis):
    n = lax.axis_size("row")
    me = lax.axis_index("row")
    share = array.shape[axis] // n
    pieces = [
        lax.dynamic_slice_in_dim(array, (me ^ d) * share, share, axis) for d in range(n)
    ]
    return jnp.concatenate(pieces, axis)


def row_blocks(block):
    n = lax.axis_size("row")
    held = {0: block}
    bit = n // 2
    while bit:
        for d in sorted(held):
            held[d | bit] = swap(held[d], bit)
        bit //= 2
    return [held[d] for d in range(n)]


def row_sum(pieces):
    n = lax.axis_size("row")
    held = dict(enumerate(pieces))
    bit = 1
    while bit < n:
        for d in [d for d in sorted(held) if not d & bit]:
            held[d] = held[d] + swap(held.pop(d | bit), bit)
        bit *= 2
    return held[0]


def reordered(block, d):
    n = lax.axis_size("row")
    share = block.shape[1] // n
    return jnp.concatenate(
        [block[:, (d ^ e) * share : ((d ^ e) + 1) * share] for e in range(n)], 1
    )


def general_body(
    zroot,
    panel_one,
    inv_one,
    panel_two_j,
    panel_two_r,
    inv_two,
    parents,
    widths,
    pattern_j,
    pattern_r,
):
    n = lax.axis_size("row")
    width_one = inv_one.shape[1]
    node_rows = width_one // n
    nodes, width_two = inv_two.shape[:2]
    root_rows = zroot.shape[0]

    inverse = own_first(inv_one[0], 1)
    factor = product(panel_one[0], inverse)
    all_factors = lax.all_gather(factor, "col", axis=0)
    gram = crossed(inverse[:, :node_rows], inverse)
    factor_tied, gram = lax.optimization_barrier((factor, gram))
    all_grams = lax.all_gather(gram, "col", axis=0)

    live = (jnp.arange(width_two)[None, :] < widths[:, None]).astype(jnp.float32)
    mask_j = jnp.repeat(pattern_j.astype(jnp.float32), TILE, axis=1)
    mask_r = jnp.repeat(pattern_r.astype(jnp.float32), TILE, axis=1)
    factor_j = []
    factor_r = []
    for i in range(nodes):
        masked_j = panel_two_j[i] * mask_j[i][:, None] * live[i][None, :]
        masked_r = panel_two_r[i] * mask_r[i][:, None] * live[i][None, :]
        factor_j.append(product(masked_j, inv_two[i]))
        factor_r.append(product(masked_r, inv_two[i]))
    near_j = jnp.concatenate(factor_j, 1)
    full_j = jnp.concatenate(row_blocks(near_j), 0)

    root = own_first(zroot, 1)
    full_factor = jnp.concatenate(
        [reordered(block, d) for d, block in enumerate(row_blocks(factor))], 0
    )
    image = product(root, full_factor)
    terms = jnp.sum(factor * image, axis=0).reshape(n, node_rows)
    own_squares = jnp.sum(inverse[:, :node_rows] ** 2, axis=0)
    var_one = (own_squares + row_sum([terms[d] for d in range(n)]))[None, :]

    all_factors, var_one = lax.optimization_barrier((all_factors, var_one))

    parent_factor = [
        lax.dynamic_index_in_dim(all_factors, parents[i], 0, False) for i in range(nodes)
    ]
    reduced = [
        factor_r[i] - product(parent_factor[i], full_j[:, i * width_two : (i + 1) * width_two])
        for i in range(nodes)
    ]
    block_r = []
    sums_j = []
    for i in range(nodes):
        block_r.append(-product(root, jnp.concatenate(row_blocks(reduced[i]), 0)))
        upper = crossed(parent_factor[i], block_r[i]).reshape(n, node_rows, width_two)
        sums_j.append(row_sum([upper[d] for d in range(n)]))
    block_j = []
    for i in range(nodes):
        parent_gram = lax.dynamic_index_in_dim(all_grams, parents[i], 0, False)
        near = product(parent_gram, full_j[:, i * width_two : (i + 1) * width_two])
        block_j.append(-(near + sums_j[i]))

    corrections = jnp.stack(
        [
            jnp.sum(factor_j[i] * block_j[i], axis=0) + jnp.sum(factor_r[i] * block_r[i], axis=0)
            for i in range(nodes)
        ]
    )
    share = width_two // n
    me = lax.axis_index("row")
    ordered = own_first(corrections, 1).reshape(nodes, n, share)
    summed = row_sum([ordered[:, d] for d in range(n)])
    squares = jnp.sum(inv_two * inv_two, axis=1)
    live_share = lax.dynamic_slice_in_dim(live, me * share, share, 1)
    square_share = lax.dynamic_slice_in_dim(squares, me * share, share, 1)
    var_two = live_share * (square_share - summed)
    return (var_one, var_two, jnp.stack(block_j), jnp.stack(block_r))


PIECE = 16
RING = 16
AHEAD = 8
STEP = 128


def mm(left, right):
    return jnp.dot(left, right, precision=PRECISION, preferred_element_type=jnp.float32)


def mm_t(left, right):
    return lax.dot_general(
        left, right, (((0,), (0,)), ((), ())), precision=PRECISION, preferred_element_type=jnp.float32
    )


def line_kernel(
    parents,
    widths,
    tiles_j,
    tiles_r,
    zroot,
    panel_one,
    inv_one,
    panel_j,
    panel_r,
    inv_two,
    var_one,
    var_two,
    z_j,
    z_r,
    root,
    own,
    near_j,
    near_r,
    part_out,
    part_own,
    held,
    staged,
    full_j,
    chosen,
    reduced,
    across,
    beside,
    part_in,
    part_y,
    cross_block,
    note,
    vec_a,
    vec_b,
    loads,
    note_send,
    note_recv,
    x_send,
    x_recv,
    line_send,
    line_recv,
    j_send,
    j_recv,
    g_send,
    g_recv,
    r_send,
    r_recv,
    u_send,
    u_recv,
    a_send,
    a_recv,
    b_send,
    b_recv,
):
    rows = root.shape[0]
    width = own.shape[1]
    node = near_j.shape[0]
    nodes, _, two = z_r.shape
    chunks = own.shape[0] // PIECE
    steps = rows // STEP
    per = STEP // PIECE
    half = width // 2

    z = lax.axis_index("col")
    r = lax.axis_index("row")
    core = r % 2
    side = r // 2
    twin = r + 1 - 2 * core
    over = (r + 2) % 4
    diag = (twin + 2) % 4
    inner = jnp.logical_or(z == 1, z == 2)
    outer = jnp.logical_not(inner)

    def remote(src, dst, send, recv, device):
        return pltpu.make_async_remote_copy(
            src_ref=src,
            dst_ref=dst,
            send_sem=send,
            recv_sem=recv,
            device_id=device,
            device_id_type=pl.DeviceIdType.MESH,
        )

    def at_row(index):
        return (lax.axis_index("groups"), index, z)

    def at_col(index):
        return (lax.axis_index("groups"), r, index)

    def span(index, size):
        return pl.ds(pl.multiple_of(index * size, size), size)

    def child(m):
        return pl.ds(m * two, two)

    def load(k):
        if k == 0:
            return pltpu.make_async_copy(panel_one.at[0], own.at[pl.ds(0, rows)], loads.at[0])
        if k < 3:
            h = k - 1
            return pltpu.make_async_copy(inv_one.at[0, pl.ds(h * half, half)], chosen.at[h], loads.at[k])
        if k < 5:
            m = k - 3
            return pltpu.make_async_copy(panel_j.at[m], near_j.at[:, child(m)], loads.at[k])
        if k == 5:
            return pltpu.make_async_copy(inv_two, part_in, loads.at[5])
        if k < 8:
            m = k - 6
            return pltpu.make_async_copy(panel_r.at[m], near_r.at[:, child(m)], loads.at[k])
        return pltpu.make_async_copy(zroot, root, loads.at[8])

    for k in range(3):
        load(k).start()

    barrier = pltpu.get_barrier_semaphore()

    def greet(device):
        pl.semaphore_signal(barrier, inc=1, device_id=device, device_id_type=pl.DeviceIdType.MESH)

    for peer in (twin, over, diag):
        greet(at_row(peer))

    @pl.when(outer)
    def _():
        greet(at_col(1 + z // 3))

    @pl.when(inner)
    def _():
        greet(at_col(3 - z))
        greet(at_col(((z - 1) * 3) % 4))

    low = z < 2
    place = jnp.where(low, z, 3 - z)
    kin = [jnp.where(low, parents[m], 3 - parents[m]) for m in range(nodes)]
    picks = [
        jnp.where(place == 1, (kin[m] + 3) % 4, jnp.where(kin[m] == 0, 0, 1 + m)) for m in range(nodes)
    ]
    note[0] = jnp.zeros(note.shape[1:], jnp.int32)
    for m in range(nodes):
        note[0, m : m + 1, :] = jnp.full((1, width), kin[m], jnp.int32)

    @pl.when(outer)
    def _():
        pl.semaphore_wait(barrier, 4)

    @pl.when(inner)
    def _():
        pl.semaphore_wait(barrier, 5)

    def note_copy():
        return remote(note.at[0], note.at[1], note_send, note_recv, at_col(1 + z // 3))

    @pl.when(outer)
    def _():
        note_copy().start()

    def line(stream, t):
        at = span(t, PIECE)
        if stream == 0:
            src, dst, device = own.at[at], held.at[2, at], at_col(1 + z // 3)
        elif stream == 1:
            src, dst, device = own.at[at], held.at[0, at], at_col(3 - z)
        elif stream == 2:
            src, dst, device = held.at[2, at], held.at[1, at], at_col(3 - z)
        else:
            src = staged.at[stream - 3, span(t % RING, PIECE)]
            dst, device = held.at[stream - 3, at], at_col(((z - 1) * 3) % 4)
        return remote(src, dst, line_send.at[stream, t], line_recv.at[stream, t], device)

    def to_inner(first, last):
        @pl.when(outer)
        def _():
            def go(t, carry):
                line(0, t).start()
                return carry

            lax.fori_loop(first, last, go, 0)

    def forward(t):
        line(0, t).wait_recv()
        line(2, t).start()

    def chunk(t):
        @pl.when(inner)
        def _():
            @pl.when(t + AHEAD < chunks)
            def _():
                line(1, t + AHEAD).start()
                forward(t + AHEAD)

            line(1, t).wait_recv()
            line(2, t).wait_recv()
            at = span(t, PIECE)
            for m in range(nodes):
                pick = note[1, m : m + 1, :]

                @pl.when(t >= RING)
                def _():
                    line(3 + m, t - RING).wait_send()

                staged[m, span(t % RING, PIECE), :] = jnp.where(
                    pick < 2, own[at, :], jnp.where(pick == 2, held[0, at, :], held[1, at, :])
                )
                line(3 + m, t).start()

        @pl.when(outer)
        def _():
            line(3, t).wait_recv()
            line(4, t).wait_recv()

    def j_copy(k):
        mine = span(r, node)
        theirs = span(over, node)
        if k == 2:
            return remote(full_j.at[theirs], full_j.at[theirs], j_send.at[2], j_recv.at[2], at_row(twin))
        return remote(near_j, full_j.at[mine], j_send.at[k], j_recv.at[k], at_row(over if k == 0 else twin))

    def g_copy(k):
        if k == 4:
            at = pl.ds(0, rows)
            columns = span(1 - core, half)
            return remote(own.at[at, columns], beside, g_send.at[4], g_recv.at[4], at_row(twin))
        top = pl.ds(k // 2 * (rows // 2), rows // 2)
        at = pl.ds(pl.multiple_of(core * rows + k // 2 * (rows // 2), rows // 2), rows // 2)
        if k % 2 == 0:
            columns = span(1 - side, half)
            return remote(own.at[top, columns], across.at[at], g_send.at[k], g_recv.at[k], at_row(over))
        return remote(across.at[at], across.at[at], g_send.at[k], g_recv.at[k], at_row(twin))

    spans = [(k * STEP, STEP) for k in range(steps - 1)]
    spans += [((steps - 1) * STEP, STEP // 2), ((steps - 1) * STEP + STEP // 2, STEP // 2)]

    def r_copy(k, part):
        first, size = spans[part]
        who = over if k == 2 else r
        at = pl.ds(pl.multiple_of(who * rows + first, size), size)
        return remote(
            reduced.at[at],
            reduced.at[at],
            r_send.at[k, part],
            r_recv.at[k, part],
            at_row(over if k == 0 else twin),
        )

    def twice(function):
        def go(h, carry):
            function(h)
            return carry

        lax.fori_loop(0, 2, go, 0)

    part_two = two // 2

    def within(m, h):
        return pl.ds(pl.multiple_of(m * two + h * part_two, part_two), part_two)

    def pick_rows(m, at):
        pick = picks[m]
        first = jnp.where(pick == 0, own[at, :], held[0, at, :])
        second = jnp.where(pick == 2, held[1, at, :], held[2, at, :])
        return jnp.where(pick < 2, first, second)

    def reduce_part(part, m):
        first, size = spans[part]
        at = pl.ds(first, size)
        to = pl.ds(pl.multiple_of(r * rows + first, size), size)
        chosen[m, at, :] = pick_rows(m, at)

        def go(h):
            columns = within(m, h)
            reduced[to, columns] = near_r[at, columns] - mm(chosen[m, at, :], full_j[:, columns])

        twice(go)
        if m == nodes - 1:
            r_copy(0, part).start()
            r_copy(1, part).start()

    def gather_part(part):
        r_copy(0, part).wait_recv()
        r_copy(2, part).start()

    def root_wait(part):
        r_copy(1, part).wait_recv()
        r_copy(2, part).wait_recv()

    def root_step(step, m):
        places = [pl.ds(pl.multiple_of(d * rows + step * STEP, STEP), STEP) for d in range(4)]

        def go(h):
            columns = within(0, h)
            left = jnp.concatenate([root[:, at] for at in places], 1)
            right = jnp.concatenate([reduced[at, within(m, h)] for at in places], 0)
            z_r[m, :, columns] -= mm(left, right)

        twice(go)

    def to_tile(vec):
        return jnp.concatenate([vec[:, i * 128 : (i + 1) * 128] for i in range(vec.shape[1] // 128)], 0)

    def shared(pieces):
        total = jnp.zeros_like(pieces[0])
        for d, one in enumerate(pieces):
            total = total + jnp.where(r == d, one, 0.0)
        return total

    def to_peers(tile, send, recv):
        return [
            remote(tile.at[0], tile.at[1 + k], send.at[k], recv.at[k], at_row(peer))
            for k, peer in enumerate((twin, over, diag))
        ]

    def colsum(left, right):
        return jnp.sum(left * right, axis=0, keepdims=True)

    def factor(first, size):
        at = pl.ds(first, size)
        own[at, :] = mm(own[at, 0:half], chosen[0]) + mm(own[at, half:width], chosen[1])

    def masked(panel, tiles, at, m, first, count):
        column = lax.broadcasted_iota(jnp.int32, (1, two), 1)
        live = (column < widths[m]).astype(jnp.float32)
        blocks = [
            panel[pl.ds(at + i * TILE, TILE), child(m)] * (live * tiles[m, first + i].astype(jnp.float32))
            for i in range(count)
        ]
        return jnp.concatenate(blocks, 0)

    for k in range(3):
        load(k).wait()
    for k in range(3, 9):
        load(k).start()
    factor(0, STEP)
    to_inner(0, per)
    early = 2

    @pl.when(inner)
    def _():
        for t in range(early):
            line(1, t).start()

    for k in range(3, 6):
        load(k).wait()
    for m in range(nodes):
        near_j[:, child(m)] = mm(masked(near_j, tiles_j, 0, m, 0, node // TILE), part_in[m])
    for k in (0, 1):
        j_copy(k).start()

    def pass_on(first, last):
        @pl.when(inner)
        def _():
            for t in range(first, last):
                forward(t)
                if t + early < AHEAD:
                    line(1, t + early).start()

    share = AHEAD // steps
    pass_on(0, share)
    for k in range(1, steps):
        factor(k * STEP, STEP)
        to_inner(k * per, (k + 1) * per)
        pass_on(k * share, (k + 1) * share)
    g_copy(4).start()

    @pl.when(inner)
    def _():
        note_copy().wait_recv()

    full_j[span(r, node), :] = near_j[...]
    for m in range(nodes):
        z_r[m] = jnp.zeros_like(z_r[m])

    def separator_rows(m):
        load(6 + m).wait()

        def go(h):
            size = rows // 2
            at = pl.multiple_of(h * size, size)
            count = size // TILE
            near_r[pl.ds(at, size), child(m)] = mm(masked(near_r, tiles_r, at, m, h * count, count), part_in[m])

        twice(go)

    narrow = node // 2
    thin = narrow * node // width
    thick = node * node // width
    left_core = 2 * side
    others = (r, 2 - left_core, 3 - left_core)

    def gram_block(down, along):
        return mm_t(chosen[0, :, down], chosen[0, :, along]) + mm_t(chosen[1, :, down], chosen[1, :, along])

    def gram_half():
        along = pl.ds(pl.multiple_of((left_core + 1) * node + core * narrow, narrow), narrow)
        block = gram_block(span(left_core, node), along)
        for k in range(node // thin):
            own[rows : rows + thin, k * narrow : (k + 1) * narrow] = block[k * thin : (k + 1) * thin, :]
        to_inner(rows // PIECE, (rows + thin) // PIECE)

    def gram(b):
        block = gram_block(span(r, node), span(others[b], node))
        first = rows + thin + b * thick
        for k in range(node // thick):
            own[first : first + thick, k * node : (k + 1) * node] = block[k * thick : (k + 1) * thick, :]
        to_inner(first // PIECE, (first + thick) // PIECE)

    one = {}

    def square_sums():
        one["squares"] = sum(
            colsum(chosen[h, :, span(r, node)], chosen[h, :, span(r, node)]) for h in range(2)
        )
        one["squares_two"] = [colsum(part_in[m], part_in[m]) for m in range(nodes)]

    def gathered_j():
        j_copy(0).wait_recv()
        j_copy(2).start()
        j_copy(1).wait_recv()
        j_copy(2).wait_recv()

    def diagonal(h):
        block = own[0:rows, h * half : (h + 1) * half]
        one[h] = colsum(block, mm(root[:, span(r, rows)], block))

    def pair():
        g_copy(4).wait_recv()
        product_two = mm(root[:, span(twin, rows)], beside[...])
        one["pair"] = 2.0 * colsum(own[0:rows, span(core, half)], product_two)

    def cross():
        g_copy(1).wait_recv()
        g_copy(3).wait_recv()
        product_two = mm(root[:, span(1 - side, 2 * rows)], across[...])
        product_two = 2.0 * colsum(own[0:rows, span(side, half)], product_two)
        sums = [
            one[h] + jnp.where(core == h, one["pair"], 0.0) + jnp.where(side == h, product_two, 0.0)
            for h in range(2)
        ]
        vec_a[0] = to_tile(jnp.concatenate(sums, 1))
        for copy in to_peers(vec_a, a_send, a_recv):
            copy.start()

    def level_one_out():
        for copy in to_peers(vec_a, a_send, a_recv):
            copy.wait()
        total = vec_a[0] + vec_a[1] + vec_a[2] + vec_a[3]
        each = total.shape[0] // 4
        mine = shared([total[d * each : (d + 1) * each, :] for d in range(4)])
        var_one[...] = one["squares"] + jnp.concatenate([mine[i : i + 1, :] for i in range(each)], 1)

    def pass_g(k):
        g_copy(k).wait_recv()
        g_copy(k + 1).start()

    def node_step(b, m):
        first = rows + thin + b * thick
        packed = pick_rows(m, pl.ds(first, thick))
        block = jnp.concatenate([packed[:, k * node : (k + 1) * node] for k in range(node // thick)], 0)
        part = mm(block, full_j[span(others[b], node), child(m)])
        if b == 0:
            z_j[m] = part
        else:
            z_j[m] += part

    def x_copy():
        place = cross_block.at[:, :, span(core, narrow)]
        return remote(place, place, x_send, x_recv, at_row(twin))

    def share_half():
        for m in range(nodes):
            packed = pick_rows(m, pl.ds(rows, thin))
            block = jnp.concatenate([packed[:, k * narrow : (k + 1) * narrow] for k in range(node // thin)], 0)
            cross_block[m, :, span(core, narrow)] = block
        x_copy().start()

    def twin_step():
        x_copy().wait_recv()
        beyond = span(twin, node)

        @pl.when(core == 0)
        def _():
            for m in range(nodes):
                z_j[m] += mm(cross_block[m], full_j[beyond, child(m)])

        @pl.when(core == 1)
        def _():
            for m in range(nodes):
                z_j[m] += mm_t(cross_block[m], full_j[beyond, child(m)])

    def upper(m, dest):
        return mm_t(chosen[m, :, span(dest, node)], z_r[m])

    def u_copy(k):
        if k < 2:
            out = part_out.at[pl.ds(k * 2 * node, 2 * node)]
            return remote(out, part_in.at[k], u_send.at[k], u_recv.at[k], at_row(twin))
        out = part_own.at[pl.ds((k - 2) * node, node)]
        return remote(out, part_y.at[k - 2], u_send.at[k], u_recv.at[k], at_row(over))

    def upper_twin(m):
        def go(h):
            at = pl.ds(pl.multiple_of((2 * m + h) * node, node), node)
            part_out[at, :] = upper(m, (twin + 2 - 2 * h) % 4)

        twice(go)
        u_copy(m).start()

    def upper_over(m):
        far = upper(m, over)
        u_copy(m).wait_recv()
        part_own[m * node : (m + 1) * node, :] = far + part_in[m, 0:node, :]
        u_copy(2 + m).start()

    def upper_own(m):
        part_in[m, node : 2 * node, :] = part_in[m, node : 2 * node, :] + upper(m, r)

    def separator_sums():
        one["sums_r"] = [colsum(near_r[:, child(m)], z_r[m]) for m in range(nodes)]

    def item(function, *arguments):
        return functools.partial(function, *arguments)

    work = {
        0: [item(separator_rows, 0)],
        1: [item(separator_rows, 1)],
        2: [gram_half],
        3: [item(gram, 0)],
        4: [item(gram, 1)],
        6: [item(gram, 2)],
        5: [square_sums],
        7: [gathered_j, item(reduce_part, 0, 0)],
        8: [item(reduce_part, 0, 1)],
        9: [load(8).wait, item(diagonal, 0)],
        11: [item(diagonal, 1)],
        14: [item(gather_part, 0), g_copy(0).start],
        15: [item(reduce_part, 1, 0)],
        16: [item(reduce_part, 1, 1)],
        17: [item(root_wait, 0), item(root_step, 0, 0)],
        18: [item(root_step, 0, 1)],
        19: [pair],
        22: [item(pass_g, 0), item(gather_part, 1), g_copy(2).start],
        23: [item(reduce_part, 2, 0)],
        24: [item(reduce_part, 2, 1)],
        25: [item(root_wait, 1), item(root_step, 1, 0)],
        26: [item(root_step, 1, 1)],
        27: [item(reduce_part, 3, 0)],
        28: [item(reduce_part, 3, 1)],
        29: [item(pass_g, 2)],
        30: [item(gather_part, 2)],
        31: [item(reduce_part, 4, 0), item(reduce_part, 4, 1)],
        32: [item(root_wait, 2), item(root_step, 2, 0)],
        33: [item(root_step, 2, 1), item(gather_part, 3)],
        34: [share_half],
        35: [item(gather_part, 4), item(root_wait, 3), item(root_wait, 4), item(root_step, 3, 0)],
        36: [item(upper_twin, 0)],
        37: [item(upper_over, 0), item(root_step, 3, 1)],
        38: [item(upper_twin, 1)],
        39: [item(upper_over, 1)],
        40: [item(node_step, 0, 0), item(node_step, 0, 1)],
        41: [cross],
        42: [twin_step, item(node_step, 1, 0), item(node_step, 1, 1)],
        43: [item(upper_own, 0), item(upper_own, 1)],
        44: [level_one_out, separator_sums],
    }
    done = 0
    for last in sorted(work) + [chunks - 1]:
        if last == done:
            chunk(last)
        else:

            def go(t, carry):
                chunk(t)
                return carry

            lax.fori_loop(done, last + 1, go, 0)
        done = last + 1
        for function in work.get(last, ()):
            function()

    sums_r = one["sums_r"]
    for m in range(nodes):
        node_step(2, m)
    for m in range(nodes):
        u_copy(2 + m).wait_recv()
        z_j[m] = -(z_j[m] + part_in[m, node : 2 * node, :] + part_y[m])
        sums_r[m] = sums_r[m] + colsum(near_j[:, child(m)], z_j[m])
    vec_b[0] = to_tile(jnp.concatenate(sums_r, 1))
    for copy in to_peers(vec_b, b_send, b_recv):
        copy.start()

    @pl.when(outer)
    def _():
        note_copy().wait_send()

        def go(t, carry):
            line(0, t).wait_send()
            return carry

        lax.fori_loop(0, chunks, go, 0)

    @pl.when(inner)
    def _():
        def go(t, carry):
            line(1, t).wait_send()
            line(2, t).wait_send()
            return carry

        lax.fori_loop(0, chunks, go, 0)

        def last(t, carry):
            line(3, t).wait_send()
            line(4, t).wait_send()
            return carry

        lax.fori_loop(chunks - RING, chunks, last, 0)

    x_copy().wait_send()
    for k in range(3):
        j_copy(k).wait_send()
    for k in range(5):
        g_copy(k).wait_send()
    for part in range(len(spans)):
        for k in range(3):
            r_copy(k, part).wait_send()
    for k in range(4):
        u_copy(k).wait_send()
    for copy in to_peers(vec_b, b_send, b_recv):
        copy.wait()
    total = vec_b[0] + vec_b[1] + vec_b[2] + vec_b[3]
    share = two // 4
    column = lax.broadcasted_iota(jnp.int32, (1, share), 1) + r * share
    for m in range(nodes):
        mine = shared([total[m * 4 + d : m * 4 + d + 1, :] for d in range(4)])
        square = shared([one["squares_two"][m][:, d * share : (d + 1) * share] for d in range(4)])
        live = (column < widths[m]).astype(jnp.float32)
        var_two[m : m + 1, :] = live * (square - mine)


def copy_kernel(*refs):
    sems = refs[-1]
    order = (3, 2, 0, 1)
    ins = [pltpu.make_async_copy(refs[k], refs[8 + k], sems.at[k]) for k in order]
    outs = [pltpu.make_async_copy(refs[8 + k], refs[4 + k], sems.at[4 + k]) for k in order]
    for copy in ins:
        copy.start()
    for first, second in zip(ins, outs):
        first.wait()
        second.start()
    for copy in outs:
        copy.wait()


def line_body(
    zroot,
    panel_one,
    inv_one,
    panel_two_j,
    panel_two_r,
    inv_two,
    parents,
    widths,
    pattern_j,
    pattern_r,
):
    n = lax.axis_size("row")
    width = inv_one.shape[1]
    node = width // n
    nodes, two = inv_two.shape[:2]
    rows = zroot.shape[0]
    height = rows + node - node // 2 * node // width
    chunks = height // PIECE
    steps = rows // STEP
    f32 = jnp.float32
    smem = pl.BlockSpec(memory_space=pltpu.SMEM)
    hbm = pl.BlockSpec(memory_space=pl.ANY)
    vmem = pl.BlockSpec(memory_space=pltpu.VMEM)
    dma = pltpu.SemaphoreType.DMA
    results = pl.pallas_call(
        line_kernel,
        out_shape=(
            jax.ShapeDtypeStruct((1, node), f32),
            jax.ShapeDtypeStruct((nodes, two // n), f32),
            jax.ShapeDtypeStruct((nodes, node, two), f32),
            jax.ShapeDtypeStruct((nodes, rows, two), f32),
        ),
        in_specs=[smem] * 4 + [hbm] * 6,
        out_specs=(vmem,) * 4,
        scratch_shapes=[
            pltpu.VMEM(zroot.shape, f32),
            pltpu.VMEM((height, width), f32),
            pltpu.VMEM((node, nodes * two), f32),
            pltpu.VMEM((rows, nodes * two), f32),
            pltpu.VMEM((nodes * 2 * node, two), f32),
            pltpu.VMEM((nodes * node, two), f32),
            pltpu.VMEM((3, height, width), f32),
            pltpu.VMEM((nodes, RING * PIECE, width), f32),
            pltpu.VMEM((width, nodes * two), f32),
            pltpu.VMEM((nodes, rows, width), f32),
            pltpu.VMEM((4 * rows, nodes * two), f32),
            pltpu.VMEM((2 * rows, width // 2), f32),
            pltpu.VMEM((rows, width // 2), f32),
            pltpu.VMEM((nodes, 2 * node, two), f32),
            pltpu.VMEM((nodes, node, two), f32),
            pltpu.VMEM((nodes, node, node), f32),
            pltpu.VMEM((2, 8, width), jnp.int32),
            pltpu.VMEM((4, width // 128, 128), f32),
            pltpu.VMEM((4, nodes * two // 128, 128), f32),
            dma((9,)),
            dma,
            dma,
            dma,
            dma,
            dma((5, chunks)),
            dma((5, chunks)),
            dma((3,)),
            dma((3,)),
            dma((5,)),
            dma((5,)),
            dma((3, steps + 1)),
            dma((3, steps + 1)),
            dma((4,)),
            dma((4,)),
            dma((3,)),
            dma((3,)),
            dma((3,)),
            dma((3,)),
        ],
        compiler_params=pltpu.CompilerParams(
            collective_id=0, has_side_effects=True, vmem_limit_bytes=60 * 1024 * 1024
        ),
    )(parents, widths, pattern_j, pattern_r, zroot, panel_one, inv_one, panel_two_j, panel_two_r, inv_two)
    return pl.pallas_call(
        copy_kernel,
        out_shape=tuple(jax.ShapeDtypeStruct(one.shape, one.dtype) for one in results),
        in_specs=[hbm] * 4,
        out_specs=(hbm,) * 4,
        scratch_shapes=[pltpu.VMEM(one.shape, one.dtype) for one in results] + [dma((8,))],
        compiler_params=pltpu.CompilerParams(vmem_limit_bytes=60 * 1024 * 1024),
    )(*results)


def solution(mesh):
    fits = mesh.shape["row"] == 4 and mesh.shape["col"] == 4
    return jax.shard_map(
        line_body if fits else general_body,
        mesh=mesh,
        in_specs=(
            P(("groups", "row"), None),
            P(("groups", "col"), "row", None),
            P(("groups", "col"), None, None),
            P(("groups", "col"), "row", None),
            P(("groups", "col"), "row", None),
            P(("groups", "col"), None, None),
            P(("groups", "col")),
            P(("groups", "col")),
            P(("groups", "col"), "row"),
            P(("groups", "col"), "row"),
        ),
        out_specs=(
            P(("groups", "col"), "row"),
            P(("groups", "col"), "row"),
            P(("groups", "col"), "row", None),
            P(("groups", "col"), "row", None),
        ),
        check_vma=False,
    )
```

```python
import functools

import jax
import jax.numpy as jnp
from jax import lax
from jax.experimental import pallas as pl
from jax.experimental.pallas import tpu as pltpu
from jax.sharding import PartitionSpec as P

TILE = 64
PRECISION = lax.Precision.HIGH


def product(left, right):
    return jnp.dot(left, right, precision=PRECISION, preferred_element_type=jnp.float32)


def crossed(left, right):
    return lax.dot_general(
        left, right, (((0,), (0,)), ((), ())), precision=PRECISION, preferred_element_type=jnp.float32
    )


def swap(block, bit):
    n = lax.axis_size("row")
    return lax.ppermute(block, "row", [(i, i ^ bit) for i in range(n)])


def own_first(array, axis):
    n = lax.axis_size("row")
    me = lax.axis_index("row")
    share = array.shape[axis] // n
    pieces = [
        lax.dynamic_slice_in_dim(array, (me ^ d) * share, share, axis) for d in range(n)
    ]
    return jnp.concatenate(pieces, axis)


def row_blocks(block):
    n = lax.axis_size("row")
    held = {0: block}
    bit = n // 2
    while bit:
        for d in sorted(held):
            held[d | bit] = swap(held[d], bit)
        bit //= 2
    return [held[d] for d in range(n)]


def row_sum(pieces):
    n = lax.axis_size("row")
    held = dict(enumerate(pieces))
    bit = 1
    while bit < n:
        for d in [d for d in sorted(held) if not d & bit]:
            held[d] = held[d] + swap(held.pop(d | bit), bit)
        bit *= 2
    return held[0]


def reordered(block, d):
    n = lax.axis_size("row")
    share = block.shape[1] // n
    return jnp.concatenate(
        [block[:, (d ^ e) * share : ((d ^ e) + 1) * share] for e in range(n)], 1
    )


def general_body(
    zroot,
    panel_one,
    inv_one,
    panel_two_j,
    panel_two_r,
    inv_two,
    parents,
    widths,
    pattern_j,
    pattern_r,
):
    n = lax.axis_size("row")
    width_one = inv_one.shape[1]
    node_rows = width_one // n
    nodes, width_two = inv_two.shape[:2]
    root_rows = zroot.shape[0]

    inverse = own_first(inv_one[0], 1)
    factor = product(panel_one[0], inverse)
    all_factors = lax.all_gather(factor, "col", axis=0)
    gram = crossed(inverse[:, :node_rows], inverse)
    factor_tied, gram = lax.optimization_barrier((factor, gram))
    all_grams = lax.all_gather(gram, "col", axis=0)

    live = (jnp.arange(width_two)[None, :] < widths[:, None]).astype(jnp.float32)
    mask_j = jnp.repeat(pattern_j.astype(jnp.float32), TILE, axis=1)
    mask_r = jnp.repeat(pattern_r.astype(jnp.float32), TILE, axis=1)
    factor_j = []
    factor_r = []
    for i in range(nodes):
        masked_j = panel_two_j[i] * mask_j[i][:, None] * live[i][None, :]
        masked_r = panel_two_r[i] * mask_r[i][:, None] * live[i][None, :]
        factor_j.append(product(masked_j, inv_two[i]))
        factor_r.append(product(masked_r, inv_two[i]))
    near_j = jnp.concatenate(factor_j, 1)
    full_j = jnp.concatenate(row_blocks(near_j), 0)

    root = own_first(zroot, 1)
    full_factor = jnp.concatenate(
        [reordered(block, d) for d, block in enumerate(row_blocks(factor))], 0
    )
    image = product(root, full_factor)
    terms = jnp.sum(factor * image, axis=0).reshape(n, node_rows)
    own_squares = jnp.sum(inverse[:, :node_rows] ** 2, axis=0)
    var_one = (own_squares + row_sum([terms[d] for d in range(n)]))[None, :]

    all_factors, var_one = lax.optimization_barrier((all_factors, var_one))

    parent_factor = [
        lax.dynamic_index_in_dim(all_factors, parents[i], 0, False) for i in range(nodes)
    ]
    reduced = [
        factor_r[i] - product(parent_factor[i], full_j[:, i * width_two : (i + 1) * width_two])
        for i in range(nodes)
    ]
    block_r = []
    sums_j = []
    for i in range(nodes):
        block_r.append(-product(root, jnp.concatenate(row_blocks(reduced[i]), 0)))
        upper = crossed(parent_factor[i], block_r[i]).reshape(n, node_rows, width_two)
        sums_j.append(row_sum([upper[d] for d in range(n)]))
    block_j = []
    for i in range(nodes):
        parent_gram = lax.dynamic_index_in_dim(all_grams, parents[i], 0, False)
        near = product(parent_gram, full_j[:, i * width_two : (i + 1) * width_two])
        block_j.append(-(near + sums_j[i]))

    corrections = jnp.stack(
        [
            jnp.sum(factor_j[i] * block_j[i], axis=0) + jnp.sum(factor_r[i] * block_r[i], axis=0)
            for i in range(nodes)
        ]
    )
    share = width_two // n
    me = lax.axis_index("row")
    ordered = own_first(corrections, 1).reshape(nodes, n, share)
    summed = row_sum([ordered[:, d] for d in range(n)])
    squares = jnp.sum(inv_two * inv_two, axis=1)
    live_share = lax.dynamic_slice_in_dim(live, me * share, share, 1)
    square_share = lax.dynamic_slice_in_dim(squares, me * share, share, 1)
    var_two = live_share * (square_share - summed)
    return (var_one, var_two, jnp.stack(block_j), jnp.stack(block_r))


PIECE = 16
RING = 16
AHEAD = 8
STEP = 128


def mm(left, right):
    return jnp.dot(left, right, precision=PRECISION, preferred_element_type=jnp.float32)


def mm_t(left, right):
    return lax.dot_general(
        left, right, (((0,), (0,)), ((), ())), precision=PRECISION, preferred_element_type=jnp.float32
    )


def line_kernel(
    parents,
    widths,
    tiles_j,
    tiles_r,
    zroot,
    panel_one,
    inv_one,
    panel_j,
    panel_r,
    inv_two,
    var_one,
    var_two,
    z_j,
    z_out,
    z_r,
    root,
    own,
    near_j,
    near_r,
    part_out,
    part_own,
    held,
    staged,
    full_j,
    chosen,
    reduced,
    across,
    beside,
    part_in,
    part_y,
    cross_block,
    note,
    vec_a,
    vec_b,
    loads,
    note_send,
    note_recv,
    x_send,
    x_recv,
    line_send,
    line_recv,
    j_send,
    j_recv,
    g_send,
    g_recv,
    r_send,
    r_recv,
    u_send,
    u_recv,
    a_send,
    a_recv,
    b_send,
    b_recv,
):
    rows = root.shape[0]
    width = own.shape[1]
    node = near_j.shape[0]
    nodes, _, two = z_r.shape
    chunks = own.shape[0] // PIECE
    steps = rows // STEP
    per = STEP // PIECE
    half = width // 2

    z = lax.axis_index("col")
    r = lax.axis_index("row")
    core = r % 2
    side = r // 2
    twin = r + 1 - 2 * core
    over = (r + 2) % 4
    diag = (twin + 2) % 4
    inner = jnp.logical_or(z == 1, z == 2)
    outer = jnp.logical_not(inner)

    def remote(src, dst, send, recv, device):
        return pltpu.make_async_remote_copy(
            src_ref=src,
            dst_ref=dst,
            send_sem=send,
            recv_sem=recv,
            device_id=device,
            device_id_type=pl.DeviceIdType.MESH,
        )

    def at_row(index):
        return (lax.axis_index("groups"), index, z)

    def at_col(index):
        return (lax.axis_index("groups"), r, index)

    def span(index, size):
        return pl.ds(pl.multiple_of(index * size, size), size)

    def child(m):
        return pl.ds(m * two, two)

    def load(k):
        if k == 0:
            return pltpu.make_async_copy(panel_one.at[0], own.at[pl.ds(0, rows)], loads.at[0])
        if k < 3:
            h = k - 1
            return pltpu.make_async_copy(inv_one.at[0, pl.ds(h * half, half)], chosen.at[h], loads.at[k])
        if k < 5:
            m = k - 3
            return pltpu.make_async_copy(panel_j.at[m], near_j.at[:, child(m)], loads.at[k])
        if k == 5:
            return pltpu.make_async_copy(inv_two, part_in, loads.at[5])
        if k < 8:
            m = k - 6
            return pltpu.make_async_copy(panel_r.at[m], near_r.at[:, child(m)], loads.at[k])
        return pltpu.make_async_copy(zroot, root, loads.at[8])

    for k in range(3):
        load(k).start()

    barrier = pltpu.get_barrier_semaphore()

    def greet(device):
        pl.semaphore_signal(barrier, inc=1, device_id=device, device_id_type=pl.DeviceIdType.MESH)

    for peer in (twin, over, diag):
        greet(at_row(peer))

    @pl.when(outer)
    def _():
        greet(at_col(1 + z // 3))

    @pl.when(inner)
    def _():
        greet(at_col(3 - z))
        greet(at_col(((z - 1) * 3) % 4))

    low = z < 2
    place = jnp.where(low, z, 3 - z)
    kin = [jnp.where(low, parents[m], 3 - parents[m]) for m in range(nodes)]
    picks = [
        jnp.where(place == 1, (kin[m] + 3) % 4, jnp.where(kin[m] == 0, 0, 1 + m)) for m in range(nodes)
    ]
    note[0] = jnp.zeros(note.shape[1:], jnp.int32)
    for m in range(nodes):
        note[0, m : m + 1, :] = jnp.full((1, width), kin[m], jnp.int32)

    @pl.when(outer)
    def _():
        pl.semaphore_wait(barrier, 4)

    @pl.when(inner)
    def _():
        pl.semaphore_wait(barrier, 5)

    def note_copy():
        return remote(note.at[0], note.at[1], note_send, note_recv, at_col(1 + z // 3))

    @pl.when(outer)
    def _():
        note_copy().start()

    def line(stream, t):
        at = span(t, PIECE)
        if stream == 0:
            src, dst, device = own.at[at], held.at[2, at], at_col(1 + z // 3)
        elif stream == 1:
            src, dst, device = own.at[at], held.at[0, at], at_col(3 - z)
        elif stream == 2:
            src, dst, device = held.at[2, at], held.at[1, at], at_col(3 - z)
        else:
            src = staged.at[stream - 3, span(t % RING, PIECE)]
            dst, device = held.at[stream - 3, at], at_col(((z - 1) * 3) % 4)
        return remote(src, dst, line_send.at[stream, t], line_recv.at[stream, t], device)

    def to_inner(first, last):
        @pl.when(outer)
        def _():
            def go(t, carry):
                line(0, t).start()
                return carry

            lax.fori_loop(first, last, go, 0)

    def forward(t):
        line(0, t).wait_recv()
        line(2, t).start()

    def chunk(t):
        @pl.when(inner)
        def _():
            @pl.when(t + AHEAD < chunks)
            def _():
                line(1, t + AHEAD).start()
                forward(t + AHEAD)

            line(1, t).wait_recv()
            line(2, t).wait_recv()
            at = span(t, PIECE)
            for m in range(nodes):
                pick = note[1, m : m + 1, :]

                @pl.when(t >= RING)
                def _():
                    line(3 + m, t - RING).wait_send()

                staged[m, span(t % RING, PIECE), :] = jnp.where(
                    pick < 2, own[at, :], jnp.where(pick == 2, held[0, at, :], held[1, at, :])
                )
                line(3 + m, t).start()

        @pl.when(outer)
        def _():
            line(3, t).wait_recv()
            line(4, t).wait_recv()

    def j_copy(k):
        mine = span(r, node)
        theirs = span(over, node)
        if k == 2:
            return remote(full_j.at[theirs], full_j.at[theirs], j_send.at[2], j_recv.at[2], at_row(twin))
        return remote(near_j, full_j.at[mine], j_send.at[k], j_recv.at[k], at_row(over if k == 0 else twin))

    def g_copy(k):
        if k == 4:
            at = pl.ds(0, rows)
            columns = span(1 - core, half)
            return remote(own.at[at, columns], beside, g_send.at[4], g_recv.at[4], at_row(twin))
        top = pl.ds(k // 2 * (rows // 2), rows // 2)
        at = pl.ds(pl.multiple_of(core * rows + k // 2 * (rows // 2), rows // 2), rows // 2)
        if k % 2 == 0:
            columns = span(1 - side, half)
            return remote(own.at[top, columns], across.at[at], g_send.at[k], g_recv.at[k], at_row(over))
        return remote(across.at[at], across.at[at], g_send.at[k], g_recv.at[k], at_row(twin))

    spans = [(k * STEP, STEP) for k in range(steps - 1)]
    spans += [((steps - 1) * STEP, STEP // 2), ((steps - 1) * STEP + STEP // 2, STEP // 2)]

    def r_copy(k, part):
        first, size = spans[part]
        who = over if k == 2 else r
        at = pl.ds(pl.multiple_of(who * rows + first, size), size)
        return remote(
            reduced.at[at],
            reduced.at[at],
            r_send.at[k, part],
            r_recv.at[k, part],
            at_row(over if k == 0 else twin),
        )

    def twice(function):
        def go(h, carry):
            function(h)
            return carry

        lax.fori_loop(0, 2, go, 0)

    part_two = two // 2

    def within(m, h):
        return pl.ds(pl.multiple_of(m * two + h * part_two, part_two), part_two)

    def pick_rows(m, at):
        pick = picks[m]
        first = jnp.where(pick == 0, own[at, :], held[0, at, :])
        second = jnp.where(pick == 2, held[1, at, :], held[2, at, :])
        return jnp.where(pick < 2, first, second)

    def reduce_part(part, m):
        first, size = spans[part]
        at = pl.ds(first, size)
        to = pl.ds(pl.multiple_of(r * rows + first, size), size)
        chosen[m, at, :] = pick_rows(m, at)

        def go(h):
            columns = within(m, h)
            reduced[to, columns] = near_r[at, columns] - mm(chosen[m, at, :], full_j[:, columns])

        twice(go)
        if m == nodes - 1:
            r_copy(0, part).start()
            r_copy(1, part).start()

    def gather_part(part):
        r_copy(0, part).wait_recv()
        r_copy(2, part).start()

    def root_wait(part):
        r_copy(1, part).wait_recv()
        r_copy(2, part).wait_recv()

    def root_step(step, m):
        places = [pl.ds(pl.multiple_of(d * rows + step * STEP, STEP), STEP) for d in range(4)]

        def go(h):
            columns = within(0, h)
            left = jnp.concatenate([root[:, at] for at in places], 1)
            right = jnp.concatenate([reduced[at, within(m, h)] for at in places], 0)
            z_r[m, :, columns] -= mm(left, right)

        twice(go)

    def to_tile(vec):
        return jnp.concatenate([vec[:, i * 128 : (i + 1) * 128] for i in range(vec.shape[1] // 128)], 0)

    def shared(pieces):
        total = jnp.zeros_like(pieces[0])
        for d, one in enumerate(pieces):
            total = total + jnp.where(r == d, one, 0.0)
        return total

    def to_peers(tile, send, recv):
        return [
            remote(tile.at[0], tile.at[1 + k], send.at[k], recv.at[k], at_row(peer))
            for k, peer in enumerate((twin, over, diag))
        ]

    def colsum(left, right):
        return jnp.sum(left * right, axis=0, keepdims=True)

    def factor(first, size):
        at = pl.ds(first, size)
        own[at, :] = mm(own[at, 0:half], chosen[0]) + mm(own[at, half:width], chosen[1])

    def masked(panel, tiles, at, m, first, count):
        column = lax.broadcasted_iota(jnp.int32, (1, two), 1)
        live = (column < widths[m]).astype(jnp.float32)
        blocks = [
            panel[pl.ds(at + i * TILE, TILE), child(m)] * (live * tiles[m, first + i].astype(jnp.float32))
            for i in range(count)
        ]
        return jnp.concatenate(blocks, 0)

    for k in range(3):
        load(k).wait()
    for k in range(3, 9):
        load(k).start()
    factor(0, STEP)
    to_inner(0, per)
    early = 2

    @pl.when(inner)
    def _():
        for t in range(early):
            line(1, t).start()

    for k in range(3, 6):
        load(k).wait()
    for m in range(nodes):
        near_j[:, child(m)] = mm(masked(near_j, tiles_j, 0, m, 0, node // TILE), part_in[m])
    for k in (0, 1):
        j_copy(k).start()

    def pass_on(first, last):
        @pl.when(inner)
        def _():
            for t in range(first, last):
                forward(t)
                if t + early < AHEAD:
                    line(1, t + early).start()

    share = AHEAD // steps
    pass_on(0, share)
    for k in range(1, steps):
        factor(k * STEP, STEP)
        to_inner(k * per, (k + 1) * per)
        pass_on(k * share, (k + 1) * share)
    g_copy(4).start()

    @pl.when(inner)
    def _():
        note_copy().wait_recv()

    full_j[span(r, node), :] = near_j[...]
    for m in range(nodes):
        z_r[m] = jnp.zeros_like(z_r[m])

    def separator_rows(m):
        load(6 + m).wait()

        def go(h):
            size = rows // 2
            at = pl.multiple_of(h * size, size)
            count = size // TILE
            near_r[pl.ds(at, size), child(m)] = mm(masked(near_r, tiles_r, at, m, h * count, count), part_in[m])

        twice(go)

    narrow = node // 2
    thin = narrow * node // width
    thick = node * node // width
    left_core = 2 * side
    others = (r, 2 - left_core, 3 - left_core)

    def gram_block(down, along):
        return mm_t(chosen[0, :, down], chosen[0, :, along]) + mm_t(chosen[1, :, down], chosen[1, :, along])

    def gram_half():
        along = pl.ds(pl.multiple_of((left_core + 1) * node + core * narrow, narrow), narrow)
        block = gram_block(span(left_core, node), along)
        for k in range(node // thin):
            own[rows : rows + thin, k * narrow : (k + 1) * narrow] = block[k * thin : (k + 1) * thin, :]
        to_inner(rows // PIECE, (rows + thin) // PIECE)

    def gram(b):
        block = gram_block(span(r, node), span(others[b], node))
        first = rows + thin + b * thick
        for k in range(node // thick):
            own[first : first + thick, k * node : (k + 1) * node] = block[k * thick : (k + 1) * thick, :]
        to_inner(first // PIECE, (first + thick) // PIECE)

    one = {}

    def square_sums():
        one["squares"] = sum(
            colsum(chosen[h, :, span(r, node)], chosen[h, :, span(r, node)]) for h in range(2)
        )
        one["squares_two"] = [colsum(part_in[m], part_in[m]) for m in range(nodes)]

    def gathered_j():
        j_copy(0).wait_recv()
        j_copy(2).start()
        j_copy(1).wait_recv()
        j_copy(2).wait_recv()

    def diagonal(h):
        block = own[0:rows, h * half : (h + 1) * half]
        one[h] = colsum(block, mm(root[:, span(r, rows)], block))

    def pair():
        g_copy(4).wait_recv()
        product_two = mm(root[:, span(twin, rows)], beside[...])
        one["pair"] = 2.0 * colsum(own[0:rows, span(core, half)], product_two)

    def cross():
        g_copy(1).wait_recv()
        g_copy(3).wait_recv()
        product_two = mm(root[:, span(1 - side, 2 * rows)], across[...])
        product_two = 2.0 * colsum(own[0:rows, span(side, half)], product_two)
        sums = [
            one[h] + jnp.where(core == h, one["pair"], 0.0) + jnp.where(side == h, product_two, 0.0)
            for h in range(2)
        ]
        vec_a[0] = to_tile(jnp.concatenate(sums, 1))
        for copy in to_peers(vec_a, a_send, a_recv):
            copy.start()

    def level_one_out():
        for copy in to_peers(vec_a, a_send, a_recv):
            copy.wait()
        total = vec_a[0] + vec_a[1] + vec_a[2] + vec_a[3]
        each = total.shape[0] // 4
        mine = shared([total[d * each : (d + 1) * each, :] for d in range(4)])
        var_one[...] = one["squares"] + jnp.concatenate([mine[i : i + 1, :] for i in range(each)], 1)

    def pass_g(k):
        g_copy(k).wait_recv()
        g_copy(k + 1).start()

    def node_step(b, m):
        first = rows + thin + b * thick
        packed = pick_rows(m, pl.ds(first, thick))
        block = jnp.concatenate([packed[:, k * node : (k + 1) * node] for k in range(node // thick)], 0)
        part = mm(block, full_j[span(others[b], node), child(m)])
        if b == 0:
            z_j[m] = part
        else:
            z_j[m] += part

    def x_copy():
        place = cross_block.at[:, :, span(core, narrow)]
        return remote(place, place, x_send, x_recv, at_row(twin))

    def share_half():
        for m in range(nodes):
            packed = pick_rows(m, pl.ds(rows, thin))
            block = jnp.concatenate([packed[:, k * narrow : (k + 1) * narrow] for k in range(node // thin)], 0)
            cross_block[m, :, span(core, narrow)] = block
        x_copy().start()

    def twin_step():
        x_copy().wait_recv()
        beyond = span(twin, node)

        @pl.when(core == 0)
        def _():
            for m in range(nodes):
                z_j[m] += mm(cross_block[m], full_j[beyond, child(m)])

        @pl.when(core == 1)
        def _():
            for m in range(nodes):
                z_j[m] += mm_t(cross_block[m], full_j[beyond, child(m)])

    def upper(m, dest):
        return mm_t(chosen[m, :, span(dest, node)], z_r[m])

    def u_copy(k):
        if k < 2:
            out = part_out.at[pl.ds(k * 2 * node, 2 * node)]
            return remote(out, part_in.at[k], u_send.at[k], u_recv.at[k], at_row(twin))
        out = part_own.at[pl.ds((k - 2) * node, node)]
        return remote(out, part_y.at[k - 2], u_send.at[k], u_recv.at[k], at_row(over))

    def upper_twin(m):
        def go(h):
            at = pl.ds(pl.multiple_of((2 * m + h) * node, node), node)
            part_out[at, :] = upper(m, (twin + 2 - 2 * h) % 4)

        twice(go)
        u_copy(m).start()

    def upper_over(m):
        far = upper(m, over)
        u_copy(m).wait_recv()
        part_own[m * node : (m + 1) * node, :] = far + part_in[m, 0:node, :]
        u_copy(2 + m).start()

    def upper_own(m):
        part_in[m, node : 2 * node, :] = part_in[m, node : 2 * node, :] + upper(m, r)

    def leave():
        return pltpu.make_async_copy(z_r, z_out, loads.at[9])

    def separator_sums():
        leave().start()
        one["sums_r"] = [colsum(near_r[:, child(m)], z_r[m]) for m in range(nodes)]

    def item(function, *arguments):
        return functools.partial(function, *arguments)

    work = {
        0: [item(separator_rows, 0)],
        1: [item(separator_rows, 1)],
        2: [gram_half],
        3: [item(gram, 0)],
        4: [item(gram, 1)],
        6: [item(gram, 2)],
        5: [square_sums],
        7: [gathered_j, item(reduce_part, 0, 0)],
        8: [item(reduce_part, 0, 1)],
        9: [load(8).wait, item(diagonal, 0)],
        11: [item(diagonal, 1)],
        14: [item(gather_part, 0), g_copy(0).start],
        15: [item(reduce_part, 1, 0)],
        16: [item(reduce_part, 1, 1)],
        17: [item(root_wait, 0), item(root_step, 0, 0)],
        18: [item(root_step, 0, 1)],
        19: [pair],
        22: [item(pass_g, 0), item(gather_part, 1), g_copy(2).start],
        23: [item(reduce_part, 2, 0)],
        24: [item(reduce_part, 2, 1)],
        25: [item(root_wait, 1), item(root_step, 1, 0)],
        26: [item(root_step, 1, 1)],
        27: [item(reduce_part, 3, 0)],
        28: [item(reduce_part, 3, 1)],
        29: [item(pass_g, 2)],
        30: [item(gather_part, 2)],
        31: [item(reduce_part, 4, 0), item(reduce_part, 4, 1)],
        32: [item(root_wait, 2), item(root_step, 2, 0)],
        33: [item(root_step, 2, 1), item(gather_part, 3)],
        34: [share_half],
        35: [item(gather_part, 4), item(root_wait, 3), item(root_wait, 4), item(root_step, 3, 0)],
        36: [item(upper_twin, 0)],
        37: [item(upper_over, 0), item(root_step, 3, 1)],
        38: [item(upper_twin, 1)],
        39: [item(upper_over, 1)],
        40: [item(node_step, 0, 0), item(node_step, 0, 1)],
        41: [cross],
        42: [twin_step, item(node_step, 1, 0), item(node_step, 1, 1)],
        43: [item(upper_own, 0), item(upper_own, 1)],
        44: [level_one_out, separator_sums],
    }
    done = 0
    for last in sorted(work) + [chunks - 1]:
        if last == done:
            chunk(last)
        else:

            def go(t, carry):
                chunk(t)
                return carry

            lax.fori_loop(done, last + 1, go, 0)
        done = last + 1
        for function in work.get(last, ()):
            function()

    sums_r = one["sums_r"]
    for m in range(nodes):
        node_step(2, m)
    for m in range(nodes):
        u_copy(2 + m).wait_recv()
        z_j[m] = -(z_j[m] + part_in[m, node : 2 * node, :] + part_y[m])
        sums_r[m] = sums_r[m] + colsum(near_j[:, child(m)], z_j[m])
    vec_b[0] = to_tile(jnp.concatenate(sums_r, 1))
    for copy in to_peers(vec_b, b_send, b_recv):
        copy.start()

    @pl.when(outer)
    def _():
        note_copy().wait_send()

        def go(t, carry):
            line(0, t).wait_send()
            return carry

        lax.fori_loop(0, chunks, go, 0)

    @pl.when(inner)
    def _():
        def go(t, carry):
            line(1, t).wait_send()
            line(2, t).wait_send()
            return carry

        lax.fori_loop(0, chunks, go, 0)

        def last(t, carry):
            line(3, t).wait_send()
            line(4, t).wait_send()
            return carry

        lax.fori_loop(chunks - RING, chunks, last, 0)

    x_copy().wait_send()
    leave().wait()
    for k in range(3):
        j_copy(k).wait_send()
    for k in range(5):
        g_copy(k).wait_send()
    for part in range(len(spans)):
        for k in range(3):
            r_copy(k, part).wait_send()
    for k in range(4):
        u_copy(k).wait_send()
    for copy in to_peers(vec_b, b_send, b_recv):
        copy.wait()
    total = vec_b[0] + vec_b[1] + vec_b[2] + vec_b[3]
    share = two // 4
    column = lax.broadcasted_iota(jnp.int32, (1, share), 1) + r * share
    for m in range(nodes):
        mine = shared([total[m * 4 + d : m * 4 + d + 1, :] for d in range(4)])
        square = shared([one["squares_two"][m][:, d * share : (d + 1) * share] for d in range(4)])
        live = (column < widths[m]).astype(jnp.float32)
        var_two[m : m + 1, :] = live * (square - mine)


def copy_kernel(*refs):
    sems = refs[-1]
    nodes, rows, _ = refs[3].shape
    parts = [(3, (m, pl.ds(h * (rows // 2), rows // 2))) for m in range(nodes) for h in range(2)]
    parts += [(2, (m,)) for m in range(nodes)] + [(0, ()), (1, ())]

    def at(ref, place):
        return ref.at[place] if place else ref

    ins = []
    outs = []
    for i, (k, place) in enumerate(parts):
        source, middle, target = (at(refs[k + 4 * d], place) for d in (0, 2, 1))
        ins.append(pltpu.make_async_copy(source, middle, sems.at[i]))
        outs.append(pltpu.make_async_copy(middle, target, sems.at[len(parts) + i]))
    for copy in ins:
        copy.start()
    for first, second in zip(ins, outs):
        first.wait()
        second.start()
    for copy in outs:
        copy.wait()


def line_body(
    zroot,
    panel_one,
    inv_one,
    panel_two_j,
    panel_two_r,
    inv_two,
    parents,
    widths,
    pattern_j,
    pattern_r,
):
    n = lax.axis_size("row")
    width = inv_one.shape[1]
    node = width // n
    nodes, two = inv_two.shape[:2]
    rows = zroot.shape[0]
    height = rows + node - node // 2 * node // width
    chunks = height // PIECE
    steps = rows // STEP
    f32 = jnp.float32
    smem = pl.BlockSpec(memory_space=pltpu.SMEM)
    hbm = pl.BlockSpec(memory_space=pl.ANY)
    vmem = pl.BlockSpec(memory_space=pltpu.VMEM)
    dma = pltpu.SemaphoreType.DMA
    results = pl.pallas_call(
        line_kernel,
        out_shape=(
            jax.ShapeDtypeStruct((1, node), f32),
            jax.ShapeDtypeStruct((nodes, two // n), f32),
            jax.ShapeDtypeStruct((nodes, node, two), f32),
            jax.ShapeDtypeStruct((nodes, rows, two), f32),
        ),
        in_specs=[smem] * 4 + [hbm] * 6,
        out_specs=(vmem, vmem, vmem, hbm),
        scratch_shapes=[
            pltpu.VMEM((nodes, rows, two), f32),
            pltpu.VMEM(zroot.shape, f32),
            pltpu.VMEM((height, width), f32),
            pltpu.VMEM((node, nodes * two), f32),
            pltpu.VMEM((rows, nodes * two), f32),
            pltpu.VMEM((nodes * 2 * node, two), f32),
            pltpu.VMEM((nodes * node, two), f32),
            pltpu.VMEM((3, height, width), f32),
            pltpu.VMEM((nodes, RING * PIECE, width), f32),
            pltpu.VMEM((width, nodes * two), f32),
            pltpu.VMEM((nodes, rows, width), f32),
            pltpu.VMEM((4 * rows, nodes * two), f32),
            pltpu.VMEM((2 * rows, width // 2), f32),
            pltpu.VMEM((rows, width // 2), f32),
            pltpu.VMEM((nodes, 2 * node, two), f32),
            pltpu.VMEM((nodes, node, two), f32),
            pltpu.VMEM((nodes, node, node), f32),
            pltpu.VMEM((2, 8, width), jnp.int32),
            pltpu.VMEM((4, width // 128, 128), f32),
            pltpu.VMEM((4, nodes * two // 128, 128), f32),
            dma((10,)),
            dma,
            dma,
            dma,
            dma,
            dma((5, chunks)),
            dma((5, chunks)),
            dma((3,)),
            dma((3,)),
            dma((5,)),
            dma((5,)),
            dma((3, steps + 1)),
            dma((3, steps + 1)),
            dma((4,)),
            dma((4,)),
            dma((3,)),
            dma((3,)),
            dma((3,)),
            dma((3,)),
        ],
        compiler_params=pltpu.CompilerParams(
            collective_id=0, has_side_effects=True, vmem_limit_bytes=60 * 1024 * 1024
        ),
    )(parents, widths, pattern_j, pattern_r, zroot, panel_one, inv_one, panel_two_j, panel_two_r, inv_two)
    return pl.pallas_call(
        copy_kernel,
        out_shape=tuple(jax.ShapeDtypeStruct(one.shape, one.dtype) for one in results),
        in_specs=[hbm] * 4,
        out_specs=(hbm,) * 4,
        scratch_shapes=[pltpu.VMEM(one.shape, one.dtype) for one in results] + [dma((2 * (3 * nodes + 2),))],
        compiler_params=pltpu.CompilerParams(vmem_limit_bytes=60 * 1024 * 1024),
    )(*results)


def solution(mesh):
    fits = mesh.shape["row"] == 4 and mesh.shape["col"] == 4
    return jax.shard_map(
        line_body if fits else general_body,
        mesh=mesh,
        in_specs=(
            P(("groups", "row"), None),
            P(("groups", "col"), "row", None),
            P(("groups", "col"), None, None),
            P(("groups", "col"), "row", None),
            P(("groups", "col"), "row", None),
            P(("groups", "col"), None, None),
            P(("groups", "col")),
            P(("groups", "col")),
            P(("groups", "col"), "row"),
            P(("groups", "col"), "row"),
        ),
        out_specs=(
            P(("groups", "col"), "row"),
            P(("groups", "col"), "row"),
            P(("groups", "col"), "row", None),
            P(("groups", "col"), "row", None),
        ),
        check_vma=False,
    )
```

```python
import functools

import jax
import jax.numpy as jnp
from jax import lax
from jax.experimental import pallas as pl
from jax.experimental.pallas import tpu as pltpu
from jax.sharding import PartitionSpec as P

TILE = 64
PRECISION = lax.Precision.HIGH


def product(left, right):
    return jnp.dot(left, right, precision=PRECISION, preferred_element_type=jnp.float32)


def crossed(left, right):
    return lax.dot_general(
        left, right, (((0,), (0,)), ((), ())), precision=PRECISION, preferred_element_type=jnp.float32
    )


def swap(block, bit):
    n = lax.axis_size("row")
    return lax.ppermute(block, "row", [(i, i ^ bit) for i in range(n)])


def own_first(array, axis):
    n = lax.axis_size("row")
    me = lax.axis_index("row")
    share = array.shape[axis] // n
    pieces = [
        lax.dynamic_slice_in_dim(array, (me ^ d) * share, share, axis) for d in range(n)
    ]
    return jnp.concatenate(pieces, axis)


def row_blocks(block):
    n = lax.axis_size("row")
    held = {0: block}
    bit = n // 2
    while bit:
        for d in sorted(held):
            held[d | bit] = swap(held[d], bit)
        bit //= 2
    return [held[d] for d in range(n)]


def row_sum(pieces):
    n = lax.axis_size("row")
    held = dict(enumerate(pieces))
    bit = 1
    while bit < n:
        for d in [d for d in sorted(held) if not d & bit]:
            held[d] = held[d] + swap(held.pop(d | bit), bit)
        bit *= 2
    return held[0]


def reordered(block, d):
    n = lax.axis_size("row")
    share = block.shape[1] // n
    return jnp.concatenate(
        [block[:, (d ^ e) * share : ((d ^ e) + 1) * share] for e in range(n)], 1
    )


def general_body(
    zroot,
    panel_one,
    inv_one,
    panel_two_j,
    panel_two_r,
    inv_two,
    parents,
    widths,
    pattern_j,
    pattern_r,
):
    n = lax.axis_size("row")
    width_one = inv_one.shape[1]
    node_rows = width_one // n
    nodes, width_two = inv_two.shape[:2]
    root_rows = zroot.shape[0]

    inverse = own_first(inv_one[0], 1)
    factor = product(panel_one[0], inverse)
    all_factors = lax.all_gather(factor, "col", axis=0)
    gram = crossed(inverse[:, :node_rows], inverse)
    factor_tied, gram = lax.optimization_barrier((factor, gram))
    all_grams = lax.all_gather(gram, "col", axis=0)

    live = (jnp.arange(width_two)[None, :] < widths[:, None]).astype(jnp.float32)
    mask_j = jnp.repeat(pattern_j.astype(jnp.float32), TILE, axis=1)
    mask_r = jnp.repeat(pattern_r.astype(jnp.float32), TILE, axis=1)
    factor_j = []
    factor_r = []
    for i in range(nodes):
        masked_j = panel_two_j[i] * mask_j[i][:, None] * live[i][None, :]
        masked_r = panel_two_r[i] * mask_r[i][:, None] * live[i][None, :]
        factor_j.append(product(masked_j, inv_two[i]))
        factor_r.append(product(masked_r, inv_two[i]))
    near_j = jnp.concatenate(factor_j, 1)
    full_j = jnp.concatenate(row_blocks(near_j), 0)

    root = own_first(zroot, 1)
    full_factor = jnp.concatenate(
        [reordered(block, d) for d, block in enumerate(row_blocks(factor))], 0
    )
    image = product(root, full_factor)
    terms = jnp.sum(factor * image, axis=0).reshape(n, node_rows)
    own_squares = jnp.sum(inverse[:, :node_rows] ** 2, axis=0)
    var_one = (own_squares + row_sum([terms[d] for d in range(n)]))[None, :]

    all_factors, var_one = lax.optimization_barrier((all_factors, var_one))

    parent_factor = [
        lax.dynamic_index_in_dim(all_factors, parents[i], 0, False) for i in range(nodes)
    ]
    reduced = [
        factor_r[i] - product(parent_factor[i], full_j[:, i * width_two : (i + 1) * width_two])
        for i in range(nodes)
    ]
    block_r = []
    sums_j = []
    for i in range(nodes):
        block_r.append(-product(root, jnp.concatenate(row_blocks(reduced[i]), 0)))
        upper = crossed(parent_factor[i], block_r[i]).reshape(n, node_rows, width_two)
        sums_j.append(row_sum([upper[d] for d in range(n)]))
    block_j = []
    for i in range(nodes):
        parent_gram = lax.dynamic_index_in_dim(all_grams, parents[i], 0, False)
        near = product(parent_gram, full_j[:, i * width_two : (i + 1) * width_two])
        block_j.append(-(near + sums_j[i]))

    corrections = jnp.stack(
        [
            jnp.sum(factor_j[i] * block_j[i], axis=0) + jnp.sum(factor_r[i] * block_r[i], axis=0)
            for i in range(nodes)
        ]
    )
    share = width_two // n
    me = lax.axis_index("row")
    ordered = own_first(corrections, 1).reshape(nodes, n, share)
    summed = row_sum([ordered[:, d] for d in range(n)])
    squares = jnp.sum(inv_two * inv_two, axis=1)
    live_share = lax.dynamic_slice_in_dim(live, me * share, share, 1)
    square_share = lax.dynamic_slice_in_dim(squares, me * share, share, 1)
    var_two = live_share * (square_share - summed)
    return (var_one, var_two, jnp.stack(block_j), jnp.stack(block_r))


PIECE = 16
RING = 16
AHEAD = 8
STEP = 128


def mm(left, right):
    return jnp.dot(left, right, precision=PRECISION, preferred_element_type=jnp.float32)


def mm_t(left, right):
    return lax.dot_general(
        left, right, (((0,), (0,)), ((), ())), precision=PRECISION, preferred_element_type=jnp.float32
    )


def line_kernel(
    parents,
    widths,
    tiles_j,
    tiles_r,
    zroot,
    panel_one,
    inv_one,
    panel_j,
    panel_r,
    inv_two,
    var_one,
    var_two,
    z_j,
    z_out,
    z_r,
    root,
    own,
    near_j,
    near_r,
    part_out,
    part_own,
    held,
    staged,
    full_j,
    chosen,
    reduced,
    across,
    beside,
    part_in,
    part_y,
    cross_block,
    note,
    vec_a,
    vec_b,
    loads,
    note_send,
    note_recv,
    x_send,
    x_recv,
    line_send,
    line_recv,
    j_send,
    j_recv,
    g_send,
    g_recv,
    r_send,
    r_recv,
    u_send,
    u_recv,
    a_send,
    a_recv,
    b_send,
    b_recv,
):
    rows = root.shape[0]
    width = own.shape[1]
    node = near_j.shape[0]
    nodes, _, two = z_r.shape
    chunks = own.shape[0] // PIECE
    steps = rows // STEP
    per = STEP // PIECE
    half = width // 2

    z = lax.axis_index("col")
    r = lax.axis_index("row")
    core = r % 2
    side = r // 2
    twin = r + 1 - 2 * core
    over = (r + 2) % 4
    diag = (twin + 2) % 4
    inner = jnp.logical_or(z == 1, z == 2)
    outer = jnp.logical_not(inner)

    def remote(src, dst, send, recv, device):
        return pltpu.make_async_remote_copy(
            src_ref=src,
            dst_ref=dst,
            send_sem=send,
            recv_sem=recv,
            device_id=device,
            device_id_type=pl.DeviceIdType.MESH,
        )

    def at_row(index):
        return (lax.axis_index("groups"), index, z)

    def at_col(index):
        return (lax.axis_index("groups"), r, index)

    def span(index, size):
        return pl.ds(pl.multiple_of(index * size, size), size)

    def child(m):
        return pl.ds(m * two, two)

    def load(k):
        if k == 0:
            return pltpu.make_async_copy(panel_one.at[0], own.at[pl.ds(0, rows)], loads.at[0])
        if k < 3:
            h = k - 1
            return pltpu.make_async_copy(inv_one.at[0, pl.ds(h * half, half)], chosen.at[h], loads.at[k])
        if k < 5:
            m = k - 3
            return pltpu.make_async_copy(panel_j.at[m], near_j.at[:, child(m)], loads.at[k])
        if k == 5:
            return pltpu.make_async_copy(inv_two, part_in, loads.at[5])
        if k < 8:
            m = k - 6
            return pltpu.make_async_copy(panel_r.at[m], near_r.at[:, child(m)], loads.at[k])
        return pltpu.make_async_copy(zroot, root, loads.at[8])

    for k in range(3):
        load(k).start()

    barrier = pltpu.get_barrier_semaphore()

    def greet(device):
        pl.semaphore_signal(barrier, inc=1, device_id=device, device_id_type=pl.DeviceIdType.MESH)

    for peer in (twin, over, diag):
        greet(at_row(peer))

    @pl.when(outer)
    def _():
        greet(at_col(1 + z // 3))

    @pl.when(inner)
    def _():
        greet(at_col(3 - z))
        greet(at_col(((z - 1) * 3) % 4))

    low = z < 2
    place = jnp.where(low, z, 3 - z)
    kin = [jnp.where(low, parents[m], 3 - parents[m]) for m in range(nodes)]
    picks = [
        jnp.where(place == 1, (kin[m] + 3) % 4, jnp.where(kin[m] == 0, 0, 1 + m)) for m in range(nodes)
    ]
    note[0] = jnp.zeros(note.shape[1:], jnp.int32)
    for m in range(nodes):
        note[0, m : m + 1, :] = jnp.full((1, width), kin[m], jnp.int32)

    @pl.when(outer)
    def _():
        pl.semaphore_wait(barrier, 4)

    @pl.when(inner)
    def _():
        pl.semaphore_wait(barrier, 5)

    def note_copy():
        return remote(note.at[0], note.at[1], note_send, note_recv, at_col(1 + z // 3))

    @pl.when(outer)
    def _():
        note_copy().start()

    def line(stream, t):
        at = span(t, PIECE)
        if stream == 0:
            src, dst, device = own.at[at], held.at[2, at], at_col(1 + z // 3)
        elif stream == 1:
            src, dst, device = own.at[at], held.at[0, at], at_col(3 - z)
        elif stream == 2:
            src, dst, device = held.at[2, at], held.at[1, at], at_col(3 - z)
        else:
            src = staged.at[stream - 3, span(t % RING, PIECE)]
            dst, device = held.at[stream - 3, at], at_col(((z - 1) * 3) % 4)
        return remote(src, dst, line_send.at[stream, t], line_recv.at[stream, t], device)

    def to_inner(first, last):
        @pl.when(outer)
        def _():
            def go(t, carry):
                line(0, t).start()
                return carry

            lax.fori_loop(first, last, go, 0)

    def forward(t):
        line(0, t).wait_recv()
        line(2, t).start()

    def chunk(t):
        @pl.when(inner)
        def _():
            @pl.when(t + AHEAD < chunks)
            def _():
                line(1, t + AHEAD).start()
                forward(t + AHEAD)

            line(1, t).wait_recv()
            line(2, t).wait_recv()
            at = span(t, PIECE)
            for m in range(nodes):
                pick = note[1, m : m + 1, :]

                @pl.when(t >= RING)
                def _():
                    line(3 + m, t - RING).wait_send()

                staged[m, span(t % RING, PIECE), :] = jnp.where(
                    pick < 2, own[at, :], jnp.where(pick == 2, held[0, at, :], held[1, at, :])
                )
                line(3 + m, t).start()

        @pl.when(outer)
        def _():
            line(3, t).wait_recv()
            line(4, t).wait_recv()

    def j_copy(k):
        mine = span(r, node)
        theirs = span(over, node)
        if k == 2:
            return remote(full_j.at[theirs], full_j.at[theirs], j_send.at[2], j_recv.at[2], at_row(twin))
        return remote(near_j, full_j.at[mine], j_send.at[k], j_recv.at[k], at_row(over if k == 0 else twin))

    def g_copy(k):
        if k == 4:
            at = pl.ds(0, rows)
            columns = span(1 - core, half)
            return remote(own.at[at, columns], beside, g_send.at[4], g_recv.at[4], at_row(twin))
        top = pl.ds(k // 2 * (rows // 2), rows // 2)
        at = pl.ds(pl.multiple_of(core * rows + k // 2 * (rows // 2), rows // 2), rows // 2)
        if k % 2 == 0:
            columns = span(1 - side, half)
            return remote(own.at[top, columns], across.at[at], g_send.at[k], g_recv.at[k], at_row(over))
        return remote(across.at[at], across.at[at], g_send.at[k], g_recv.at[k], at_row(twin))

    spans = [(k * STEP, STEP) for k in range(steps - 1)]
    spans += [((steps - 1) * STEP, STEP // 2), ((steps - 1) * STEP + STEP // 2, STEP // 2)]

    def r_copy(k, part):
        first, size = spans[part]
        who = over if k == 2 else r
        at = pl.ds(pl.multiple_of(who * rows + first, size), size)
        return remote(
            reduced.at[at],
            reduced.at[at],
            r_send.at[k, part],
            r_recv.at[k, part],
            at_row(over if k == 0 else twin),
        )

    def twice(function):
        def go(h, carry):
            function(h)
            return carry

        lax.fori_loop(0, 2, go, 0)

    part_two = two // 2

    def within(m, h):
        return pl.ds(pl.multiple_of(m * two + h * part_two, part_two), part_two)

    def pick_rows(m, at):
        pick = picks[m]
        first = jnp.where(pick == 0, own[at, :], held[0, at, :])
        second = jnp.where(pick == 2, held[1, at, :], held[2, at, :])
        return jnp.where(pick < 2, first, second)

    def reduce_part(part, m):
        first, size = spans[part]
        at = pl.ds(first, size)
        to = pl.ds(pl.multiple_of(r * rows + first, size), size)
        chosen[m, at, :] = pick_rows(m, at)

        def go(h):
            columns = within(m, h)
            reduced[to, columns] = near_r[at, columns] - mm(chosen[m, at, :], full_j[:, columns])

        twice(go)
        if m == nodes - 1:
            r_copy(0, part).start()
            r_copy(1, part).start()

    def gather_part(part):
        r_copy(0, part).wait_recv()
        r_copy(2, part).start()

    def root_wait(part):
        r_copy(1, part).wait_recv()
        r_copy(2, part).wait_recv()

    def root_step(step, m):
        places = [pl.ds(pl.multiple_of(d * rows + step * STEP, STEP), STEP) for d in range(4)]

        def go(h):
            columns = within(0, h)
            left = jnp.concatenate([root[:, at] for at in places], 1)
            right = jnp.concatenate([reduced[at, within(m, h)] for at in places], 0)
            z_r[m, :, columns] -= mm(left, right)

        twice(go)

    def to_tile(vec):
        return jnp.concatenate([vec[:, i * 128 : (i + 1) * 128] for i in range(vec.shape[1] // 128)], 0)

    def shared(pieces):
        total = jnp.zeros_like(pieces[0])
        for d, one in enumerate(pieces):
            total = total + jnp.where(r == d, one, 0.0)
        return total

    def to_peers(tile, send, recv):
        return [
            remote(tile.at[0], tile.at[1 + k], send.at[k], recv.at[k], at_row(peer))
            for k, peer in enumerate((twin, over, diag))
        ]

    def colsum(left, right):
        return jnp.sum(left * right, axis=0, keepdims=True)

    def factor(first, size):
        at = pl.ds(first, size)
        own[at, :] = mm(own[at, 0:half], chosen[0]) + mm(own[at, half:width], chosen[1])

    def masked(panel, tiles, at, m, first, count):
        column = lax.broadcasted_iota(jnp.int32, (1, two), 1)
        live = (column < widths[m]).astype(jnp.float32)
        blocks = [
            panel[pl.ds(at + i * TILE, TILE), child(m)] * (live * tiles[m, first + i].astype(jnp.float32))
            for i in range(count)
        ]
        return jnp.concatenate(blocks, 0)

    for k in range(3):
        load(k).wait()
    for k in range(3, 9):
        load(k).start()
    factor(0, STEP)
    to_inner(0, per)
    early = 2

    @pl.when(inner)
    def _():
        for t in range(early):
            line(1, t).start()

    for k in range(3, 6):
        load(k).wait()
    for m in range(nodes):
        near_j[:, child(m)] = mm(masked(near_j, tiles_j, 0, m, 0, node // TILE), part_in[m])
    for k in (0, 1):
        j_copy(k).start()

    def pass_on(first, last):
        @pl.when(inner)
        def _():
            for t in range(first, last):
                forward(t)
                if t + early < AHEAD:
                    line(1, t + early).start()

    share = AHEAD // steps
    pass_on(0, share)
    for k in range(1, steps):
        factor(k * STEP, STEP)
        to_inner(k * per, (k + 1) * per)
        pass_on(k * share, (k + 1) * share)
    g_copy(4).start()

    @pl.when(inner)
    def _():
        note_copy().wait_recv()

    full_j[span(r, node), :] = near_j[...]
    for m in range(nodes):
        z_r[m] = jnp.zeros_like(z_r[m])

    def separator_rows(m):
        load(6 + m).wait()

        def go(h):
            size = rows // 2
            at = pl.multiple_of(h * size, size)
            count = size // TILE
            near_r[pl.ds(at, size), child(m)] = mm(masked(near_r, tiles_r, at, m, h * count, count), part_in[m])

        twice(go)

    narrow = node // 2
    thin = narrow * node // width
    thick = node * node // width
    left_core = 2 * side
    others = (r, 2 - left_core, 3 - left_core)

    def gram_block(down, along):
        return mm_t(chosen[0, :, down], chosen[0, :, along]) + mm_t(chosen[1, :, down], chosen[1, :, along])

    def gram_half():
        along = pl.ds(pl.multiple_of((left_core + 1) * node + core * narrow, narrow), narrow)
        block = gram_block(span(left_core, node), along)
        for k in range(node // thin):
            own[rows : rows + thin, k * narrow : (k + 1) * narrow] = block[k * thin : (k + 1) * thin, :]
        to_inner(rows // PIECE, (rows + thin) // PIECE)

    def gram(b):
        block = gram_block(span(r, node), span(others[b], node))
        first = rows + thin + b * thick
        for k in range(node // thick):
            own[first : first + thick, k * node : (k + 1) * node] = block[k * thick : (k + 1) * thick, :]
        to_inner(first // PIECE, (first + thick) // PIECE)

    one = {}

    def square_sums():
        one["squares"] = sum(
            colsum(chosen[h, :, span(r, node)], chosen[h, :, span(r, node)]) for h in range(2)
        )
        one["squares_two"] = [colsum(part_in[m], part_in[m]) for m in range(nodes)]

    def gathered_j():
        j_copy(0).wait_recv()
        j_copy(2).start()
        j_copy(1).wait_recv()
        j_copy(2).wait_recv()

    def diagonal(h):
        block = own[0:rows, h * half : (h + 1) * half]
        one[h] = colsum(block, mm(root[:, span(r, rows)], block))

    def pair():
        g_copy(4).wait_recv()
        product_two = mm(root[:, span(twin, rows)], beside[...])
        one["pair"] = 2.0 * colsum(own[0:rows, span(core, half)], product_two)

    def cross():
        g_copy(1).wait_recv()
        g_copy(3).wait_recv()
        product_two = mm(root[:, span(1 - side, 2 * rows)], across[...])
        product_two = 2.0 * colsum(own[0:rows, span(side, half)], product_two)
        sums = [
            one[h] + jnp.where(core == h, one["pair"], 0.0) + jnp.where(side == h, product_two, 0.0)
            for h in range(2)
        ]
        vec_a[0] = to_tile(jnp.concatenate(sums, 1))
        for copy in to_peers(vec_a, a_send, a_recv):
            copy.start()

    def level_one_out():
        for copy in to_peers(vec_a, a_send, a_recv):
            copy.wait()
        total = vec_a[0] + vec_a[1] + vec_a[2] + vec_a[3]
        each = total.shape[0] // 4
        mine = shared([total[d * each : (d + 1) * each, :] for d in range(4)])
        var_one[...] = one["squares"] + jnp.concatenate([mine[i : i + 1, :] for i in range(each)], 1)

    def pass_g(k):
        g_copy(k).wait_recv()
        g_copy(k + 1).start()

    def node_step(b, m):
        first = rows + thin + b * thick
        packed = pick_rows(m, pl.ds(first, thick))
        block = jnp.concatenate([packed[:, k * node : (k + 1) * node] for k in range(node // thick)], 0)
        part = mm(block, full_j[span(others[b], node), child(m)])
        if b == 0:
            z_j[m] = part
        else:
            z_j[m] += part

    def x_copy():
        place = cross_block.at[:, :, span(core, narrow)]
        return remote(place, place, x_send, x_recv, at_row(twin))

    def share_half():
        for m in range(nodes):
            packed = pick_rows(m, pl.ds(rows, thin))
            block = jnp.concatenate([packed[:, k * narrow : (k + 1) * narrow] for k in range(node // thin)], 0)
            cross_block[m, :, span(core, narrow)] = block
        x_copy().start()

    def twin_step():
        x_copy().wait_recv()
        beyond = span(twin, node)

        @pl.when(core == 0)
        def _():
            for m in range(nodes):
                z_j[m] += mm(cross_block[m], full_j[beyond, child(m)])

        @pl.when(core == 1)
        def _():
            for m in range(nodes):
                z_j[m] += mm_t(cross_block[m], full_j[beyond, child(m)])

    def upper(m, dest):
        return mm_t(chosen[m, :, span(dest, node)], z_r[m])

    def u_copy(k):
        if k < 2:
            out = part_out.at[pl.ds(k * 2 * node, 2 * node)]
            return remote(out, part_in.at[k], u_send.at[k], u_recv.at[k], at_row(twin))
        out = part_own.at[pl.ds((k - 2) * node, node)]
        return remote(out, part_y.at[k - 2], u_send.at[k], u_recv.at[k], at_row(over))

    def upper_twin(m):
        def go(h):
            at = pl.ds(pl.multiple_of((2 * m + h) * node, node), node)
            part_out[at, :] = upper(m, (twin + 2 - 2 * h) % 4)

        twice(go)
        u_copy(m).start()

    def upper_over(m):
        far = upper(m, over)
        u_copy(m).wait_recv()
        part_own[m * node : (m + 1) * node, :] = far + part_in[m, 0:node, :]
        u_copy(2 + m).start()

    def upper_own(m):
        part_in[m, node : 2 * node, :] = part_in[m, node : 2 * node, :] + upper(m, r)

    def leave():
        return pltpu.make_async_copy(z_r, z_out, loads.at[9])

    def separator_sums():
        leave().start()
        one["sums_r"] = [colsum(near_r[:, child(m)], z_r[m]) for m in range(nodes)]

    def item(function, *arguments):
        return functools.partial(function, *arguments)

    work = {
        0: [item(separator_rows, 0)],
        1: [item(separator_rows, 1)],
        2: [gram_half],
        3: [item(gram, 0)],
        4: [item(gram, 1)],
        6: [item(gram, 2)],
        5: [square_sums],
        7: [gathered_j, item(reduce_part, 0, 0)],
        8: [item(reduce_part, 0, 1)],
        9: [load(8).wait, item(diagonal, 0)],
        11: [item(diagonal, 1)],
        14: [item(gather_part, 0), g_copy(0).start],
        15: [item(reduce_part, 1, 0)],
        16: [item(reduce_part, 1, 1)],
        17: [item(root_wait, 0), item(root_step, 0, 0)],
        18: [item(root_step, 0, 1), g_copy(2).start],
        19: [pair],
        22: [item(pass_g, 0), item(gather_part, 1)],
        23: [item(reduce_part, 2, 0)],
        24: [item(reduce_part, 2, 1)],
        25: [item(root_wait, 1), item(root_step, 1, 0)],
        26: [item(root_step, 1, 1)],
        27: [item(reduce_part, 3, 0)],
        28: [item(reduce_part, 3, 1)],
        29: [item(pass_g, 2)],
        30: [item(gather_part, 2)],
        31: [item(reduce_part, 4, 0), item(reduce_part, 4, 1)],
        32: [item(root_wait, 2), item(root_step, 2, 0)],
        33: [item(root_step, 2, 1), item(gather_part, 3)],
        34: [share_half],
        35: [item(gather_part, 4), item(root_wait, 3), item(root_wait, 4), item(root_step, 3, 0)],
        36: [item(upper_twin, 0)],
        37: [item(upper_over, 0), item(root_step, 3, 1)],
        38: [item(upper_twin, 1)],
        39: [item(upper_over, 1)],
        40: [item(node_step, 0, 0), item(node_step, 0, 1)],
        41: [cross],
        42: [twin_step, item(node_step, 1, 0), item(node_step, 1, 1)],
        43: [item(upper_own, 0), item(upper_own, 1)],
        44: [level_one_out, separator_sums],
    }
    done = 0
    for last in sorted(work) + [chunks - 1]:
        if last == done:
            chunk(last)
        else:

            def go(t, carry):
                chunk(t)
                return carry

            lax.fori_loop(done, last + 1, go, 0)
        done = last + 1
        for function in work.get(last, ()):
            function()

    sums_r = one["sums_r"]
    for m in range(nodes):
        node_step(2, m)
    for m in range(nodes):
        u_copy(2 + m).wait_recv()
        z_j[m] = -(z_j[m] + part_in[m, node : 2 * node, :] + part_y[m])
        sums_r[m] = sums_r[m] + colsum(near_j[:, child(m)], z_j[m])
    vec_b[0] = to_tile(jnp.concatenate(sums_r, 1))
    for copy in to_peers(vec_b, b_send, b_recv):
        copy.start()

    @pl.when(outer)
    def _():
        note_copy().wait_send()

        def go(t, carry):
            line(0, t).wait_send()
            return carry

        lax.fori_loop(0, chunks, go, 0)

    @pl.when(inner)
    def _():
        def go(t, carry):
            line(1, t).wait_send()
            line(2, t).wait_send()
            return carry

        lax.fori_loop(0, chunks, go, 0)

        def last(t, carry):
            line(3, t).wait_send()
            line(4, t).wait_send()
            return carry

        lax.fori_loop(chunks - RING, chunks, last, 0)

    x_copy().wait_send()
    leave().wait()
    for k in range(3):
        j_copy(k).wait_send()
    for k in range(5):
        g_copy(k).wait_send()
    for part in range(len(spans)):
        for k in range(3):
            r_copy(k, part).wait_send()
    for k in range(4):
        u_copy(k).wait_send()
    for copy in to_peers(vec_b, b_send, b_recv):
        copy.wait()
    total = vec_b[0] + vec_b[1] + vec_b[2] + vec_b[3]
    share = two // 4
    column = lax.broadcasted_iota(jnp.int32, (1, share), 1) + r * share
    for m in range(nodes):
        mine = shared([total[m * 4 + d : m * 4 + d + 1, :] for d in range(4)])
        square = shared([one["squares_two"][m][:, d * share : (d + 1) * share] for d in range(4)])
        live = (column < widths[m]).astype(jnp.float32)
        var_two[m : m + 1, :] = live * (square - mine)


def copy_kernel(*refs):
    sems = refs[-1]
    nodes, rows, _ = refs[3].shape
    parts = [(3, (m, pl.ds(h * (rows // 2), rows // 2))) for m in range(nodes) for h in range(2)]
    parts += [(2, (m,)) for m in range(nodes)] + [(0, ()), (1, ())]

    def at(ref, place):
        return ref.at[place] if place else ref

    ins = []
    outs = []
    for i, (k, place) in enumerate(parts):
        source, middle, target = (at(refs[k + 4 * d], place) for d in (0, 2, 1))
        ins.append(pltpu.make_async_copy(source, middle, sems.at[i]))
        outs.append(pltpu.make_async_copy(middle, target, sems.at[len(parts) + i]))
    for copy in ins:
        copy.start()
    for first, second in zip(ins, outs):
        first.wait()
        second.start()
    for copy in outs:
        copy.wait()


def line_body(
    zroot,
    panel_one,
    inv_one,
    panel_two_j,
    panel_two_r,
    inv_two,
    parents,
    widths,
    pattern_j,
    pattern_r,
):
    n = lax.axis_size("row")
    width = inv_one.shape[1]
    node = width // n
    nodes, two = inv_two.shape[:2]
    rows = zroot.shape[0]
    height = rows + node - node // 2 * node // width
    chunks = height // PIECE
    steps = rows // STEP
    f32 = jnp.float32
    smem = pl.BlockSpec(memory_space=pltpu.SMEM)
    hbm = pl.BlockSpec(memory_space=pl.ANY)
    vmem = pl.BlockSpec(memory_space=pltpu.VMEM)
    dma = pltpu.SemaphoreType.DMA
    results = pl.pallas_call(
        line_kernel,
        out_shape=(
            jax.ShapeDtypeStruct((1, node), f32),
            jax.ShapeDtypeStruct((nodes, two // n), f32),
            jax.ShapeDtypeStruct((nodes, node, two), f32),
            jax.ShapeDtypeStruct((nodes, rows, two), f32),
        ),
        in_specs=[smem] * 4 + [hbm] * 6,
        out_specs=(vmem, vmem, vmem, hbm),
        scratch_shapes=[
            pltpu.VMEM((nodes, rows, two), f32),
            pltpu.VMEM(zroot.shape, f32),
            pltpu.VMEM((height, width), f32),
            pltpu.VMEM((node, nodes * two), f32),
            pltpu.VMEM((rows, nodes * two), f32),
            pltpu.VMEM((nodes * 2 * node, two), f32),
            pltpu.VMEM((nodes * node, two), f32),
            pltpu.VMEM((3, height, width), f32),
            pltpu.VMEM((nodes, RING * PIECE, width), f32),
            pltpu.VMEM((width, nodes * two), f32),
            pltpu.VMEM((nodes, rows, width), f32),
            pltpu.VMEM((4 * rows, nodes * two), f32),
            pltpu.VMEM((2 * rows, width // 2), f32),
            pltpu.VMEM((rows, width // 2), f32),
            pltpu.VMEM((nodes, 2 * node, two), f32),
            pltpu.VMEM((nodes, node, two), f32),
            pltpu.VMEM((nodes, node, node), f32),
            pltpu.VMEM((2, 8, width), jnp.int32),
            pltpu.VMEM((4, width // 128, 128), f32),
            pltpu.VMEM((4, nodes * two // 128, 128), f32),
            dma((10,)),
            dma,
            dma,
            dma,
            dma,
            dma((5, chunks)),
            dma((5, chunks)),
            dma((3,)),
            dma((3,)),
            dma((5,)),
            dma((5,)),
            dma((3, steps + 1)),
            dma((3, steps + 1)),
            dma((4,)),
            dma((4,)),
            dma((3,)),
            dma((3,)),
            dma((3,)),
            dma((3,)),
        ],
        compiler_params=pltpu.CompilerParams(
            collective_id=0, has_side_effects=True, vmem_limit_bytes=60 * 1024 * 1024
        ),
    )(parents, widths, pattern_j, pattern_r, zroot, panel_one, inv_one, panel_two_j, panel_two_r, inv_two)
    return pl.pallas_call(
        copy_kernel,
        out_shape=tuple(jax.ShapeDtypeStruct(one.shape, one.dtype) for one in results),
        in_specs=[hbm] * 4,
        out_specs=(hbm,) * 4,
        scratch_shapes=[pltpu.VMEM(one.shape, one.dtype) for one in results] + [dma((2 * (3 * nodes + 2),))],
        compiler_params=pltpu.CompilerParams(vmem_limit_bytes=60 * 1024 * 1024),
    )(*results)


def solution(mesh):
    fits = mesh.shape["row"] == 4 and mesh.shape["col"] == 4
    return jax.shard_map(
        line_body if fits else general_body,
        mesh=mesh,
        in_specs=(
            P(("groups", "row"), None),
            P(("groups", "col"), "row", None),
            P(("groups", "col"), None, None),
            P(("groups", "col"), "row", None),
            P(("groups", "col"), "row", None),
            P(("groups", "col"), None, None),
            P(("groups", "col")),
            P(("groups", "col")),
            P(("groups", "col"), "row"),
            P(("groups", "col"), "row"),
        ),
        out_specs=(
            P(("groups", "col"), "row"),
            P(("groups", "col"), "row"),
            P(("groups", "col"), "row", None),
            P(("groups", "col"), "row", None),
        ),
        check_vma=False,
    )
```
